32 devices in a mesh: dp: 4 (over y, core), expert: 8 (over z, x).
Axes of the slice: x: 2, y: 2, z: 4, core: 2. Of those that a mesh axis runs over, the one named last changes fastest.
Arguments:
- tokens: bfloat16 [32, 576, 768], P(('dp', 'expert')), may hold values from -6 to 6
- segment_ids: int32 [32, 576], P(('dp', 'expert')), may hold values from 0 to 3, never falling along the last dimension, each value on 1 to 288 neighbouring positions
- pad_mask: int32 [32, 576], P(('dp', 'expert')), may hold values 0 or 1
- routes: int32 [32, 576, 2], P(('dp', 'expert')), may hold values from 0 to 7, all different within a row; in each aligned block of 576 rows (0 to 575, 576 to 1151, ..., all dimensions but the last counted through in order) at most 288 rows name the same one
- priority: int32 [32, 576], P(('dp', 'expert')), may hold values from 0 to 63
- gain_attn: float32 [768], replicated, may hold values from 0.5 to 1.5
- w_qkv: bfloat16 [768, 2304], replicated, may hold values from -0.21875 to 0.21875
- w_o: bfloat16 [768, 768], replicated, may hold values from -1.75 to 1.75
- gain_moe: float32 [768], replicated, may hold values from 0.5 to 1.5
- w_router: bfloat16 [768, 8], replicated, may hold values from -0.15625 to 0.15625
- w_in: bfloat16 [8, 768, 3072], P('expert', None, 'dp'), may hold values from -0.21875 to 0.21875
- w_out: bfloat16 [8, 3072, 768], P('expert', 'dp'), may hold values from -0.4375 to 0.4375
- cotangent: bfloat16 [32, 576, 768], P(('dp', 'expert')), may hold values from -6 to 6
Outputs:
- block_out: bfloat16 [32, 576, 768], P(('dp', 'expert'))
- grad_tokens: float32 [32, 576, 768], P(('dp', 'expert'))
- grad_gain_attn: float32 [768], replicated
- grad_w_qkv: float32 [768, 2304], replicated
- grad_w_o: float32 [768, 768], replicated
- grad_gain_moe: float32 [768], replicated
- grad_w_router: float32 [768, 8], replicated
- grad_w_in: float32 [8, 768, 3072], P('expert', None, 'dp')
- grad_w_out: float32 [8, 3072, 768], P('expert', 'dp')
The draws below stay inside these ranges and needn't reach their ends.
Inputs may be any that keep to these rules, and one draw needn't show every extreme that they name: `routes`: in each aligned block of 576 patches (one device's patches) no expert is named by more than 288 pairs, a bound that some block reaches; the two experts of a patch differ. `segment_ids`: never falling along a row.
All inputs are finite; a program needn't handle non-finite values. No bound on the sum of `pad_mask` on one device may be relied on, other than what follows from the above.
Results may differ from the reference program's by a relative error of at most 0.014.
Values may be sent and summed in bfloat16 or wider, within the bound.
No kernel may reach another device: no remote copies, remote signals or barrier semaphores. Data moves between devices by JAX's collectives and lax.ppermute only.
A program may use at most 256 MiB of HBM per device.

```python
import math
import jax
import jax.numpy as jnp
import numpy as np
from jax import lax

D = 768
HEADS = 12
HEAD_DIM = 64
FF = 3072
EXPERTS = 8
LEN = 576
LEVELS = 64
BINS = 128
TOK_DEV = 576
ROWS = 32
TOKENS = 18432
SLOTS = 288
CAP = 4839


def plant(values, stream_key, smallest, top_value):
    longest = values.shape.index(max(values.shape))
    spots = []
    for shift in (0, 1):
        where = [jax.random.randint(jax.random.fold_in(stream_key, axis), (), 0, length) for axis, length in enumerate(values.shape)]
        where[longest] = (where[longest] + shift) % values.shape[longest]
        spots.append(tuple(where))
    return values.at[spots[0]].set(smallest).at[spots[1]].set(top_value)


def shard_levels(key, shape, pieces, low, high):
    gain, own = 1.0, jax.random.fold_in(key, 6)
    for dim, shards_of in pieces:
        steps = jnp.exp(jax.random.uniform(jax.random.fold_in(own, dim), (shards_of,), jnp.float32, low / len(pieces), high / len(pieces)))
        gain = gain * jnp.repeat(steps, shape[dim] // shards_of).reshape([-1 if axis == dim else 1 for axis in range(len(shape))])
    return gain


def length_profile(count, total, limit, slope):
    weights = [(1 << 20) // math.isqrt(grade ** slope) + 1 for grade in range(2, count + 1)]
    rest, counts = total - limit - (count - 1), [1] * (count - 1)
    while rest > 0:
        movable = [i for i in range(count - 1) if counts[i] < limit]
        whole, budget = sum([weights[i] for i in movable]), rest
        for i in movable:
            addition = min(limit - counts[i], max(1, budget * weights[i] // whole), rest)
            counts[i] = counts[i] + addition
            rest = rest - addition
    return np.array([limit] + counts)


def uneven(key, count, total, most, skew):
    if count == 2:
        one = jax.random.randint(key, (), max(1, total - most), min(most, total - 1) + 1)
        return jnp.stack([one, total - one])
    lengths = jnp.asarray(length_profile(count, total, most, skew), jnp.int32)
    couples = (count - 1) // 2
    donor, sink = lengths[1:1 + 2 * couples:2], lengths[2:2 + 2 * couples:2]
    slack = jnp.minimum(donor - 1, most - sink)
    passed = jax.random.randint(jax.random.fold_in(key, 1), (couples,), 0, 1 << 20) % (slack + 1)
    lengths = lengths.at[1:1 + 2 * couples:2].set(donor - passed).at[2:2 + 2 * couples:2].set(sink + passed)
    return lengths[jax.random.permutation(jax.random.fold_in(key, 2), count)]


def deal_out(rng, own, number, rows, count, top, most, lean):
    sequence = jax.random.permutation(rng, count)
    heavy_load, common = portions_of(count, rows * top, most, lean, True), portions_of(count, rows * top, most, lean, False)
    places = jnp.arange(count)

    def named(tallies, turn):
        used = int((tallies > 0).sum())
        fixed = max(1, used // 4)
        shifted = fixed + (places - fixed + turn * (used - fixed)) % max(1, count - fixed)
        return jnp.zeros((count,), jnp.int32).at[sequence[jnp.where(places < fixed, places, shifted)]].set(jnp.asarray(tallies, jnp.int32))

    tallies = jnp.where(number % 4 == 0, named(heavy_load, number // 4), named(common, number - number // 4 - 1))
    mixed = jax.random.permutation(jax.random.fold_in(own, 3), count)
    giver, sink = mixed[0:count // 2 * 2:2], mixed[1:count // 2 * 2:2]
    room = jnp.minimum(tallies[giver] - 1, most - tallies[sink]) // 2
    room = jnp.where((giver == sequence[0]) | (sink == sequence[0]) | (tallies[sink] == 0), 0, jnp.maximum(room, 0))
    shifted = jax.random.randint(jax.random.fold_in(own, 4), (count // 2,), 0, 1 << 20) % (room + 1)
    tallies = tallies.at[giver].add(-shifted).at[sink].add(shifted)
    items = jnp.searchsorted(jnp.cumsum(tallies), jnp.arange(rows * top), side="right").astype(jnp.int32)
    table = items.reshape(top, rows).T
    table = table[jax.random.permutation(jax.random.fold_in(own, 1), rows)]
    turn = jax.random.randint(jax.random.fold_in(own, 2), (rows, 1), 0, top)
    return jnp.take_along_axis(table, (jnp.arange(top)[None, :] + turn) % top, axis=1)


def portions_of(number_of, total, most, lean, full):
    weights = [(1 << 20) // math.isqrt(rank ** lean) + 1 for rank in range(1, number_of + 1)]
    largest = most if full else min(most, max(-(-total // number_of), total * weights[0] // sum(weights)))
    least = 1 if total - largest >= number_of - 1 else 0
    holding, surplus = [largest] + [least] * (number_of - 1), total - largest - least * (number_of - 1)
    while surplus > 0:
        movable = [i for i in range(1, number_of) if holding[i] < largest] or [i for i in range(1, number_of) if holding[i] < most]
        whole, left = sum([weights[i] for i in movable]), surplus
        for i in movable:
            extra = min(most - holding[i], max(1, left * weights[i] // whole), surplus)
            holding[i] = holding[i] + extra
            surplus = surplus - extra
    return np.array(holding)


def gaussian(key, extent, deviation, bound, shards=(), held_as=jnp.bfloat16):
    gain = shard_levels(key, extent, shards, -0.22, 0.18) if shards else 1.0
    entries = jax.random.normal(key, extent, jnp.float32) * deviation * gain
    return jnp.minimum(jnp.maximum(entries, -bound), bound).astype(held_as)


def setup_inputs(seed: int = 0) -> dict:
    key_of = jax.random.split(jax.random.key(seed), 14)
    tokens = gaussian(key_of[0], (ROWS, LEN, D), 1.0, 6.0, ((0, 32),))
    segment_ids = jax.vmap(lambda own: jnp.searchsorted(jnp.cumsum(uneven(own, 4, LEN, LEN // 2, 1)), jnp.arange(LEN), side="right"))(jax.random.split(key_of[1], ROWS)).reshape((ROWS, LEN)).astype(jnp.int32)
    pad_mask = plant((jax.random.randint(key_of[2], (ROWS, LEN), 0, 8) < 7).astype(jnp.int32), jax.random.fold_in(key_of[2], 1), 0, 1)
    routes_keys = jax.random.split(jax.random.fold_in(key_of[3], 1), ROWS * LEN // TOK_DEV)
    routes_turns = jax.random.permutation(jax.random.fold_in(key_of[3], 3), ROWS * LEN // TOK_DEV)
    routes = jax.vmap(lambda own, number: deal_out(jax.random.fold_in(key_of[3], 2), own, number, TOK_DEV, EXPERTS, 2, SLOTS, 1))(routes_keys, routes_turns).reshape((ROWS, LEN, 2))
    priority = plant(jax.random.randint(key_of[4], (ROWS, LEN), 0, LEVELS), jax.random.fold_in(key_of[4], 1), 0, LEVELS - 1).astype(jnp.int32)
    gain_attn = jnp.clip(1.0 + 0.1 * jax.random.normal(key_of[5], (D,), jnp.float32), 0.5, 1.5)
    w_qkv = gaussian(key_of[6], (D, 3 * D), D ** -0.5, 0.21875)
    w_o = gaussian(key_of[7], (D, D), (D // 64) ** -0.5, 1.75)
    gain_moe = jnp.clip(1.0 + 0.1 * jax.random.normal(key_of[8], (D,), jnp.float32), 0.5, 1.5)
    w_router = gaussian(key_of[9], (D, EXPERTS), (2 * D) ** -0.5, 0.15625)
    w_in = gaussian(key_of[10], (EXPERTS, D, FF), D ** -0.5, 0.21875, ((0, 8), (2, 4)))
    w_out = gaussian(key_of[11], (EXPERTS, FF, D), (max(4 * FF // (EXPERTS * EXPERTS), 1)) ** -0.5, 0.4375, ((0, 8), (1, 4)))
    cotangent = gaussian(key_of[12], (ROWS, LEN, D), 1.0, 6.0, ((0, 32),))
    return {"tokens": tokens, "segment_ids": segment_ids, "pad_mask": pad_mask, "routes": routes, "priority": priority, "gain_attn": gain_attn, "w_qkv": w_qkv, "w_o": w_o, "gain_moe": gain_moe, "w_router": w_router, "w_in": w_in, "w_out": w_out, "cotangent": cotangent}


@jax.custom_vjp
def low(v):
    return lax.optimization_barrier(v.astype(jnp.bfloat16)).astype(jnp.float32)

@jax.custom_vjp
def low_back(v):
    return v

def low_keep(v):
    return (low(v), None)

def low_pass(kept, grad):
    return (grad,)

def back_keep(v):
    return (v, None)

def back_low(kept, grad):
    return (low(grad),)
low.defvjp(low_keep, low_pass)
low_back.defvjp(back_keep, back_low)

def layer_norm(values, gain_vector):
    center = values - lax.optimization_barrier(jnp.mean(values, axis=-1, keepdims=True))
    spread = lax.optimization_barrier(jnp.mean(center * center, axis=-1, keepdims=True))
    return center * lax.rsqrt(spread + 1e-06) * gain_vector

def matmul(left_side, right_side):
    return jnp.dot(left_side, right_side, precision=lax.Precision.HIGHEST, preferred_element_type=jnp.float32)

def attend(row_values, segment, padding, gain_attn, w_qkv, w_o):
    length = row_values.shape[0]
    normed = low(layer_norm(row_values, gain_attn))
    projected = low(low_back(matmul(normed, w_qkv))).reshape(length, 3, HEADS, HEAD_DIM)
    queries = projected[:, 0]
    key_rows = projected[:, 1]
    value_rows = projected[:, 2]
    raw_scores = jnp.einsum('qhd,khd->hqk', queries, key_rows, precision=lax.Precision.HIGHEST)
    places = jnp.arange(length)
    allowed = (segment[:, None] == segment[None, :]) & ((padding[None, :] > 0) | (places[:, None] == places[None, :]))
    scores = jnp.where(allowed[None], low_back(raw_scores) * HEAD_DIM ** (-0.5), -1e+30)
    attention = low(jax.nn.softmax(scores, axis=-1))
    mixture = jnp.einsum('hqk,khd->qhd', attention, value_rows, precision=lax.Precision.HIGHEST)
    mixture = low(low_back(mixture)).reshape(length, HEADS * HEAD_DIM)
    return row_values + low_back(matmul(mixture, w_o))

def routing(routes, priority, pad_mask):
    flat_routes = routes.reshape(TOKENS, 2).astype(jnp.int32)
    valid_pair = jnp.broadcast_to((pad_mask.reshape(TOKENS) > 0)[:, None], (TOKENS, 2))
    level_rank = LEVELS - 1 - priority.reshape(TOKENS)[:, None].astype(jnp.int32)
    class_id = jnp.arange(2, dtype=jnp.int32)[None, :] * LEVELS + level_rank
    token_index = jnp.broadcast_to(jnp.arange(TOKENS, dtype=jnp.int32)[:, None], (TOKENS, 2))
    pair_code = jnp.where(valid_pair, flat_routes * BINS + class_id, EXPERTS * BINS).astype(jnp.int32)
    pair_order = jnp.lexsort((token_index.reshape(2 * TOKENS), pair_code.reshape(2 * TOKENS))).astype(jnp.int32)
    position = jnp.zeros((2 * TOKENS,), jnp.int32).at[pair_order].set(jnp.arange(2 * TOKENS, dtype=jnp.int32))
    position = position.reshape(TOKENS, 2)
    expert_load = jnp.zeros((EXPERTS,), jnp.int32).at[flat_routes].add(valid_pair.astype(jnp.int32))
    load_start = (jnp.cumsum(expert_load) - expert_load).astype(jnp.int32)
    pair_rank = (position - load_start[flat_routes]).astype(jnp.int32)
    kept_pair = valid_pair & (pair_rank < CAP)
    target_rank = jnp.where(kept_pair, pair_rank, CAP).astype(jnp.int32)
    slot_table = jnp.full((EXPERTS, CAP), TOKENS, jnp.int32).at[flat_routes, target_rank].set(token_index, mode='drop')
    return (flat_routes, kept_pair, jnp.clip(pair_rank, 0, CAP - 1).astype(jnp.int32), slot_table)

def forward(tokens, gain_attn, w_qkv, w_o, gain_moe, w_router, w_in, w_out, segment_ids, pad_mask, flat_routes, kept_pair, pair_rank, slot_table):
    attend_row = jax.checkpoint(lambda packed: attend(packed[0], packed[1], packed[2], gain_attn, w_qkv, w_o))
    hidden = lax.map(attend_row, (tokens, segment_ids, pad_mask)).reshape(TOKENS, D)
    normed = low(layer_norm(hidden, gain_moe))
    router = jax.nn.softmax(low_back(matmul(normed, w_router)), axis=-1)
    gate_value = jnp.take_along_axis(router, flat_routes, axis=1)
    padded = jnp.concatenate([normed, jnp.zeros((1, D), jnp.float32)], axis=0)

    def expert(packed):
        token_index, w_first, w_second = packed
        in_rows = low_back(padded[token_index])
        active = low(jax.nn.gelu(low_back(matmul(in_rows, w_first)), approximate=True))
        return low(low_back(matmul(active, w_second)))
    outputs = lax.map(jax.checkpoint(expert), (slot_table, w_in, w_out))
    picked = outputs[flat_routes, pair_rank]
    expert_sum = lax.optimization_barrier(jnp.sum(jnp.where(kept_pair, gate_value, 0.0)[:, :, None] * picked, axis=1))
    return (hidden + expert_sum).reshape(ROWS, LEN, D)

def reference(tokens, segment_ids, pad_mask, routes, priority, gain_attn, w_qkv, w_o, gain_moe, w_router, w_in, w_out, cotangent):
    flat_routes, kept_pair, pair_rank, slot_table = routing(routes, priority, pad_mask)
    inputs = (tokens.astype(jnp.float32), gain_attn.astype(jnp.float32), w_qkv.astype(jnp.float32), w_o.astype(jnp.float32), gain_moe.astype(jnp.float32), w_router.astype(jnp.float32), w_in.astype(jnp.float32), w_out.astype(jnp.float32))

    def closed(*values):
        return forward(*values, segment_ids, pad_mask, flat_routes, kept_pair, pair_rank, slot_table)
    result, pullback = jax.vjp(closed, *inputs)
    gradients = pullback(cotangent.astype(jnp.float32))
    return (result.astype(jnp.bfloat16), gradients[0], gradients[1], gradients[2], gradients[3], gradients[4], gradients[5], gradients[6], gradients[7])
```

```python
import functools

import jax
import jax.numpy as jnp
from jax import lax
from jax.experimental import pallas as pl
from jax.experimental.pallas import tpu as pltpu
from jax.sharding import PartitionSpec as P

HEADS = 12
HEAD_DIM = 64
LEVELS = 64
BINS = 2 * LEVELS
LIMIT = 60 * 1024 * 1024
F32 = jnp.float32
BF16 = jnp.bfloat16


def dot(a, b, ca=1, cb=0, precision=None):
    return lax.dot_general(
        a, b, (((ca,), (cb,)), ((), ())), precision=precision, preferred_element_type=F32
    )


def whole(shape):
    zeros = (0,) * len(shape)
    return pl.BlockSpec(shape, lambda *_: zeros, pipeline_mode=pl.Buffered(1))


def whole_out(shape):
    zeros = (0,) * len(shape)
    return pl.BlockSpec(shape, lambda *_: zeros)


def iota(shape, dim):
    return lax.broadcasted_iota(jnp.int32, shape, dim)


def call(kernel, grid, ins, in_specs, outs, out_specs, scratch=(), flops=0, moved=0):
    return pl.pallas_call(
        kernel,
        grid=grid,
        in_specs=in_specs,
        out_specs=out_specs,
        out_shape=outs,
        scratch_shapes=list(scratch),
        compiler_params=pltpu.CompilerParams(vmem_limit_bytes=LIMIT),
        cost_estimate=pl.CostEstimate(flops=flops, bytes_accessed=moved, transcendentals=0),
    )(*ins)


def shape_of(shape, dtype):
    return jax.ShapeDtypeStruct(shape, dtype)


def norm_parts(values):
    center = values - jnp.mean(values, axis=-1, keepdims=True)
    spread = jnp.mean(center * center, axis=-1, keepdims=True)
    scale = lax.rsqrt(spread + 1e-06)
    return center * scale, scale


def norm_back(unit, scale, grad_unit):
    return scale * (
        grad_unit
        - jnp.mean(grad_unit, axis=-1, keepdims=True)
        - unit * jnp.mean(grad_unit * unit, axis=-1, keepdims=True)
    )


def class_rows(level_row, which, tokens):
    return (iota((BINS, tokens), 0) == which * LEVELS + (LEVELS - 1) - level_row).astype(F32)


def route_kernel(slots, experts, routes_ref, prio_ref, pad_ref, hist_ref, info_ref):
    tokens = routes_ref.shape[0]
    pair_cols = routes_ref[...].astype(F32)
    pick = (iota((8, 2), 0) == iota((8, 2), 1)).astype(F32)
    rows = dot(pick, pair_cols, 1, 1)
    prio = prio_ref[...]
    valid = (pad_ref[...] > 0).astype(F32)
    early = iota((tokens, tokens), 0) < iota((tokens, tokens), 1)
    hot = [(iota((experts, tokens), 0) == rows[k : k + 1].astype(jnp.int32)).astype(F32) for k in (0, 1)]
    count = dot((hot[0] + hot[1]).astype(BF16), early.astype(BF16))
    hist = jnp.zeros((experts, BINS), F32)
    sides = jnp.where(iota((8, tokens), 0) == 0, prio.astype(F32), valid)
    eye = (iota((8, 8), 0) == iota((8, 8), 1)).astype(F32)
    cols = dot(sides, eye, 0, 0)
    prio_col = cols[:, 0:1]
    valid_col = cols[:, 1:2]
    for k in (0, 1):
        slot = jnp.sum(hot[k] * count, axis=0, keepdims=True)
        info_ref[k : k + 1, :] = rows[k : k + 1]
        info_ref[2 + k : 3 + k, :] = rows[k : k + 1] * slots + slot
        hist = hist + dot(hot[k] * valid, class_rows(prio, k, tokens), 1, 1)
        code_row = rows[k : k + 1] * LEVELS + prio.astype(F32)
        code_col = jnp.where(valid_col > 0, pair_cols[:, k : k + 1] * LEVELS + prio_col, -1.0)
        same = (code_col == code_row) & early
        info_ref[4 + k : 5 + k, :] = jnp.sum(same.astype(F32), axis=0, keepdims=True)
    info_ref[6:7, :] = prio.astype(F32)
    info_ref[7:8, :] = valid
    hist_ref[...] = hist.astype(jnp.int32)


def slot_hot(target_rows, expert, slots, tokens):
    place = iota((slots, tokens), 0) + expert * slots
    return ((place == target_rows[0:1]) | (place == target_rows[1:2])).astype(F32).astype(BF16)


def spread_kernel(slots, info_ref, rows_ref, out_ref):
    target = info_ref[2:4, :].astype(jnp.int32)
    hot = slot_hot(target, pl.program_id(0), slots, rows_ref.shape[0])
    out_ref[0] = dot(hot, rows_ref[...]).astype(BF16)


def keep_kernel(slots, capacity, me_ref, hist_ref, info_ref, rows_ref, out_ref, kept_ref):
    devices, experts, bins = hist_ref.shape
    tokens = rows_ref.shape[0]

    @pl.when(pl.program_id(0) == 0)
    def _():
        def add(j, sums):
            block = hist_ref[j].astype(F32)
            lower = (j < me_ref[0]).astype(F32)
            return sums[0] + block, sums[1] + block * lower

        zero = jnp.zeros((experts, bins), F32)
        totals, before = lax.fori_loop(0, devices, add, (zero, zero))
        early = (iota((bins, bins), 0) < iota((bins, bins), 1)).astype(F32)
        exact = lax.Precision.HIGHEST
        base = dot(totals, early, precision=exact) + before
        prio = info_ref[6:7, :].astype(jnp.int32)
        valid = info_ref[7:8, :] > 0
        for k in (0, 1):
            hot = (iota((experts, tokens), 0) == info_ref[k : k + 1, :].astype(jnp.int32)).astype(F32)
            spot = dot(base, class_rows(prio, k, tokens), precision=exact)
            rank = jnp.sum(hot * spot, axis=0, keepdims=True) + info_ref[4 + k : 5 + k, :]
            kept = valid & (rank < capacity - 0.5)
            kept_ref[k : k + 1, :] = jnp.where(kept, info_ref[2 + k : 3 + k, :].astype(jnp.int32), -1)
        kept_ref[2:8, :] = jnp.full((6, tokens), -1, jnp.int32)

    hot = slot_hot(kept_ref[0:2, :], pl.program_id(0), slots, tokens)
    out_ref[0] = dot(hot, rows_ref[...]).astype(BF16)


def attend_kernel(
    tok_ref, seg_ref, pad_ref, ga_ref, wqkv_ref, wo_ref, gm_ref,
    hidden_ref, normed_ref, proj_ref, mix_ref, prob_ref, nmoe_ref, bias_ref,
):
    step = pl.program_id(0)
    tokens, features = tok_ref.shape

    @pl.when(step == 0)
    def _():
        unit, _ = norm_parts(tok_ref[...].astype(F32))
        normed = (unit * ga_ref[...]).astype(BF16)
        normed_ref[...] = normed
        for part in range(3):
            at = slice(part * features, (part + 1) * features)
            proj_ref[:, at] = dot(normed, wqkv_ref[:, at]).astype(BF16)
        seg = seg_ref[...].astype(F32)
        eye = (iota((8, 8), 0) == iota((8, 8), 1)).astype(F32)
        seg_col = dot(jnp.broadcast_to(seg, (8, tokens)), eye, 0, 0)[:, 0:1]
        own = iota((tokens, tokens), 0) == iota((tokens, tokens), 1)
        allowed = (seg_col == seg) & ((pad_ref[...] > 0) | own)
        bias_ref[...] = jnp.where(allowed, 0.0, -1e30)

    at = lambda part: pl.ds(pl.multiple_of(part * features + step * 128, 128), 128)
    query, keys, value = proj_ref[:, at(0)], proj_ref[:, at(1)], proj_ref[:, at(2)]
    first = iota((tokens, 128), 1) < HEAD_DIM
    mixed = []
    for h in (0, 1):
        mine = first if h == 0 else ~first
        own_query = jnp.where(mine, query.astype(F32) * HEAD_DIM ** (-0.5), 0.0).astype(BF16)
        scores = dot(own_query, keys, 1, 1) + bias_ref[...]
        top = jnp.max(scores, axis=-1, keepdims=True)
        exponent = jnp.exp(scores - top)
        total = jnp.sum(exponent, axis=-1, keepdims=True)
        prob = (exponent * (1.0 / total)).astype(BF16)
        prob_ref[h] = prob
        mixed.append(dot(prob, value))
    mix_ref[:, at(0)] = jnp.where(first, mixed[0], mixed[1]).astype(BF16)

    @pl.when(step == pl.num_programs(0) - 1)
    def _():
        hidden = tok_ref[...].astype(F32) + dot(mix_ref[...], wo_ref[...])
        hidden_ref[...] = hidden
        unit, _ = norm_parts(hidden)
        nmoe_ref[...] = (unit * gm_ref[...]).astype(BF16)


def gather_rows(kept_ref, rows_ref, tokens):
    experts, slots, features = rows_ref.shape

    def add(e, total):
        hot = slot_hot(kept_ref[0:2, :], e, slots, tokens)
        return total + dot(hot, rows_ref[e], 0, 0)

    return lax.fori_loop(0, experts, add, jnp.zeros((tokens, features), F32))


def block_kernel(kept_ref, rows_ref, hidden_ref, out_ref):
    tokens = hidden_ref.shape[0]
    out_ref[...] = (hidden_ref[...] + gather_rows(kept_ref, rows_ref, tokens)).astype(BF16)


def attend_back_kernel(
    kept_ref, rows_ref, hidden_ref, cot_ref, tok_ref, ga_ref, gm_ref, wqkv_ref, wo_ref,
    normed_ref, proj_ref, mix_ref, prob_ref,
    gtok_ref, gqkv_ref, go_ref, gain_ref, dhid_ref, dmix_ref, dproj_ref,
):
    step = pl.program_id(0)
    tokens, features = tok_ref.shape

    @pl.when(step == 0)
    def _():
        grad = gather_rows(kept_ref, rows_ref, tokens)
        unit, scale = norm_parts(hidden_ref[...])
        gain_ref[1:2, :] = jnp.sum(grad * unit, axis=0, keepdims=True)
        dhid = cot_ref[...].astype(F32) + norm_back(unit, scale, grad * gm_ref[...])
        dhid_ref[...] = dhid
        branch = dhid.astype(BF16)
        go_ref[...] = dot(mix_ref[...], branch, 0, 0).astype(BF16)
        dmix_ref[...] = dot(branch, wo_ref[...], 1, 1).astype(BF16)

    at = lambda part: pl.ds(pl.multiple_of(part * features + step * 128, 128), 128)
    query, keys, value = proj_ref[:, at(0)], proj_ref[:, at(1)], proj_ref[:, at(2)]
    dmix = dmix_ref[:, at(0)]
    product = dmix.astype(F32) * mix_ref[:, at(0)].astype(F32)
    first = iota((tokens, 128), 1) < HEAD_DIM
    parts = []
    for h in (0, 1):
        mine = first if h == 0 else ~first
        own_dmix = jnp.where(mine, dmix.astype(F32), 0.0).astype(BF16)
        delta = jnp.sum(jnp.where(mine, product, 0.0), axis=-1, keepdims=True)
        prob = prob_ref[h]
        dprob = dot(own_dmix, value, 1, 1)
        dscore = (prob.astype(F32) * (dprob - delta) * HEAD_DIM ** (-0.5)).astype(BF16)
        parts.append((dot(dscore, keys), dot(dscore, query, 0, 0), dot(prob, dmix, 0, 0)))
    for part in range(3):
        dproj_ref[:, at(part)] = jnp.where(first, parts[0][part], parts[1][part]).astype(BF16)

    @pl.when(step == pl.num_programs(0) - 1)
    def _():
        grad = jnp.zeros((tokens, features), F32)
        for part in range(3):
            cols = slice(part * features, (part + 1) * features)
            gqkv_ref[:, cols] = dot(normed_ref[...], dproj_ref[:, cols], 0, 0).astype(BF16)
            grad = grad + dot(dproj_ref[:, cols], wqkv_ref[:, cols], 1, 1)
        unit, scale = norm_parts(tok_ref[...].astype(F32))
        gain_ref[0:1, :] = jnp.sum(grad * unit, axis=0, keepdims=True)
        gain_ref[2:8, :] = jnp.zeros((6, features), F32)
        gtok_ref[...] = dhid_ref[...] + norm_back(unit, scale, grad * ga_ref[...])


def expert_kernel(pieces, *refs):
    x_ref, g_ref, wr_ref, own_ref = refs[:4]
    win = refs[4 : 4 + pieces]
    wout = refs[4 + pieces : 4 + 2 * pieces]
    y_ref, dx_ref, dexp_ref, gwr_ref = refs[4 + 2 * pieces : 8 + 2 * pieces]
    act = refs[8 + 2 * pieces : 8 + 3 * pieces]
    dpre = refs[8 + 3 * pieces :]
    x = x_ref[0]
    g = g_ref[0].astype(F32)
    logits = dot(x, wr_ref[...])
    exponent = jnp.exp(logits - jnp.max(logits, axis=-1, keepdims=True))
    router = exponent / jnp.sum(exponent, axis=-1, keepdims=True)
    gate = jnp.sum(router * own_ref[...], axis=-1, keepdims=True)
    dexp = (gate * g).astype(BF16)
    dexp_ref[...] = dexp
    out = jnp.zeros(x.shape, F32)
    dx = jnp.zeros(x.shape, F32)
    for r in range(pieces):
        pre = dot(x, win[r][...])
        square = pre * pre
        bend = jnp.tanh(0.7978845608028654 * pre * (1.0 + 0.044715 * square))
        half = 0.5 * (1.0 + bend)
        slope = half + (0.5 * 0.7978845608028654) * pre * (1.0 - bend * bend) * (1.0 + 0.134145 * square)
        active = (pre * half).astype(BF16)
        act[r][...] = active
        dpreact = (dot(dexp, wout[r][...], 1, 1) * slope).astype(BF16)
        dpre[r][...] = dpreact
        out = out + dot(active, wout[r][...])
        dx = dx + dot(dpreact, win[r][...], 1, 1)
    out = out.astype(BF16).astype(F32)
    y_ref[0] = (gate * out).astype(BF16)
    dgate = jnp.sum(g * out, axis=-1, keepdims=True)
    dlogits = (dgate * gate * (own_ref[...] - router)).astype(BF16)
    dx_ref[0] = (dx + dot(dlogits, wr_ref[...], 1, 1)).astype(BF16)

    @pl.when(pl.program_id(0) == 0)
    def _():
        gwr_ref[...] = jnp.zeros(gwr_ref.shape, F32)

    gwr_ref[...] += dot(x, dlogits, 0, 0)


def swap(value, axis, bit):
    size = lax.axis_size(axis)
    return lax.ppermute(value, axis, [(i, i ^ bit) for i in range(size)])


def bits_of(axis):
    size = lax.axis_size(axis)
    return [1 << b for b in range(size.bit_length() - 1)]


def all_sum(value, steps):
    rows = value.shape[0]
    place = []
    for axis, bit in steps:
        half = value.shape[0] // 2
        mine = ((lax.axis_index(axis) & bit) > 0).astype(jnp.int32)
        keep = lax.dynamic_slice_in_dim(value, mine * half, half, 0)
        give = lax.dynamic_slice_in_dim(value, (1 - mine) * half, half, 0)
        value = (keep.astype(F32) + swap(give, axis, bit).astype(F32)).astype(BF16)
        place.append(mine)
    for (axis, bit), mine in zip(reversed(steps), reversed(place)):
        other = swap(value, axis, bit)
        low = jnp.where(mine > 0, other, value)
        high = jnp.where(mine > 0, value, other)
        value = jnp.concatenate([low, high], axis=0)
    return value


def local(
    tokens, segment_ids, pad_mask, routes, priority, gain_attn, w_qkv, w_o, gain_moe, w_router,
    w_in, w_out, cotangent,
):
    sequences, length, features = tokens.shape
    count = sequences * length
    experts = w_router.shape[1]
    groups = lax.axis_size("expert")
    replicas = lax.axis_size("dp")
    devices = groups * replicas
    most = 4 * count // experts
    slots = -(-most // 16) * 16
    capacity = (42 * count * devices + 20 * experts - 1) // (20 * experts)
    me = lax.axis_index(("dp", "expert"))
    tok = tokens.reshape(count, features)
    cot = cotangent.reshape(count, features)
    ga = gain_attn.reshape(1, features)
    gm = gain_moe.reshape(1, features)
    sent = shape_of((experts, slots, features), BF16)
    pair_cost = 2 * experts * slots * count * features

    win, wout = {0: w_in[0]}, {0: w_out[0]}
    for bit in reversed(bits_of("dp")):
        for r in list(win):
            win[r ^ bit] = swap(win[r], "dp", bit)
            wout[r ^ bit] = swap(wout[r], "dp", bit)

    hist, info = call(
        functools.partial(route_kernel, slots, experts),
        (1,),
        (routes.reshape(count, 2), priority.reshape(1, count), pad_mask.reshape(1, count)),
        [whole((count, 2)), whole((1, count)), whole((1, count))],
        (shape_of((experts, BINS), jnp.int32), shape_of((8, count), F32)),
        (whole_out((experts, BINS)), whole_out((8, count))),
        flops=4 * count * count * experts,
    )
    every = lax.all_to_all(
        jnp.broadcast_to(hist[None], (devices, experts, BINS)), ("dp", "expert"), 0, 0, tiled=True
    )
    row_block = pl.BlockSpec((1, slots, features), lambda e: (e, 0, 0))
    g_sent = call(
        functools.partial(spread_kernel, slots),
        (experts,),
        (info, cot),
        [whole((8, count)), whole((count, features))],
        sent,
        row_block,
        flops=pair_cost,
    )
    g_rows = lax.all_to_all(g_sent, "expert", 0, 0, tiled=True)

    pairs = features // 128
    tile = lambda dtype: shape_of((count, features), dtype)
    full = (count, features)
    prob_block = pl.BlockSpec((2, count, count), lambda i: (i, 0, 0))
    hidden, normed, proj, mix, prob, normed_moe = call(
        attend_kernel,
        (pairs,),
        (tok, segment_ids.reshape(1, count), pad_mask.reshape(1, count), ga, w_qkv, w_o, gm),
        [whole(full), whole((1, count)), whole((1, count)), whole((1, features)), whole(w_qkv.shape), whole(w_o.shape), whole((1, features))],
        (tile(F32), tile(BF16), shape_of((count, 3 * features), BF16), tile(BF16), shape_of((HEADS, count, count), BF16), tile(BF16)),
        (whole_out(full), whole_out(full), whole_out((count, 3 * features)), whole_out(full), prob_block, whole_out(full)),
        [pltpu.VMEM((count, count), F32)],
        flops=16 * 10**9,
    )
    x_sent, kept = call(
        functools.partial(keep_kernel, slots, capacity),
        (experts,),
        (me.astype(jnp.int32).reshape(1), every, info, normed_moe),
        [pl.BlockSpec(memory_space=pltpu.SMEM), whole((devices, experts, BINS)), whole((8, count)), whole(full)],
        (sent, shape_of((8, count), jnp.int32)),
        (row_block, whole_out((8, count))),
        flops=pair_cost,
    )
    x_rows = lax.all_to_all(x_sent, "expert", 0, 0, tiled=True)

    hidden_units = w_in.shape[2]
    own = (iota((1, experts), 1) == lax.axis_index("expert")).astype(F32)
    flat = experts * slots
    unit_rows = shape_of((flat, hidden_units), BF16)
    unit_block = pl.BlockSpec((slots, hidden_units), lambda e: (e, 0))
    outs = call(
        functools.partial(expert_kernel, replicas),
        (experts,),
        (x_rows, g_rows, w_router, own, *[win[r] for r in range(replicas)], *[wout[r] for r in range(replicas)]),
        [row_block, row_block, whole(w_router.shape), whole((1, experts))]
        + [whole((features, hidden_units))] * replicas
        + [whole((hidden_units, features))] * replicas,
        (sent, sent, shape_of((flat, features), BF16), shape_of(w_router.shape, F32), *[unit_rows] * (2 * replicas)),
        (row_block, row_block, pl.BlockSpec((slots, features), lambda e: (e, 0)), whole_out(w_router.shape), *[unit_block] * (2 * replicas)),
        flops=8 * flat * features * hidden_units * replicas,
    )
    y_sent, d_sent, dexp, grad_router = outs[:4]
    act, dpre = outs[4 : 4 + replicas], outs[4 + replicas :]
    d_rows = lax.all_to_all(d_sent, "expert", 0, 0, tiled=True)
    y_rows = lax.all_to_all(y_sent, "expert", 0, 0, tiled=True)

    flat_x = x_rows.reshape(flat, features)
    gin = {r: dot(flat_x, dpre[r], 0, 0).astype(BF16) for r in range(replicas)}
    gout = {r: dot(act[r], dexp, 0, 0).astype(BF16) for r in range(replicas)}
    for bit in bits_of("dp"):
        for r in list(gin):
            if r & bit:
                other_in, other_out = swap(gin.pop(r), "dp", bit), swap(gout.pop(r), "dp", bit)
                sum_in = gin[r ^ bit].astype(F32) + other_in.astype(F32)
                sum_out = gout[r ^ bit].astype(F32) + other_out.astype(F32)
                last = len(gin) == 1
                gin[r ^ bit] = sum_in if last else sum_in.astype(BF16)
                gout[r ^ bit] = sum_out if last else sum_out.astype(BF16)

    gtok, gqkv, go, gains = call(
        attend_back_kernel,
        (pairs,),
        (kept, d_rows, hidden, cot, tok, ga, gm, w_qkv, w_o, normed, proj, mix, prob),
        [whole((8, count)), whole((experts, slots, features)), whole(full), whole(full), whole(full), whole((1, features)), whole((1, features)), whole(w_qkv.shape), whole(w_o.shape), whole(full), whole((count, 3 * features)), whole(full), prob_block],
        (tile(F32), shape_of(w_qkv.shape, BF16), shape_of(w_o.shape, BF16), shape_of((8, features), F32)),
        (whole_out(full), whole_out(w_qkv.shape), whole_out(w_o.shape), whole_out((8, features))),
        [pltpu.VMEM(full, F32), pltpu.VMEM(full, BF16), pltpu.VMEM((count, 3 * features), BF16)],
        flops=30 * 10**9,
    )
    block_out = call(
        block_kernel,
        (1,),
        (kept, y_rows, hidden),
        [whole((8, count)), whole((experts, slots, features)), whole(full)],
        tile(BF16),
        whole_out(full),
        flops=pair_cost,
    )
    small = jnp.concatenate(
        [gains[0].reshape(features, 1), gains[1].reshape(features, 1), grad_router], axis=1
    )
    small = jnp.pad(small, ((0, 0), (0, -small.shape[1] % 128))).astype(BF16)
    steps = [("dp", b) for b in bits_of("dp")] + [("expert", b) for b in bits_of("expert")]
    total = all_sum(jnp.concatenate([gqkv, go, small], axis=1), steps).astype(F32)
    edge = 3 * features
    return (
        block_out.reshape(sequences, length, features),
        gtok.reshape(sequences, length, features),
        total[:, edge + features],
        total[:, :edge],
        total[:, edge : edge + features],
        total[:, edge + features + 1],
        total[:, edge + features + 2 : edge + features + 2 + experts],
        gin[0][None],
        gout[0][None],
    )


def solution(mesh):
    rows = P(("dp", "expert"), None, None)
    flat = P(("dp", "expert"), None)
    first = P("expert", None, "dp")
    second = P("expert", "dp", None)
    return jax.shard_map(
        local,
        mesh=mesh,
        in_specs=(rows, flat, flat, rows, flat, P(), P(), P(), P(), P(), first, second, rows),
        out_specs=(rows, rows, P(), P(), P(), P(), P(), first, second),
        check_vma=False,
    )
```

```python
import functools

import jax
import jax.numpy as jnp
from jax import lax
from jax.experimental import pallas as pl
from jax.experimental.pallas import tpu as pltpu
from jax.sharding import PartitionSpec as P

HEADS = 12
HEAD_DIM = 64
LEVELS = 64
BINS = 2 * LEVELS
LIMIT = 60 * 1024 * 1024
F32 = jnp.float32
BF16 = jnp.bfloat16


def dot(a, b, ca=1, cb=0, precision=None):
    return lax.dot_general(
        a, b, (((ca,), (cb,)), ((), ())), precision=precision, preferred_element_type=F32
    )


def whole(shape):
    zeros = (0,) * len(shape)
    return pl.BlockSpec(shape, lambda *_: zeros, pipeline_mode=pl.Buffered(1))


def whole_out(shape):
    zeros = (0,) * len(shape)
    return pl.BlockSpec(shape, lambda *_: zeros)


def iota(shape, dim):
    return lax.broadcasted_iota(jnp.int32, shape, dim)


def call(kernel, grid, ins, in_specs, outs, out_specs, scratch=(), us=1, after=(), alias=()):
    late = len(after)

    def body(*refs):
        kernel(*refs[late:])

    return pl.pallas_call(
        body,
        grid=grid,
        in_specs=[pl.BlockSpec(memory_space=pl.ANY)] * late + in_specs,
        out_specs=out_specs,
        out_shape=outs,
        scratch_shapes=list(scratch),
        input_output_aliases={late + i: o for i, o in alias},
        compiler_params=pltpu.CompilerParams(vmem_limit_bytes=LIMIT),
        cost_estimate=pl.CostEstimate(flops=us * 10**6, bytes_accessed=0, transcendentals=0),
    )(*after, *ins)


def shape_of(shape, dtype):
    return jax.ShapeDtypeStruct(shape, dtype)


def norm_parts(values):
    center = values - jnp.mean(values, axis=-1, keepdims=True)
    spread = jnp.mean(center * center, axis=-1, keepdims=True)
    scale = lax.rsqrt(spread + 1e-06)
    return center * scale, scale


def norm_back(unit, scale, grad_unit):
    return scale * (
        grad_unit
        - jnp.mean(grad_unit, axis=-1, keepdims=True)
        - unit * jnp.mean(grad_unit * unit, axis=-1, keepdims=True)
    )


def class_rows(level_row, which, tokens):
    return (iota((BINS, tokens), 0) == which * LEVELS + (LEVELS - 1) - level_row).astype(F32)


def route_kernel(slots, experts, routes_ref, prio_ref, pad_ref, hist_ref, info_ref, target_ref):
    tokens = routes_ref.shape[0]
    pair_cols = routes_ref[...].astype(F32)
    pick = (iota((8, 2), 0) == iota((8, 2), 1)).astype(F32)
    rows = dot(pick, pair_cols, 1, 1)
    prio = prio_ref[...]
    valid = (pad_ref[...] > 0).astype(F32)
    early = iota((tokens, tokens), 0) < iota((tokens, tokens), 1)
    hot = [(iota((experts, tokens), 0) == rows[k : k + 1].astype(jnp.int32)).astype(F32) for k in (0, 1)]
    count = dot((hot[0] + hot[1]).astype(BF16), early.astype(BF16))
    hist = jnp.zeros((experts, BINS), F32)
    sides = jnp.where(iota((8, tokens), 0) == 0, prio.astype(F32), valid)
    eye = (iota((8, 8), 0) == iota((8, 8), 1)).astype(F32)
    cols = dot(sides, eye, 0, 0)
    prio_col = cols[:, 0:1]
    valid_col = cols[:, 1:2]
    for k in (0, 1):
        slot = jnp.sum(hot[k] * count, axis=0, keepdims=True)
        info_ref[k : k + 1, :] = rows[k : k + 1]
        info_ref[2 + k : 3 + k, :] = rows[k : k + 1] * slots + slot
        hist = hist + dot(hot[k] * valid, class_rows(prio, k, tokens), 1, 1)
        code_row = rows[k : k + 1] * LEVELS + prio.astype(F32)
        code_col = jnp.where(valid_col > 0, pair_cols[:, k : k + 1] * LEVELS + prio_col, -1.0)
        same = (code_col == code_row) & early
        info_ref[4 + k : 5 + k, :] = jnp.sum(same.astype(F32), axis=0, keepdims=True)
    info_ref[6:7, :] = prio.astype(F32)
    info_ref[7:8, :] = valid
    target_ref[...] = jnp.full(target_ref.shape, -1, jnp.int32)
    target_ref[0:2, :] = info_ref[2:4, :].astype(jnp.int32)
    hist_ref[...] = hist.astype(jnp.int32)


def slot_hot(target_rows, expert, slots, tokens):
    place = iota((slots, tokens), 0) + expert * slots
    return ((place == target_rows[0:1]) | (place == target_rows[1:2])).astype(F32).astype(BF16)


def spread_kernel(slots, spot_ref, target_ref, rows_ref, *out_refs):
    for j, out_ref in enumerate(out_refs):
        hot = slot_hot(target_ref[0:2, :], spot_ref[0] ^ j, slots, rows_ref.shape[0])
        out_ref[...] = dot(hot, rows_ref[...]).astype(BF16)


def spread_joint_kernel(slots, spot_ref, targetx_ref, targetg_ref, x_ref, g_ref, out_ref):
    expert, tokens = spot_ref[3] + pl.program_id(0), x_ref.shape[0]
    out_ref[0, :slots] = dot(slot_hot(targetx_ref[0:2, :], expert, slots, tokens), x_ref[...]).astype(BF16)
    out_ref[0, slots:] = dot(slot_hot(targetg_ref[0:2, :], expert, slots, tokens), g_ref[...]).astype(BF16)


def keep_kernel(
    capacity, me_ref, hist_ref, info_ref, target_ref, tok_ref, mix_ref, wo_ref, gm_ref,
    kept_ref, hidden_ref, nmoe_ref,
):
    devices, experts, bins = hist_ref.shape
    tokens = info_ref.shape[1]

    def add(j, sums):
        block = hist_ref[j].astype(F32)
        lower = (j < me_ref[0]).astype(F32)
        return sums[0] + block, sums[1] + block * lower

    zero = jnp.zeros((experts, bins), F32)
    totals, before = lax.fori_loop(0, devices, add, (zero, zero))
    early = (iota((bins, bins), 0) < iota((bins, bins), 1)).astype(F32)
    exact = lax.Precision.HIGHEST
    base = dot(totals, early, precision=exact) + before
    prio = info_ref[6:7, :].astype(jnp.int32)
    valid = info_ref[7:8, :] > 0
    kept_ref[...] = jnp.full(kept_ref.shape, -1, jnp.int32)
    for k in (0, 1):
        hot = (iota((experts, tokens), 0) == info_ref[k : k + 1, :].astype(jnp.int32)).astype(F32)
        spot = dot(base, class_rows(prio, k, tokens), precision=exact)
        rank = jnp.sum(hot * spot, axis=0, keepdims=True) + info_ref[4 + k : 5 + k, :]
        kept = valid & (rank < capacity - 0.5)
        kept_ref[k : k + 1, :] = jnp.where(kept, target_ref[k : k + 1, :], -1)
    hidden = tok_ref[...].astype(F32) + dot(mix_ref[...], wo_ref[...])
    hidden_ref[...] = hidden
    unit, _ = norm_parts(hidden)
    nmoe_ref[...] = (unit * gm_ref[...]).astype(BF16)


def attend_kernel(
    tok_ref, seg_ref, pad_ref, ga_ref, wqkv_ref, normed_ref, proj_ref, mix_ref, prob_ref, bias_ref,
):
    step = pl.program_id(0)
    tokens, features = tok_ref.shape

    @pl.when(step == 0)
    def _():
        unit, _ = norm_parts(tok_ref[...].astype(F32))
        normed = (unit * ga_ref[...]).astype(BF16)
        normed_ref[...] = normed
        for part in range(3):
            at = slice(part * features, (part + 1) * features)
            proj_ref[:, at] = dot(normed, wqkv_ref[:, at]).astype(BF16)
        seg = seg_ref[...].astype(F32)
        eye = (iota((8, 8), 0) == iota((8, 8), 1)).astype(F32)
        seg_col = dot(jnp.broadcast_to(seg, (8, tokens)), eye, 0, 0)[:, 0:1]
        own = iota((tokens, tokens), 0) == iota((tokens, tokens), 1)
        allowed = (seg_col == seg) & ((pad_ref[...] > 0) | own)
        bias_ref[...] = jnp.where(allowed, 0.0, -1e30)

    at = lambda part: pl.ds(pl.multiple_of(part * features + step * 128, 128), 128)
    query, keys, value = proj_ref[:, at(0)], proj_ref[:, at(1)], proj_ref[:, at(2)]
    first = iota((tokens, 128), 1) < HEAD_DIM
    mixed = []
    for h in (0, 1):
        mine = first if h == 0 else ~first
        own_query = jnp.where(mine, query.astype(F32) * HEAD_DIM ** (-0.5), 0.0).astype(BF16)
        scores = dot(own_query, keys, 1, 1) + bias_ref[...]
        top = jnp.max(scores, axis=-1, keepdims=True)
        exponent = jnp.exp(scores - top)
        total = jnp.sum(exponent, axis=-1, keepdims=True)
        prob = (exponent * (1.0 / total)).astype(BF16)
        prob_ref[h] = prob
        mixed.append(dot(prob, value))
    mix_ref[:, at(0)] = jnp.where(first, mixed[0], mixed[1]).astype(BF16)


def gather_rows(spot_ref, kept_ref, rows_refs):
    slots, features = rows_refs[0].shape
    tokens = kept_ref.shape[1]
    total = jnp.zeros((tokens, features), F32)
    for j, rows_ref in enumerate(rows_refs):
        hot = slot_hot(kept_ref[0:2, :], spot_ref[0] ^ j, slots, tokens)
        total = total + dot(hot, rows_ref[...], 0, 0)
    return total


def near_kernel(spot_ref, kept_ref, hidden_ref, *refs):
    d_ref, block_ref = refs[-2:]
    slots, tokens = refs[0].shape[0] // 2, kept_ref.shape[1]
    d_total = jnp.zeros(d_ref.shape, F32)
    y_total = hidden_ref[...]
    for j, rows_ref in enumerate(refs[:-2]):
        hot = slot_hot(kept_ref[0:2, :], spot_ref[0] ^ j, slots, tokens)
        d_total = d_total + dot(hot, rows_ref[:slots, :], 0, 0)
        y_total = y_total + dot(hot, rows_ref[slots:, :], 0, 0)
    d_ref[...] = d_total
    block_ref[...] = y_total


def gather_kernel(spot_ref, kept_ref, *refs):
    refs[-1][...] = gather_rows(spot_ref, kept_ref, refs[:-1]).astype(BF16)


def block_kernel(block_ref, far_ref, out_ref):
    out_ref[...] = (block_ref[...] + far_ref[...].astype(F32)).astype(BF16)


def left_grad_kernel(rows_ref, grad_ref, out_ref):
    out_ref[...] = dot(rows_ref[...], grad_ref[...], 0, 0).astype(BF16)


def right_grad_kernel(rows_ref, grad_ref, _, out_ref, __):
    out_ref[...] = dot(rows_ref[...], grad_ref[...], 0, 0).astype(BF16)


def halves_by(bit, value):
    rows = value.shape[0] // 2
    low, high = value[:rows], value[rows:]
    return jnp.where(bit > 0, high, low), jnp.where(bit > 0, low, high)


def as_column(row, column):
    at = (iota((8, 128), 1) == column) & (iota((8, 128), 0) == 0)
    return dot(jnp.broadcast_to(row, (8, row.shape[1])), at.astype(F32), 0, 0, lax.Precision.HIGHEST)


def hidden_back_kernel(
    spot_ref, near_ref, far_ref, hidden_ref, cot_ref, gm_ref, wo_ref, mix_ref, gwra_ref, gwrb_ref, _,
    dhid_ref, dmix_ref, keep_ref, give_ref, __,
):
    features = hidden_ref.shape[1]
    bit = spot_ref[1]
    grad = near_ref[...] + far_ref[...].astype(F32)
    unit, scale = norm_parts(hidden_ref[...])
    gain = jnp.sum(grad * unit, axis=0, keepdims=True)
    dhid = cot_ref[...].astype(F32) + norm_back(unit, scale, grad * gm_ref[...])
    dhid_ref[...] = dhid
    branch = dhid.astype(BF16)
    keep, give = halves_by(bit, dot(mix_ref[...], branch, 0, 0))
    keep_ref[:, :features], give_ref[:, :features] = keep.astype(BF16), give.astype(BF16)
    dmix_ref[...] = dot(branch, wo_ref[...], 1, 1).astype(BF16)
    experts = gwra_ref.shape[1]
    wide = (iota((experts, 128), 0) == iota((experts, 128), 1)).astype(F32)
    side = dot(gwra_ref[...] + gwrb_ref[...], wide, precision=lax.Precision.HIGHEST)
    side = side + as_column(gain, experts)
    keep, give = halves_by(bit, side)
    keep_ref[:, features:], give_ref[:, features:] = keep.astype(BF16), give.astype(BF16)


def head_pair_back(offset, dmix_ref, proj_ref, mix_ref, prob_ref, dproj_ref):
    step = pl.program_id(0)
    tokens, features = mix_ref.shape
    width = dproj_ref.shape[1] // 3
    at = lambda part: pl.ds(pl.multiple_of(part * features + (step + offset) * 128, 128), 128)
    query, keys, value = proj_ref[:, at(0)], proj_ref[:, at(1)], proj_ref[:, at(2)]
    dmix = dmix_ref[:, at(0)]
    product = dmix.astype(F32) * mix_ref[:, at(0)].astype(F32)
    first = iota((tokens, 128), 1) < HEAD_DIM
    parts = []
    for h in (0, 1):
        mine = first if h == 0 else ~first
        own_dmix = jnp.where(mine, dmix.astype(F32), 0.0).astype(BF16)
        delta = jnp.sum(jnp.where(mine, product, 0.0), axis=-1, keepdims=True)
        prob = prob_ref[h]
        dprob = dot(own_dmix, value, 1, 1)
        dscore = (prob.astype(F32) * (dprob - delta) * HEAD_DIM ** (-0.5)).astype(BF16)
        parts.append((dot(dscore, keys), dot(dscore, query, 0, 0), dot(prob, dmix, 0, 0)))
    for part in range(3):
        to = pl.ds(pl.multiple_of(part * width + step * 128, 128), 128)
        dproj_ref[:, to] = jnp.where(first, parts[0][part], parts[1][part]).astype(BF16)


def first_heads_kernel(
    spot_ref, dmix_ref, normed_ref, proj_ref, mix_ref, prob_ref, keep_ref, give_ref, dproj_ref,
):
    head_pair_back(0, dmix_ref, proj_ref, mix_ref, prob_ref, dproj_ref)

    @pl.when(pl.program_id(0) == pl.num_programs(0) - 1)
    def _():
        keep, give = halves_by(spot_ref[1], dot(normed_ref[...], dproj_ref[...], 0, 0))
        keep_ref[...], give_ref[...] = keep.astype(BF16), give.astype(BF16)


def last_heads_kernel(
    spot_ref, dmix_ref, normed_ref, proj_ref, mix_ref, prob_ref, other_ref, dhid_ref, tok_ref, ga_ref, wqkv_ref,
    gtok_ref, keep_ref, give_ref, dproj_ref,
):
    head_pair_back(pl.num_programs(0), dmix_ref, proj_ref, mix_ref, prob_ref, dproj_ref)
    tokens, features = tok_ref.shape
    width = dproj_ref.shape[1]

    @pl.when(pl.program_id(0) == pl.num_programs(0) - 1)
    def _():
        keep, give = halves_by(spot_ref[1], dot(normed_ref[...], dproj_ref[...], 0, 0))
        keep_ref[:, :width], give_ref[:, :width] = keep.astype(BF16), give.astype(BF16)
        grad = jnp.zeros((tokens, features), F32)
        half = features // 2
        for part in range(3):
            at = slice(part * half, (part + 1) * half)
            for place, ref in ((0, other_ref), (1, dproj_ref)):
                start = part * features + place * half
                grad = grad + dot(ref[:, at], wqkv_ref[:, start : start + half], 1, 1)
        unit, scale = norm_parts(tok_ref[...].astype(F32))
        gtok_ref[...] = dhid_ref[...] + norm_back(unit, scale, grad * ga_ref[...])
        side = as_column(jnp.sum(grad * unit, axis=0, keepdims=True), 0)
        keep, give = halves_by(spot_ref[1], side)
        keep_ref[:, width:], give_ref[:, width:] = keep.astype(BF16), give.astype(BF16)


def take(refs, count):
    return refs[:count], refs[count:]


def expert_kernel(pieces, group, near, *refs):
    step = pl.program_id(0)
    (spot_ref, wr_ref, own_ref, win_ref, wout_ref), refs = take(refs, 5)
    mine = (spot_ref[0] - spot_ref[3]) ^ step
    if near:
        x_refs, refs = take(refs, group)
        g_refs, refs = take(refs, group)
        back_refs, refs = take(refs, group)
    else:
        (far_ref,), refs = take(refs, 1)
        refs = refs[4:]
        dx_refs, refs = take(refs, group)
        y_refs, refs = take(refs, group)
    gwr_ref, dexp_ref, xcopy_ref, act_ref, dpre_ref, now_ref = refs
    slots = dexp_ref.shape[0]
    if near:
        for j in range(group):

            @pl.when(step == j)
            def _():
                xcopy_ref[...] = x_refs[j][...]
                now_ref[...] = g_refs[j][...]

    else:
        xcopy_ref[...] = far_ref[mine, :slots, :]
        now_ref[...] = far_ref[mine, slots:, :]

    x = xcopy_ref[...]
    g = now_ref[...].astype(F32)
    logits = dot(x, wr_ref[...])
    exponent = jnp.exp(logits - jnp.max(logits, axis=-1, keepdims=True))
    router = exponent / jnp.sum(exponent, axis=-1, keepdims=True)
    gate = jnp.sum(router * own_ref[...], axis=-1, keepdims=True)
    dexp = (gate * g).astype(BF16)
    dexp_ref[...] = dexp
    out = jnp.zeros(x.shape, F32)
    dx = jnp.zeros(x.shape, F32)
    width = win_ref.shape[1] // pieces
    for r in range(pieces):
        at = slice(r * width, (r + 1) * width)
        pre = dot(x, win_ref[:, at])
        square = pre * pre
        bend = jnp.tanh(0.7978845608028654 * pre * (1.0 + 0.044715 * square))
        half = 0.5 * (1.0 + bend)
        slope = half + (0.5 * 0.7978845608028654) * pre * (1.0 - bend * bend) * (1.0 + 0.134145 * square)
        active = (pre * half).astype(BF16)
        act_ref[:, at] = active
        dpreact = (dot(dexp, wout_ref[at, :], 1, 1) * slope).astype(BF16)
        dpre_ref[:, at] = dpreact
        out = out + dot(active, wout_ref[at, :])
        dx = dx + dot(dpreact, win_ref[:, at], 1, 1)
    out = out.astype(BF16).astype(F32)
    y = (gate * out).astype(BF16)
    dgate = jnp.sum(g * out, axis=-1, keepdims=True)
    dlogits = (dgate * gate * (own_ref[...] - router)).astype(BF16)
    dx = (dx + dot(dlogits, wr_ref[...], 1, 1)).astype(BF16)
    if near:
        for j in range(group):

            @pl.when(step == j)
            def _():
                back_refs[j][:slots, :] = dx
                back_refs[j][slots:, :] = y

    else:
        for j in range(group):

            @pl.when(step == j)
            def _():
                y_refs[j][...] = y
                dx_refs[j][...] = dx

    @pl.when(step == 0)
    def _():
        gwr_ref[...] = jnp.zeros(gwr_ref.shape, F32)

    gwr_ref[...] += dot(x, dlogits, 0, 0)


def swap(value, axis, bit):
    size = lax.axis_size(axis)
    return lax.ppermute(value, axis, [(i, i ^ bit) for i in range(size)])


def bits_of(axis):
    size = lax.axis_size(axis)
    return [1 << b for b in range(size.bit_length() - 1)]


def half_sum_kernel(at, spot_ref, keep_ref, other_ref, next_ref, give_ref):
    total = keep_ref[...].astype(F32) + other_ref[...].astype(F32)
    keep, give = halves_by(spot_ref[at], total)
    next_ref[...], give_ref[...] = keep.astype(BF16), give.astype(BF16)


def deal_kernel(groups, spot_ref, keep_ref, other_ref, own_ref, *refs):
    out_refs, total_ref = refs[:-1], refs[-1]
    total = keep_ref[...].astype(F32) + other_ref[...].astype(F32)
    rows, columns = total.shape
    total_ref[...] = total.reshape(groups, rows // groups, columns)
    own_ref[...] = total_ref[spot_ref[5]]
    for j, out_ref in enumerate(out_refs):
        out_ref[...] = total_ref[spot_ref[5] ^ (j + 1)].astype(BF16)


def pile_kernel(own_ref, *refs):
    total = own_ref[...]
    for ref in refs[:-1]:
        total = total + ref[...].astype(F32)
    refs[-1][...] = total.astype(BF16)


def line_up_kernel(spot_ref, *refs):
    out_ref, total_ref = refs[-2:]
    for j, ref in enumerate(refs[:-2]):
        total_ref[spot_ref[5] ^ j] = ref[...].astype(F32)
    out_ref[...] = total_ref[...].reshape(out_ref.shape).astype(BF16)


def finish_kernel(orders, spot_ref, *refs):
    piece_refs, out_refs = refs[: 8 * len(orders)], refs[8 * len(orders) :]
    for place, (first, second, targets) in enumerate(orders):
        for k in range(8):
            ref = piece_refs[8 * place + k]
            rows = ref.shape[0]
            spot = (
                (spot_ref[1] ^ (k >> 2)) * 4 + (spot_ref[first] ^ (k >> 1 & 1)) * 2 + (spot_ref[second] ^ (k & 1))
            )
            at = pl.ds(pl.multiple_of(spot * rows, 8), rows)
            for start, width, out, column in targets:
                out_refs[out][at, column : column + width] = ref[:, start : start + width].astype(F32)


LINKS = {2: ("dp", 2), 4: ("expert", 1)}


def halve(spot, at, keep, arrived, *after):
    scalar = pl.BlockSpec(memory_space=pltpu.SMEM)
    part = (keep.shape[0] // 2, keep.shape[1])
    keep, give = call(
        functools.partial(half_sum_kernel, at), (1,), (spot, keep, arrived),
        [scalar, whole(keep.shape), whole(keep.shape)],
        [shape_of(part, BF16)] * 2, [whole_out(part)] * 2,
        after=after,
    )
    return keep, swap(give, *LINKS[at])


def deal_out(spot, keep, arrived, groups):
    scalar = pl.BlockSpec(memory_space=pltpu.SMEM)
    rows, columns = keep.shape
    piece = (rows // groups, columns)
    dealt = call(
        functools.partial(deal_kernel, groups), (1,), (spot, keep, arrived),
        [scalar, whole(keep.shape), whole(keep.shape)],
        (shape_of(piece, F32), *[shape_of(piece, BF16)] * (groups - 1)),
        (whole_out(piece),) * groups,
        [pltpu.VMEM((groups, *piece), F32)],
    )
    total = call(
        pile_kernel, (1,), (dealt[0], *[swap(v, "expert", 2 * (j + 1)) for j, v in enumerate(dealt[1:])]),
        [whole(piece)] * groups, shape_of(piece, BF16), whole_out(piece),
    )
    own = call(
        line_up_kernel, (1,), (spot, total, *[swap(total, "expert", 2 * j) for j in range(1, groups)]),
        [scalar] + [whole(piece)] * groups,
        shape_of(keep.shape, BF16), whole_out(keep.shape), [pltpu.VMEM((groups, *piece), F32)],
    )
    pieces = [own]
    for link in (LINKS[4], LINKS[2], ("dp", 1)):
        pieces = pieces + [swap(v, *link) for v in pieces]
    return pieces


def all_sum(value, steps):
    rows = value.shape[0]
    place = []
    for axis, bit in steps:
        half = value.shape[0] // 2
        mine = ((lax.axis_index(axis) & bit) > 0).astype(jnp.int32)
        keep = lax.dynamic_slice_in_dim(value, mine * half, half, 0)
        give = lax.dynamic_slice_in_dim(value, (1 - mine) * half, half, 0)
        value = (keep.astype(F32) + swap(give, axis, bit).astype(F32)).astype(BF16)
        place.append(mine)
    for (axis, bit), mine in zip(reversed(steps), reversed(place)):
        other = swap(value, axis, bit)
        low = jnp.where(mine > 0, other, value)
        high = jnp.where(mine > 0, value, other)
        value = jnp.concatenate([low, high], axis=0)
    return value


def local(
    tokens, segment_ids, pad_mask, routes, priority, gain_attn, w_qkv, w_o, gain_moe, w_router,
    w_in, w_out, cotangent,
):
    sequences, length, features = tokens.shape
    count = sequences * length
    experts = w_router.shape[1]
    groups = lax.axis_size("expert")
    replicas = lax.axis_size("dp")
    devices = groups * replicas
    group = groups // 2
    most = 4 * count // experts
    slots = -(-most // 16) * 16
    capacity = (42 * count * devices + 20 * experts - 1) // (20 * experts)
    me = lax.axis_index(("dp", "expert")).astype(jnp.int32).reshape(1)
    replica = lax.axis_index("dp")
    column = lax.axis_index("expert")
    spot = jnp.stack(
        [column, replica & 1, replica >> 1 & 1, column // group * group, column & 1, column >> 1]
    ).astype(jnp.int32)
    tok = tokens.reshape(count, features)
    cot = cotangent.reshape(count, features)
    ga = gain_attn.reshape(1, features)
    gm = gain_moe.reshape(1, features)
    full = (count, features)
    scalar = pl.BlockSpec(memory_space=pltpu.SMEM)
    sent = shape_of((slots, features), BF16)

    def across(value):
        return swap(value, "expert", group)

    def among(values):
        return [v if j == 0 else swap(v, "expert", j) for j, v in enumerate(values)]

    def spread(target, rows, us, *after):
        return call(
            functools.partial(spread_kernel, slots),
            (1,),
            (spot, target, rows),
            [scalar, whole((8, count)), whole(full)],
            [sent] * group,
            [whole_out((slots, features))] * group,
            us=us,
            after=after,
        )

    halves = [list(range(group)), list(range(group, groups))]
    joint = (group, 2 * slots, features)

    def half_exchange(value):
        return lax.all_to_all(value, "expert", 0, 0, axis_index_groups=halves, tiled=True)

    far_cot = across(cot)
    full_in = lax.all_gather(w_in[0], "dp", axis=1, tiled=True)
    full_out = lax.all_gather(w_out[0], "dp", axis=0, tiled=True)

    hist, info, target = call(
        functools.partial(route_kernel, slots, experts),
        (1,),
        (routes.reshape(count, 2), priority.reshape(1, count), pad_mask.reshape(1, count)),
        [whole((count, 2)), whole((1, count)), whole((1, count))],
        (shape_of((experts, BINS), jnp.int32), shape_of((8, count), F32), shape_of((8, count), jnp.int32)),
        (whole_out((experts, BINS)), whole_out((8, count)), whole_out((8, count))),
    )
    far_target = across(target)
    near_g_sent = spread(target, cot, 1)
    near_g = among(near_g_sent)
    every = lax.all_to_all(
        jnp.broadcast_to(hist[None], (devices, experts, BINS)), ("dp", "expert"), 0, 0, tiled=True
    )

    pairs = features // 128
    tile = lambda dtype: shape_of((count, features), dtype)
    prob_block = pl.BlockSpec((2, count, count), lambda i: (i, 0, 0))
    normed, proj, mix, prob = call(
        attend_kernel,
        (pairs,),
        (tok, segment_ids.reshape(1, count), pad_mask.reshape(1, count), ga, w_qkv),
        [whole(full), whole((1, count)), whole((1, count)), whole((1, features)), whole(w_qkv.shape)],
        (tile(BF16), shape_of((count, 3 * features), BF16), tile(BF16), shape_of((HEADS, count, count), BF16)),
        (whole_out(full), whole_out((count, 3 * features)), whole_out(full), prob_block),
        [pltpu.VMEM((count, count), F32)],
        us=20000,
        after=(near_g_sent[0],),
    )
    kept, hidden, normed_moe = call(
        functools.partial(keep_kernel, capacity),
        (1,),
        (me, every, info, target, tok, mix, w_o, gm),
        [scalar, whole((devices, experts, BINS)), whole((8, count)), whole((8, count)), whole(full), whole(full), whole(w_o.shape), whole((1, features))],
        (shape_of((8, count), jnp.int32), tile(F32), tile(BF16)),
        (whole_out((8, count)), whole_out(full), whole_out(full)),
    )
    far_x = across(normed_moe)
    far_kept = across(kept)
    near_x = spread(kept, normed_moe, 20000, *near_g)
    near_x_sent, near_x = near_x, among(near_x)
    far_sent = call(
        functools.partial(spread_joint_kernel, slots),
        (group,),
        (spot, far_kept, far_target, far_x, far_cot),
        [scalar] + [whole((8, count))] * 2 + [whole(full)] * 2,
        shape_of(joint, BF16),
        pl.BlockSpec((1, 2 * slots, features), lambda e: (e, 0, 0)),
        after=(near_x_sent[0], *near_x[1:]),
    )
    far_rows = half_exchange(far_sent)

    hidden_units = w_out.shape[1] * replicas
    own = (iota((1, experts), 1) == column).astype(F32)
    flat = group * slots
    slot_spec = whole_out((slots, features))
    weights = (spot, w_router, own, full_in, full_out)
    weight_specs = [scalar, whole(w_router.shape), whole((1, experts)), whole(full_in.shape), whole(full_out.shape)]
    tall = [shape_of((2 * flat, n), BF16) for n in (features, features, hidden_units, hidden_units)]
    tall_blocks = lambda first: [
        pl.BlockSpec((slots, v.shape[1]), lambda e: (first + e, 0)) for v in tall
    ]
    outs = call(
        functools.partial(expert_kernel, 4, group, True),
        (group,),
        (*weights, *near_x, *near_g),
        weight_specs + [whole((slots, features))] * (2 * group),
        (*[shape_of((2 * slots, features), BF16)] * group, shape_of(w_router.shape, F32), *tall),
        (*[whole_out((2 * slots, features))] * group, whole_out(w_router.shape), *tall_blocks(0)),
        [pltpu.VMEM((slots, features), BF16)],
        us=35000,
        after=(far_sent,),
    )
    near_back, outs = take(outs, group)
    near_back = among(near_back)
    gwr_a, kept_rows = outs[0], outs[1:]
    outs = call(
        functools.partial(expert_kernel, 4, group, False),
        (group,),
        (*weights, far_rows, *kept_rows),
        weight_specs + [whole(joint)] + [pl.BlockSpec(memory_space=pl.ANY)] * 4,
        (*[sent] * (2 * group), shape_of(w_router.shape, F32), *tall),
        (*[slot_spec] * (2 * group), whole_out(w_router.shape), *tall_blocks(group)),
        [pltpu.VMEM((slots, features), BF16)],
        after=(gwr_a,),
        alias=[(6 + i, 2 * group + 1 + i) for i in range(4)],
    )
    d_far, outs = take(outs, group)
    y_far, outs = take(outs, group)
    gwr_b, all_dexp, all_x, all_act, all_dpre = outs
    d_far, y_far = among(d_far), among(y_far)
    near_d, block_part = call(
        near_kernel,
        (1,),
        (spot, kept, hidden, *near_back),
        [scalar, whole((8, count)), whole(full)] + [whole((2 * slots, features))] * group,
        (tile(F32), tile(F32)),
        (whole_out(full), whole_out(full)),
        after=(gwr_b,),
    )

    def gather(rows, *after):
        return call(
            gather_kernel,
            (1,),
            (spot, far_kept, *rows),
            [scalar, whole((8, count))] + [whole((slots, features))] * group,
            tile(BF16),
            whole_out(full),
            after=after,
        )

    anywhere = pl.BlockSpec(memory_space=pl.ANY)
    part = hidden_units // 4
    gout = call(
        left_grad_kernel,
        (4,),
        (all_act, all_dexp),
        [pl.BlockSpec((2 * flat, part), lambda i: (0, i)), whole((2 * flat, features))],
        shape_of((hidden_units, features), BF16),
        pl.BlockSpec((part, features), lambda i: (i, 0)),
        after=(near_d,),
    )
    d_far = gather(d_far, gout)
    gin, gout = call(
        right_grad_kernel,
        (4,),
        (all_x, all_dpre, gout),
        [whole((2 * flat, features)), pl.BlockSpec((2 * flat, part), lambda i: (0, i)), anywhere],
        (shape_of((features, hidden_units), BF16), shape_of((hidden_units, features), BF16)),
        (pl.BlockSpec((features, part), lambda i: (0, i)), anywhere),
        after=(d_far,),
        alias=[(2, 1)],
    )
    y_far = gather(y_far, gin)
    d_far = across(d_far)
    gout = lax.psum_scatter(gout, "dp", scatter_dimension=0, tiled=True).astype(F32)
    gin = lax.psum_scatter(gin, "dp", scatter_dimension=1, tiled=True).astype(F32)

    o_half = (features // 2, features + 128)
    a_half = (features // 2, 3 * features // 2)
    b_half = (features // 2, 3 * features // 2 + 128)
    dhid, dmix, keep_o, give_o, y_far = call(
        hidden_back_kernel,
        (1,),
        (spot, near_d, d_far, hidden, cot, gm, w_o, mix, gwr_a, gwr_b, y_far),
        [scalar] + [whole(full)] * 4 + [whole((1, features)), whole(w_o.shape), whole(full)] + [whole(gwr_a.shape)] * 2 + [anywhere],
        (tile(F32), tile(BF16), *[shape_of(o_half, BF16)] * 2, tile(BF16)),
        (whole_out(full), whole_out(full), *[whole_out(o_half)] * 2, anywhere),
        alias=[(10, 4)],
    )
    y_far = across(y_far)
    some = 3 * features // 2
    head_specs = lambda offset: [scalar] + [whole(full)] * 2 + [whole((count, 3 * features)), whole(full)] + [
        pl.BlockSpec((2, count, count), lambda i: (i + offset, 0, 0))
    ]
    keep_a, give_a, dproj_a = call(
        first_heads_kernel,
        (pairs // 2,),
        (spot, dmix, normed, proj, mix, prob),
        head_specs(0),
        (shape_of(a_half, BF16), shape_of(a_half, BF16), shape_of((count, some), BF16)),
        (whole_out(a_half), whole_out(a_half), whole_out((count, some))),
        us=13000,
    )
    by_hand = replicas == 4 and groups == 8 and features % (8 * devices) == 0
    if by_hand:
        sum_o = halve(spot, 2, keep_o, swap(give_o, "dp", 1), dproj_a)
    gtok, keep_b, give_b = call(
        last_heads_kernel,
        (pairs // 2,),
        (spot, dmix, normed, proj, mix, prob, dproj_a, dhid, tok, ga, w_qkv),
        head_specs(pairs // 2) + [whole((count, some)), whole(full), whole(full), whole((1, features)), whole(w_qkv.shape)],
        (tile(F32), shape_of(b_half, BF16), shape_of(b_half, BF16)),
        (whole_out(full), whole_out(b_half), whole_out(b_half)),
        [pltpu.VMEM((count, some), BF16)],
        us=14000,
        after=sum_o[:1] if by_hand else (),
    )
    block_out = call(
        block_kernel,
        (1,),
        (block_part, y_far),
        [whole(full)] * 2,
        tile(BF16),
        whole_out(full),
        after=(gtok,),
    )
    if by_hand:
        rows = groups // 2
        sum_a = halve(spot, 2, keep_a, swap(give_a, "dp", 1), gtok)
        sum_o = halve(spot, 4, *sum_o)
        sum_b = halve(spot, 2, keep_b, swap(give_b, "dp", 1), sum_o[0], sum_a[0])
        sum_a = halve(spot, 4, *sum_a)
        sum_b = halve(spot, 4, *sum_b)
        pieces = [v for total in (sum_o, sum_a, sum_b) for v in deal_out(spot, *total, rows)]
        half = features // 2
        heads = lambda place: tuple(
            (part * half, half, 2, part * features + place * half) for part in range(3)
        )
        orders = (
            (2, 4, ((0, features, 0, 0), (features, 128, 1, 0))),
            (2, 4, heads(0)),
            (2, 4, heads(1) + ((some, 128, 3, 0),)),
        )
        shapes = [(features, features), (features, 128), (features, 3 * features), (features, 128)]
        grad_o, side_o, grad_qkv, side_q = call(
            functools.partial(finish_kernel, orders),
            (1,),
            (spot, *pieces),
            [scalar] + [whole(v.shape) for v in pieces],
            [shape_of(v, F32) for v in shapes],
            [whole_out(v) for v in shapes],
            after=(gin, gout),
        )
    else:
        low = (replica & 1) == 0

        def rejoin(keep, give):
            return jnp.concatenate([jnp.where(low, keep, give), jnp.where(low, give, keep)], axis=0)

        gain_steps = [("dp", b) for b in bits_of("dp")] + [("expert", b) for b in bits_of("expert")]
        both = all_sum(rejoin(keep_o, give_o), gain_steps).astype(F32)
        grad_o, side_o = both[:, :features], both[:, features:]
        first = all_sum(rejoin(keep_a, give_a), gain_steps).astype(F32)
        last = all_sum(rejoin(keep_b, give_b), gain_steps).astype(F32)
        half = features // 2
        cut = lambda part: slice(part * half, (part + 1) * half)
        grad_qkv = jnp.concatenate([v[:, cut(part)] for part in range(3) for v in (first, last)], axis=1)
        side_q = last[:, some:]
    return (
        block_out.reshape(sequences, length, features),
        gtok.reshape(sequences, length, features),
        side_q[:, 0],
        grad_qkv,
        grad_o,
        side_o[:, experts],
        side_o[:, :experts],
        gin[None],
        gout[None],
    )


def solution(mesh):
    rows = P(("dp", "expert"), None, None)
    flat = P(("dp", "expert"), None)
    first = P("expert", None, "dp")
    second = P("expert", "dp", None)
    return jax.shard_map(
        local,
        mesh=mesh,
        in_specs=(rows, flat, flat, rows, flat, P(), P(), P(), P(), P(), first, second, rows),
        out_specs=(rows, rows, P(), P(), P(), P(), P(), first, second),
        check_vma=False,
    )
```

```python
import functools

import jax
import jax.numpy as jnp
from jax import lax
from jax.experimental import pallas as pl
from jax.experimental.pallas import tpu as pltpu
from jax.sharding import PartitionSpec as P

HEADS = 12
HEAD_DIM = 64
LEVELS = 64
BINS = 2 * LEVELS
LIMIT = 60 * 1024 * 1024
F32 = jnp.float32
BF16 = jnp.bfloat16


def dot(a, b, ca=1, cb=0, precision=None):
    return lax.dot_general(
        a, b, (((ca,), (cb,)), ((), ())), precision=precision, preferred_element_type=F32
    )


def whole(shape):
    zeros = (0,) * len(shape)
    return pl.BlockSpec(shape, lambda *_: zeros, pipeline_mode=pl.Buffered(1))


def whole_out(shape):
    zeros = (0,) * len(shape)
    return pl.BlockSpec(shape, lambda *_: zeros)


def iota(shape, dim):
    return lax.broadcasted_iota(jnp.int32, shape, dim)


def call(kernel, grid, ins, in_specs, outs, out_specs, scratch=(), us=1, after=(), alias=()):
    late = len(after)

    def body(*refs):
        kernel(*refs[late:])

    return pl.pallas_call(
        body,
        grid=grid,
        in_specs=[pl.BlockSpec(memory_space=pl.ANY)] * late + in_specs,
        out_specs=out_specs,
        out_shape=outs,
        scratch_shapes=list(scratch),
        input_output_aliases={late + i: o for i, o in alias},
        compiler_params=pltpu.CompilerParams(vmem_limit_bytes=LIMIT),
        cost_estimate=pl.CostEstimate(flops=us * 10**6, bytes_accessed=0, transcendentals=0),
    )(*after, *ins)


def shape_of(shape, dtype):
    return jax.ShapeDtypeStruct(shape, dtype)


def norm_parts(values):
    center = values - jnp.mean(values, axis=-1, keepdims=True)
    spread = jnp.mean(center * center, axis=-1, keepdims=True)
    scale = lax.rsqrt(spread + 1e-06)
    return center * scale, scale


def norm_back(unit, scale, grad_unit):
    return scale * (
        grad_unit
        - jnp.mean(grad_unit, axis=-1, keepdims=True)
        - unit * jnp.mean(grad_unit * unit, axis=-1, keepdims=True)
    )


def class_rows(level_row, which, tokens):
    return (iota((BINS, tokens), 0) == which * LEVELS + (LEVELS - 1) - level_row).astype(F32)


def route_kernel(slots, experts, routes_ref, prio_ref, pad_ref, hist_ref, info_ref, target_ref):
    tokens = routes_ref.shape[0]
    pair_cols = routes_ref[...].astype(F32)
    pick = (iota((8, 2), 0) == iota((8, 2), 1)).astype(F32)
    rows = dot(pick, pair_cols, 1, 1)
    prio = prio_ref[...]
    valid = (pad_ref[...] > 0).astype(F32)
    early = iota((tokens, tokens), 0) < iota((tokens, tokens), 1)
    hot = [(iota((experts, tokens), 0) == rows[k : k + 1].astype(jnp.int32)).astype(F32) for k in (0, 1)]
    count = dot((hot[0] + hot[1]).astype(BF16), early.astype(BF16))
    hist = jnp.zeros((experts, BINS), F32)
    sides = jnp.where(iota((8, tokens), 0) == 0, prio.astype(F32), valid)
    eye = (iota((8, 8), 0) == iota((8, 8), 1)).astype(F32)
    cols = dot(sides, eye, 0, 0)
    prio_col = cols[:, 0:1]
    valid_col = cols[:, 1:2]
    for k in (0, 1):
        slot = jnp.sum(hot[k] * count, axis=0, keepdims=True)
        info_ref[k : k + 1, :] = rows[k : k + 1]
        info_ref[2 + k : 3 + k, :] = rows[k : k + 1] * slots + slot
        hist = hist + dot(hot[k] * valid, class_rows(prio, k, tokens), 1, 1)
        code_row = rows[k : k + 1] * LEVELS + prio.astype(F32)
        code_col = jnp.where(valid_col > 0, pair_cols[:, k : k + 1] * LEVELS + prio_col, -1.0)
        same = (code_col == code_row) & early
        info_ref[4 + k : 5 + k, :] = jnp.sum(same.astype(F32), axis=0, keepdims=True)
    info_ref[6:7, :] = prio.astype(F32)
    info_ref[7:8, :] = valid
    target_ref[...] = jnp.full(target_ref.shape, -1, jnp.int32)
    target_ref[0:2, :] = info_ref[2:4, :].astype(jnp.int32)
    hist_ref[...] = jnp.broadcast_to(hist.astype(jnp.int32)[None], hist_ref.shape)


def slot_hot(target_rows, expert, slots, tokens):
    place = iota((slots, tokens), 0) + expert * slots
    return ((place == target_rows[0:1]) | (place == target_rows[1:2])).astype(F32).astype(BF16)


def spread_kernel(slots, spot_ref, target_ref, rows_ref, *out_refs):
    tokens = target_ref.shape[1]
    for j, out_ref in enumerate(out_refs):
        hot = slot_hot(target_ref[0:2, :], spot_ref[0] ^ j, slots, tokens)
        out_ref[...] = dot(hot, rows_ref[:tokens, :]).astype(BF16)


def spread_joint_kernel(slots, spot_ref, x_ref, g_ref, out_ref, kept_ref):
    expert, tokens = spot_ref[3] + pl.program_id(0), g_ref.shape[0]

    @pl.when(pl.program_id(0) == 0)
    def _():
        codes = x_ref[tokens:, :tokens].astype(F32).astype(jnp.int32)
        kept_ref[...] = jnp.full(kept_ref.shape, -1, jnp.int32)
        for k in (0, 1):
            kept_ref[k : k + 1, :] = codes[2 * k : 2 * k + 1] * 64 + codes[2 * k + 1 : 2 * k + 2] - 1

    hot = slot_hot(kept_ref[0:2, :], expert, slots, tokens)
    out_ref[0, :slots] = dot(hot, x_ref[:tokens, :]).astype(BF16)
    out_ref[0, slots:] = dot(hot, g_ref[...]).astype(BF16)


def hidden_kernel(
    capacity, me_ref, hist_ref, info_ref, target_ref, tok_ref, mix_ref, wo_ref, gm_ref,
    hidden_ref, cross_ref, kept_ref,
):
    devices, experts, bins = hist_ref.shape
    tokens = info_ref.shape[1]
    hidden = tok_ref[...].astype(F32) + dot(mix_ref[...], wo_ref[...])
    hidden_ref[...] = hidden
    unit, _ = norm_parts(hidden)
    cross_ref[:tokens, :] = (unit * gm_ref[...]).astype(BF16)

    def add(j, sums):
        block = hist_ref[j].astype(F32)
        lower = (j < me_ref[0]).astype(F32)
        return sums[0] + block, sums[1] + block * lower

    zero = jnp.zeros((experts, bins), F32)
    totals, before = lax.fori_loop(0, devices, add, (zero, zero))
    early = (iota((bins, bins), 0) < iota((bins, bins), 1)).astype(F32)
    exact = lax.Precision.HIGHEST
    base = dot(totals, early, precision=exact) + before
    prio = info_ref[6:7, :].astype(jnp.int32)
    valid = info_ref[7:8, :] > 0
    kept_ref[...] = jnp.full(kept_ref.shape, -1, jnp.int32)
    codes = jnp.zeros((16, tokens), jnp.int32)
    row = iota((16, tokens), 0)
    for k in (0, 1):
        hot = (iota((experts, tokens), 0) == info_ref[k : k + 1, :].astype(jnp.int32)).astype(F32)
        spot = dot(base, class_rows(prio, k, tokens), precision=exact)
        rank = jnp.sum(hot * spot, axis=0, keepdims=True) + info_ref[4 + k : 5 + k, :]
        kept = valid & (rank < capacity - 0.5)
        place = jnp.where(kept, target_ref[k : k + 1, :], -1)
        kept_ref[k : k + 1, :] = place
        codes = jnp.where(row == 2 * k, (place + 1) >> 6, codes)
        codes = jnp.where(row == 2 * k + 1, (place + 1) & 63, codes)
    cross_ref[tokens:, :] = jnp.zeros((16, cross_ref.shape[1]), BF16)
    cross_ref[tokens:, :tokens] = codes.astype(F32).astype(BF16)


def project_kernel(tok_ref, ga_ref, wqkv_ref, normed_ref, proj_ref):
    unit, _ = norm_parts(tok_ref[...].astype(F32))
    normed = (unit * ga_ref[...]).astype(BF16)
    normed_ref[...] = normed
    features = tok_ref.shape[1]
    for part in range(3):
        at = slice(part * features, (part + 1) * features)
        proj_ref[:, at] = dot(normed, wqkv_ref[:, at]).astype(BF16)


def attend_kernel(query_ref, keys_ref, value_ref, seg_ref, pad_ref, mix_ref, prob_ref, bias_ref):
    step = pl.program_id(0)
    tokens = query_ref.shape[0]

    @pl.when(step == 0)
    def _():
        seg = seg_ref[...].astype(F32)
        eye = (iota((8, 8), 0) == iota((8, 8), 1)).astype(F32)
        seg_col = dot(jnp.broadcast_to(seg, (8, tokens)), eye, 0, 0)[:, 0:1]
        own = iota((tokens, tokens), 0) == iota((tokens, tokens), 1)
        allowed = (seg_col == seg) & ((pad_ref[...] > 0) | own)
        bias_ref[...] = jnp.where(allowed, 0.0, -1e30)

    query, keys, value = query_ref[...], keys_ref[...], value_ref[...]
    first = iota((tokens, 128), 1) < HEAD_DIM
    mixed = []
    for h in (0, 1):
        mine = first if h == 0 else ~first
        own_query = jnp.where(mine, query.astype(F32) * HEAD_DIM ** (-0.5), 0.0).astype(BF16)
        scores = dot(own_query, keys, 1, 1) + bias_ref[...]
        top = jnp.max(scores, axis=-1, keepdims=True)
        exponent = jnp.exp(scores - top)
        total = jnp.sum(exponent, axis=-1, keepdims=True)
        prob = (exponent * (1.0 / total)).astype(BF16)
        prob_ref[h] = prob
        mixed.append(dot(prob, value))
    mix_ref[...] = jnp.where(first, mixed[0], mixed[1]).astype(BF16)


def gather_rows(spot_ref, kept_ref, rows_refs):
    slots, features = rows_refs[0].shape
    tokens = kept_ref.shape[1]
    total = jnp.zeros((tokens, features), F32)
    for j, rows_ref in enumerate(rows_refs):
        hot = slot_hot(kept_ref[0:2, :], spot_ref[0] ^ j, slots, tokens)
        total = total + dot(hot, rows_ref[...], 0, 0)
    return total


def near_kernel(spot_ref, kept_ref, hidden_ref, *refs):
    d_ref, block_ref = refs[-2:]
    slots, tokens = refs[0].shape[0] // 2, kept_ref.shape[1]
    d_total = jnp.zeros(d_ref.shape, F32)
    y_total = hidden_ref[...]
    for j, rows_ref in enumerate(refs[:-2]):
        hot = slot_hot(kept_ref[0:2, :], spot_ref[0] ^ j, slots, tokens)
        d_total = d_total + dot(hot, rows_ref[:slots, :], 0, 0)
        y_total = y_total + dot(hot, rows_ref[slots:, :], 0, 0)
    d_ref[...] = d_total
    block_ref[...] = y_total


def gather_pass_kernel(group, spot_ref, kept_ref, *refs):
    refs[2 * group][...] = gather_rows(spot_ref, kept_ref, refs[:group]).astype(BF16)


def gather_kernel(spot_ref, kept_ref, *refs):
    refs[-1][...] = gather_rows(spot_ref, kept_ref, refs[:-1]).astype(BF16)


def block_kernel(block_ref, far_ref, out_ref):
    out_ref[...] = (block_ref[...] + far_ref[...].astype(F32)).astype(BF16)


def weight_grad_kernel(rows_ref, grad_ref, *refs):
    refs[-1][0] = dot(rows_ref[...], grad_ref[...], 0, 0).astype(BF16)


def widen_kernel(both_ref, in_ref, out_ref):
    in_ref[...] = both_ref[0].astype(F32).T
    out_ref[...] = both_ref[1].astype(F32)


def halves_by(bit, value):
    rows = value.shape[0] // 2
    low, high = value[:rows], value[rows:]
    return jnp.where(bit > 0, high, low), jnp.where(bit > 0, low, high)


def as_column(row, column):
    at = (iota((8, 128), 1) == column) & (iota((8, 128), 0) == 0)
    return dot(jnp.broadcast_to(row, (8, row.shape[1])), at.astype(F32), 0, 0, lax.Precision.HIGHEST)


def hidden_back_kernel(
    spot_ref, near_ref, far_ref, hidden_ref, cot_ref, gm_ref, wo_ref, mix_ref, gwra_ref, gwrb_ref, _,
    dhid_ref, dmix_ref, keep_ref, give_ref, __,
):
    features = hidden_ref.shape[1]
    bit = spot_ref[1]
    grad = near_ref[...] + far_ref[...].astype(F32)
    unit, scale = norm_parts(hidden_ref[...])
    gain = jnp.sum(grad * unit, axis=0, keepdims=True)
    dhid = cot_ref[...].astype(F32) + norm_back(unit, scale, grad * gm_ref[...])
    dhid_ref[...] = dhid
    branch = dhid.astype(BF16)
    keep, give = halves_by(bit, dot(mix_ref[...], branch, 0, 0))
    keep_ref[:, :features], give_ref[:, :features] = keep.astype(BF16), give.astype(BF16)
    dmix_ref[...] = dot(branch, wo_ref[...], 1, 1).astype(BF16)
    experts = gwra_ref.shape[1]
    wide = (iota((experts, 128), 0) == iota((experts, 128), 1)).astype(F32)
    side = dot(gwra_ref[...] + gwrb_ref[...], wide, precision=lax.Precision.HIGHEST)
    side = side + as_column(gain, experts)
    keep, give = halves_by(bit, side)
    keep_ref[:, features:], give_ref[:, features:] = keep.astype(BF16), give.astype(BF16)


def head_pair_back(offset, dmix_ref, proj_ref, mix_ref, prob_ref, dproj_ref):
    step = pl.program_id(0)
    tokens, features = mix_ref.shape
    width = dproj_ref.shape[1] // 3
    at = lambda part: pl.ds(pl.multiple_of(part * features + (step + offset) * 128, 128), 128)
    query, keys, value = proj_ref[:, at(0)], proj_ref[:, at(1)], proj_ref[:, at(2)]
    dmix = dmix_ref[:, at(0)]
    product = dmix.astype(F32) * mix_ref[:, at(0)].astype(F32)
    first = iota((tokens, 128), 1) < HEAD_DIM
    parts = []
    for h in (0, 1):
        mine = first if h == 0 else ~first
        own_dmix = jnp.where(mine, dmix.astype(F32), 0.0).astype(BF16)
        delta = jnp.sum(jnp.where(mine, product, 0.0), axis=-1, keepdims=True)
        prob = prob_ref[h]
        dprob = dot(own_dmix, value, 1, 1)
        dscore = (prob.astype(F32) * (dprob - delta) * HEAD_DIM ** (-0.5)).astype(BF16)
        parts.append((dot(dscore, keys), dot(dscore, query, 0, 0), dot(prob, dmix, 0, 0)))
    for part in range(3):
        to = pl.ds(pl.multiple_of(part * width + step * 128, 128), 128)
        dproj_ref[:, to] = jnp.where(first, parts[0][part], parts[1][part]).astype(BF16)


def first_heads_kernel(
    spot_ref, dmix_ref, normed_ref, proj_ref, mix_ref, prob_ref, keep_ref, give_ref, dproj_ref,
):
    head_pair_back(0, dmix_ref, proj_ref, mix_ref, prob_ref, dproj_ref)

    @pl.when(pl.program_id(0) == pl.num_programs(0) - 1)
    def _():
        keep, give = halves_by(spot_ref[1], dot(normed_ref[...], dproj_ref[...], 0, 0))
        keep_ref[...], give_ref[...] = keep.astype(BF16), give.astype(BF16)


def last_heads_kernel(
    spot_ref, dmix_ref, normed_ref, proj_ref, mix_ref, prob_ref, other_ref, dhid_ref, tok_ref, ga_ref, wqkv_ref,
    gtok_ref, keep_ref, give_ref, dproj_ref,
):
    head_pair_back(pl.num_programs(0), dmix_ref, proj_ref, mix_ref, prob_ref, dproj_ref)
    tokens, features = tok_ref.shape
    width = dproj_ref.shape[1]

    @pl.when(pl.program_id(0) == pl.num_programs(0) - 1)
    def _():
        keep, give = halves_by(spot_ref[1], dot(normed_ref[...], dproj_ref[...], 0, 0))
        keep_ref[:, :width], give_ref[:, :width] = keep.astype(BF16), give.astype(BF16)
        grad = jnp.zeros((tokens, features), F32)
        half = features // 2
        for part in range(3):
            at = slice(part * half, (part + 1) * half)
            for place, ref in ((0, other_ref), (1, dproj_ref)):
                start = part * features + place * half
                grad = grad + dot(ref[:, at], wqkv_ref[:, start : start + half], 1, 1)
        unit, scale = norm_parts(tok_ref[...].astype(F32))
        gtok_ref[...] = dhid_ref[...] + norm_back(unit, scale, grad * ga_ref[...])
        side = as_column(jnp.sum(grad * unit, axis=0, keepdims=True), 0)
        keep, give = halves_by(spot_ref[1], side)
        keep_ref[:, width:], give_ref[:, width:] = keep.astype(BF16), give.astype(BF16)


def take(refs, count):
    return refs[:count], refs[count:]


def expert_kernel(pieces, group, near, *refs):
    step = pl.program_id(0)
    (spot_ref, wr_ref, own_ref, win_ref, wout_ref), refs = take(refs, 5)
    mine = (spot_ref[0] - spot_ref[3]) ^ step
    if near:
        x_refs, refs = take(refs, group)
        g_refs, refs = take(refs, group)
        back_refs, refs = take(refs, group)
    else:
        (far_ref,), refs = take(refs, 1)
        refs = refs[4:]
        dx_refs, refs = take(refs, group)
        y_refs, refs = take(refs, group)
    gwr_ref, dexp_ref, xcopy_ref, act_ref, dpre_ref, now_ref = refs
    slots = dexp_ref.shape[0]
    if near:
        for j in range(group):

            @pl.when(step == j)
            def _():
                xcopy_ref[...] = x_refs[j][...]
                now_ref[...] = g_refs[j][...]

    else:
        xcopy_ref[...] = far_ref[mine, :slots, :]
        now_ref[...] = far_ref[mine, slots:, :]

    x = xcopy_ref[...]
    g = now_ref[...].astype(F32)
    logits = dot(x, wr_ref[...])
    exponent = jnp.exp(logits - jnp.max(logits, axis=-1, keepdims=True))
    router = exponent / jnp.sum(exponent, axis=-1, keepdims=True)
    gate = jnp.sum(router * own_ref[...], axis=-1, keepdims=True)
    dexp = (gate * g).astype(BF16)
    dexp_ref[...] = dexp
    out = jnp.zeros(x.shape, F32)
    dx = jnp.zeros(x.shape, F32)
    width = win_ref.shape[1] // pieces
    for r in range(pieces):
        at = slice(r * width, (r + 1) * width)
        pre = dot(x, win_ref[:, at])
        square = pre * pre
        bend = jnp.tanh(0.7978845608028654 * pre * (1.0 + 0.044715 * square))
        half = 0.5 * (1.0 + bend)
        slope = half + (0.5 * 0.7978845608028654) * pre * (1.0 - bend * bend) * (1.0 + 0.134145 * square)
        active = (pre * half).astype(BF16)
        act_ref[:, at] = active
        dpreact = (dot(dexp, wout_ref[at, :], 1, 1) * slope).astype(BF16)
        dpre_ref[:, at] = dpreact
        out = out + dot(active, wout_ref[at, :])
        dx = dx + dot(dpreact, win_ref[:, at], 1, 1)
    out = out.astype(BF16).astype(F32)
    y = (gate * out).astype(BF16)
    dgate = jnp.sum(g * out, axis=-1, keepdims=True)
    dlogits = (dgate * gate * (own_ref[...] - router)).astype(BF16)
    dx = (dx + dot(dlogits, wr_ref[...], 1, 1)).astype(BF16)
    if near:
        for j in range(group):

            @pl.when(step == j)
            def _():
                back_refs[j][:slots, :] = dx
                back_refs[j][slots:, :] = y

    else:
        for j in range(group):

            @pl.when(step == j)
            def _():
                y_refs[j][...] = y
                dx_refs[j][...] = dx

    @pl.when(step == 0)
    def _():
        gwr_ref[...] = jnp.zeros(gwr_ref.shape, F32)

    gwr_ref[...] += dot(x, dlogits, 0, 0)


def swap(value, axis, bit):
    size = lax.axis_size(axis)
    return lax.ppermute(value, axis, [(i, i ^ bit) for i in range(size)])


def bits_of(axis):
    size = lax.axis_size(axis)
    return [1 << b for b in range(size.bit_length() - 1)]


def deal_plane_kernel(spot_ref, *refs):
    in_refs, (own_ref, *out_refs, total_ref) = refs[:-5], refs[-5:]
    start = 0
    for keep_ref, other_ref in zip(in_refs[::2], in_refs[1::2]):
        total = keep_ref[...].astype(F32) + other_ref[...].astype(F32)
        rows, columns = total.shape
        total_ref[:, :, start : start + columns] = total.reshape(4, rows // 4, columns)
        start += columns
    spot = spot_ref[2] * 2 + spot_ref[4]
    own_ref[...] = total_ref[spot]
    for j, out_ref in enumerate(out_refs):
        out_ref[...] = total_ref[spot ^ (j + 1)].astype(BF16)


def deal_line_kernel(groups, spot_ref, own_ref, *refs):
    in_refs, (first_ref, *out_refs, total_ref) = refs[:3], refs[3:]
    total = own_ref[...]
    for ref in in_refs:
        total = total + ref[...].astype(F32)
    rows, columns = total.shape
    total_ref[...] = total.reshape(groups, rows // groups, columns)
    first_ref[...] = total_ref[spot_ref[5]]
    for j, out_ref in enumerate(out_refs):
        out_ref[...] = total_ref[spot_ref[5] ^ (j + 1)].astype(BF16)


def pile_kernel(own_ref, *refs):
    total = own_ref[...]
    for ref in refs[:-1]:
        total = total + ref[...].astype(F32)
    refs[-1][...] = total.astype(BF16)


def line_up_kernel(spot_ref, *refs):
    out_ref, total_ref = refs[-2:]
    for j, ref in enumerate(refs[:-2]):
        total_ref[spot_ref[5] ^ j] = ref[...].astype(F32)
    out_ref[...] = total_ref[...].reshape(out_ref.shape).astype(BF16)


def line_up_plane_kernel(spot_ref, *refs):
    out_ref, total_ref = refs[-2:]
    for j, ref in enumerate(refs[:-2]):
        total_ref[(spot_ref[2] * 2 + spot_ref[4]) ^ j] = ref[...]
    out_ref[...] = total_ref[...].reshape(out_ref.shape)


def finish_kernel(orders, experts, spot_ref, *refs):
    piece_refs, refs = take(refs, 2 * len(orders))
    grad_o_ref, grad_qkv_ref, gain_attn_ref, gain_moe_ref, router_ref, side_o_ref, side_q_ref = refs
    out_refs = grad_o_ref, side_o_ref, grad_qkv_ref, side_q_ref
    for place, targets in enumerate(orders):
        for k in range(2):
            ref = piece_refs[2 * place + k]
            rows = ref.shape[0]
            at = pl.ds(pl.multiple_of((spot_ref[1] ^ k) * rows, 8), rows)
            for start, width, out, column in targets:
                out_refs[out][at, column : column + width] = ref[:, start : start + width].astype(F32)
    side_o = side_o_ref[...]
    router_ref[...] = side_o[:, :experts]
    gain_moe_ref[...] = side_o.T[experts : experts + 1, :]
    gain_attn_ref[...] = side_q_ref[...].T[0:1, :]


def plane_swap(value, j):
    groups = lax.axis_size("expert")
    size = lax.axis_size("dp") * groups
    apart = (j >> 1) * 2 * groups + (j & 1)
    return lax.ppermute(value, ("dp", "expert"), [(i, i ^ apart) for i in range(size)])


def plane_deal(spot, halves, *after):
    scalar = pl.BlockSpec(memory_space=pltpu.SMEM)
    ins = [v for pair in halves for v in pair]
    rows, columns = halves[0][0].shape[0] // 4, sum(pair[0].shape[1] for pair in halves)
    piece = (rows, columns)
    return call(
        deal_plane_kernel, (1,), (spot, *ins), [scalar] + [whole(v.shape) for v in ins],
        [shape_of(piece, F32)] + [shape_of(piece, BF16)] * 3, [whole_out(piece)] * 4,
        [pltpu.VMEM((4, *piece), F32)],
        after=after,
    )


def line_deal(spot, dealt, groups, us, *after):
    scalar = pl.BlockSpec(memory_space=pltpu.SMEM)
    own, *out = dealt
    rows, columns = own.shape
    piece = (rows // groups, columns)
    arrived = [plane_swap(v, j + 1) for j, v in enumerate(out)]
    scratch = [pltpu.VMEM((groups, *piece), F32)]
    own, *out = call(
        functools.partial(deal_line_kernel, groups), (1,), (spot, own, *arrived),
        [scalar] + [whole((rows, columns))] * 4,
        (shape_of(piece, F32), *[shape_of(piece, BF16)] * (groups - 1)),
        (whole_out(piece),) * groups,
        scratch,
        us=us,
        after=after,
    )
    return [own] + [swap(v, "expert", 2 * (j + 1)) for j, v in enumerate(out)]


def line_up(spot, parts, *late_pile):
    scalar = pl.BlockSpec(memory_space=pltpu.SMEM)
    groups, piece = len(parts), parts[0].shape
    rows, columns = groups * piece[0], piece[1]
    scratch = [pltpu.VMEM((groups, *piece), F32)]
    total = call(
        pile_kernel, (1,), parts, [whole(piece)] * groups, shape_of(piece, BF16), whole_out(piece),
        after=late_pile,
    )
    own = call(
        line_up_kernel, (1,), (spot, total, *[swap(total, "expert", 2 * j) for j in range(1, groups)]),
        [scalar] + [whole(piece)] * groups,
        shape_of((rows, columns), BF16), whole_out((rows, columns)), scratch,
    )
    return own, [plane_swap(own, j) for j in (1, 2, 3)]


def line_up_plane(spot, own, arrived, *after):
    scalar = pl.BlockSpec(memory_space=pltpu.SMEM)
    rows, columns = own.shape
    half = (4 * rows, columns)
    own = call(
        line_up_plane_kernel, (1,), (spot, own, *arrived),
        [scalar] + [whole((rows, columns))] * 4,
        shape_of(half, BF16), whole_out(half), [pltpu.VMEM((4, rows, columns), BF16)],
        after=after,
    )
    return [own, swap(own, "dp", 1)]


def all_sum(value, steps):
    rows = value.shape[0]
    place = []
    for axis, bit in steps:
        half = value.shape[0] // 2
        mine = ((lax.axis_index(axis) & bit) > 0).astype(jnp.int32)
        keep = lax.dynamic_slice_in_dim(value, mine * half, half, 0)
        give = lax.dynamic_slice_in_dim(value, (1 - mine) * half, half, 0)
        value = (keep.astype(F32) + swap(give, axis, bit).astype(F32)).astype(BF16)
        place.append(mine)
    for (axis, bit), mine in zip(reversed(steps), reversed(place)):
        other = swap(value, axis, bit)
        low = jnp.where(mine > 0, other, value)
        high = jnp.where(mine > 0, value, other)
        value = jnp.concatenate([low, high], axis=0)
    return value


def local(
    tokens, segment_ids, pad_mask, routes, priority, gain_attn, w_qkv, w_o, gain_moe, w_router,
    w_in, w_out, cotangent,
):
    sequences, length, features = tokens.shape
    count = sequences * length
    experts = w_router.shape[1]
    groups = lax.axis_size("expert")
    replicas = lax.axis_size("dp")
    devices = groups * replicas
    group = groups // 2
    most = 4 * count // experts
    slots = -(-most // 16) * 16
    capacity = (42 * count * devices + 20 * experts - 1) // (20 * experts)
    me = lax.axis_index(("dp", "expert")).astype(jnp.int32).reshape(1)
    replica = lax.axis_index("dp")
    column = lax.axis_index("expert")
    spot = jnp.stack(
        [column, replica & 1, replica >> 1 & 1, column // group * group, column & 1, column >> 1]
    ).astype(jnp.int32)
    tok = tokens.reshape(count, features)
    cot = cotangent.reshape(count, features)
    ga = gain_attn.reshape(1, features)
    gm = gain_moe.reshape(1, features)
    full = (count, features)
    scalar = pl.BlockSpec(memory_space=pltpu.SMEM)
    sent = shape_of((slots, features), BF16)

    def across(value):
        return swap(value, "expert", group)

    def among(values):
        return [v if j == 0 else swap(v, "expert", j) for j, v in enumerate(values)]

    halves = [list(range(group)), list(range(group, groups))]
    joint = (group, 2 * slots, features)

    def half_exchange(value):
        return lax.all_to_all(value, "expert", 0, 0, axis_index_groups=halves, tiled=True)

    far_cot = across(cot)
    full_in = lax.all_gather(w_in[0], "dp", axis=1, tiled=True)
    full_out = lax.all_gather(w_out[0], "dp", axis=0, tiled=True)

    pairs = features // 128
    tile = lambda dtype: shape_of((count, features), dtype)
    prob_block = pl.BlockSpec((2, count, count), lambda i: (i, 0, 0))
    hist_shape = (devices, experts, BINS)
    hist, info, target = call(
        functools.partial(route_kernel, slots, experts),
        (1,),
        (routes.reshape(count, 2), priority.reshape(1, count), pad_mask.reshape(1, count)),
        [whole((count, 2)), whole((1, count)), whole((1, count))],
        (shape_of(hist_shape, jnp.int32), shape_of((8, count), F32), shape_of((8, count), jnp.int32)),
        (whole_out(hist_shape), whole_out((8, count)), whole_out((8, count))),
    )
    def spread(target, rows, us, *after):
        return call(
            functools.partial(spread_kernel, slots),
            (1,),
            (spot, target, rows),
            [scalar, whole((8, count)), whole(rows.shape)],
            [sent] * group,
            [whole_out((slots, features))] * group,
            us=us,
            after=after,
        )

    near_g_sent = spread(target, cot, 1)
    near_g = among(near_g_sent)
    every = lax.all_to_all(hist, ("dp", "expert"), 0, 0, tiled=True)
    normed, proj = call(
        project_kernel,
        (1,),
        (tok, ga, w_qkv),
        [whole(full), whole((1, features)), whole(w_qkv.shape)],
        (tile(BF16), shape_of((count, 3 * features), BF16)),
        (whole_out(full), whole_out((count, 3 * features))),
        after=(near_g_sent[0],),
    )
    lanes = lambda part: pl.BlockSpec((count, 128), lambda i: (0, part * pairs + i))
    mix, prob = call(
        attend_kernel,
        (pairs,),
        (proj, proj, proj, segment_ids.reshape(1, count), pad_mask.reshape(1, count)),
        [lanes(0), lanes(1), lanes(2), whole((1, count)), whole((1, count))],
        (tile(BF16), shape_of((HEADS, count, count), BF16)),
        (lanes(0), prob_block),
        [pltpu.VMEM((count, count), F32)],
        us=20000,
        after=(target,),
    )
    cross_shape = (count + 16, features)
    hidden, cross, kept = call(
        functools.partial(hidden_kernel, capacity),
        (1,),
        (me, every, info, target, tok, mix, w_o, gm),
        [scalar, whole(hist_shape), whole((8, count)), whole((8, count)), whole(full), whole(full), whole(w_o.shape), whole((1, features))],
        (tile(F32), shape_of(cross_shape, BF16), shape_of((8, count), jnp.int32)),
        (whole_out(full), whole_out(cross_shape), whole_out((8, count))),
    )
    far_x = across(cross)
    near_sent = spread(kept, cross, 20000, *near_g)
    near_x = among(near_sent)
    far_sent, far_kept = call(
        functools.partial(spread_joint_kernel, slots),
        (group,),
        (spot, far_x, far_cot),
        [scalar, whole(cross_shape), whole(full)],
        (shape_of(joint, BF16), shape_of((8, count), jnp.int32)),
        (pl.BlockSpec((1, 2 * slots, features), lambda e: (e, 0, 0)), whole_out((8, count))),
        after=(near_sent[0],),
    )
    far_rows = half_exchange(far_sent)

    hidden_units = w_out.shape[1] * replicas
    own = (iota((1, experts), 1) == column).astype(F32)
    flat = group * slots
    slot_spec = whole_out((slots, features))
    weights = (spot, w_router, own, full_in, full_out)
    weight_specs = [scalar, whole(w_router.shape), whole((1, experts)), whole(full_in.shape), whole(full_out.shape)]
    tall = [shape_of((2 * flat, n), BF16) for n in (features, features, hidden_units, hidden_units)]
    tall_blocks = lambda first: [
        pl.BlockSpec((slots, v.shape[1]), lambda e: (first + e, 0)) for v in tall
    ]
    outs = call(
        functools.partial(expert_kernel, 4, group, True),
        (group,),
        (*weights, *near_x, *near_g),
        weight_specs + [whole((slots, features))] * (2 * group),
        (*[shape_of((2 * slots, features), BF16)] * group, shape_of(w_router.shape, F32), *tall),
        (*[whole_out((2 * slots, features))] * group, whole_out(w_router.shape), *tall_blocks(0)),
        [pltpu.VMEM((slots, features), BF16)],
        us=300000,
        after=(far_sent,),
    )
    near_back, outs = take(outs, group)
    near_back = among(near_back)
    gwr_a, kept_rows = outs[0], outs[1:]
    outs = call(
        functools.partial(expert_kernel, 4, group, False),
        (group,),
        (*weights, far_rows, *kept_rows),
        weight_specs + [whole(joint)] + [pl.BlockSpec(memory_space=pl.ANY)] * 4,
        (*[sent] * (2 * group), shape_of(w_router.shape, F32), *tall),
        (*[slot_spec] * (2 * group), whole_out(w_router.shape), *tall_blocks(group)),
        [pltpu.VMEM((slots, features), BF16)],
        after=(gwr_a,),
        alias=[(6 + i, 2 * group + 1 + i) for i in range(4)],
    )
    d_far, outs = take(outs, group)
    y_far, outs = take(outs, group)
    gwr_b, all_dexp, all_x, all_act, all_dpre = outs
    d_far = among(d_far)
    def gather(rows, *after):
        return call(
            gather_kernel,
            (1,),
            (spot, far_kept, *rows),
            [scalar, whole((8, count))] + [whole((slots, features))] * group,
            tile(BF16),
            whole_out(full),
            after=after,
        )

    anywhere = pl.BlockSpec(memory_space=pl.ANY)
    part = hidden_units // 4
    both_shape = shape_of((2, hidden_units, features), BF16)

    def weight_grad(which, rows, grad, us, after, *given):
        return call(
            weight_grad_kernel,
            (4,),
            (rows, grad, *given),
            [pl.BlockSpec((2 * flat, part), lambda i: (0, i)), whole((2 * flat, features))] + [anywhere] * len(given),
            both_shape,
            pl.BlockSpec((1, part, features), lambda i: (which, i, 0)),
            us=us,
            after=after,
            alias=[(2, 0)] if given else (),
        )

    both = weight_grad(1, all_act, all_dexp, 1, near_back)
    d_far, *y_far = call(
        functools.partial(gather_pass_kernel, group),
        (1,),
        (spot, far_kept, *d_far, *y_far),
        [scalar, whole((8, count))] + [whole((slots, features))] * group + [anywhere] * group,
        [tile(BF16)] + [sent] * group,
        [whole_out(full)] + [anywhere] * group,
        after=(both,),
        alias=[(2 + group + j, 1 + j) for j in range(group)],
    )
    y_far = among(y_far)
    both = weight_grad(0, all_dpre, all_x, 60000, (d_far,), both)
    near_d, block_part = call(
        near_kernel,
        (1,),
        (spot, kept, hidden, *near_back),
        [scalar, whole((8, count)), whole(full)] + [whole((2 * slots, features))] * group,
        (tile(F32), tile(F32)),
        (whole_out(full), whole_out(full)),
        after=(both,),
    )

    y_far = gather(y_far, near_d)
    d_far = across(d_far)
    both = lax.psum_scatter(both, "dp", scatter_dimension=1, tiled=True)

    o_half = (features // 2, features + 128)
    a_half = (features // 2, 3 * features // 2)
    b_half = (features // 2, 3 * features // 2 + 128)
    dhid, dmix, keep_o, give_o, y_far = call(
        hidden_back_kernel,
        (1,),
        (spot, near_d, d_far, hidden, cot, gm, w_o, mix, gwr_a, gwr_b, y_far),
        [scalar] + [whole(full)] * 4 + [whole((1, features)), whole(w_o.shape), whole(full)] + [whole(gwr_a.shape)] * 2 + [anywhere],
        (tile(F32), tile(BF16), *[shape_of(o_half, BF16)] * 2, tile(BF16)),
        (whole_out(full), whole_out(full), *[whole_out(o_half)] * 2, anywhere),
        us=400000,
        alias=[(10, 4)],
    )
    y_far = across(y_far)
    some = 3 * features // 2
    head_specs = lambda offset: [scalar] + [whole(full)] * 2 + [whole((count, 3 * features)), whole(full)] + [
        pl.BlockSpec((2, count, count), lambda i: (i + offset, 0, 0))
    ]
    keep_a, give_a, dproj_a = call(
        first_heads_kernel,
        (pairs // 2,),
        (spot, dmix, normed, proj, mix, prob),
        head_specs(0),
        (shape_of(a_half, BF16), shape_of(a_half, BF16), shape_of((count, some), BF16)),
        (whole_out(a_half), whole_out(a_half), whole_out((count, some))),
        us=13000,
    )
    by_hand = replicas == 4 and groups == 8 and features % (8 * devices) == 0
    if by_hand:
        beside = lambda keep, give: (keep, swap(give, "dp", 1))
        early = plane_deal(spot, [beside(keep_o, give_o), beside(keep_a, give_a)])
    gtok, keep_b, give_b = call(
        last_heads_kernel,
        (pairs // 2,),
        (spot, dmix, normed, proj, mix, prob, dproj_a, dhid, tok, ga, w_qkv),
        head_specs(pairs // 2) + [whole((count, some)), whole(full), whole(full), whole((1, features)), whole(w_qkv.shape)],
        (tile(F32), shape_of(b_half, BF16), shape_of(b_half, BF16)),
        (whole_out(full), whole_out(b_half), whole_out(b_half)),
        [pltpu.VMEM((count, some), BF16)],
        us=4000,
        after=early[:1] if by_hand else (),
    )
    block_out = call(
        block_kernel,
        (1,),
        (block_part, y_far),
        [whole(full)] * 2,
        tile(BF16),
        whole_out(full),
        after=(gtok,),
    )
    shapes = [w_in.shape[1:], w_out.shape[1:]]
    gin, gout = call(
        widen_kernel,
        (1,),
        (both,),
        [whole(both.shape)],
        [shape_of(v, F32) for v in shapes],
        [whole_out(v) for v in shapes],
        after=(gtok,),
    )
    if by_hand:
        rows = groups // 2
        early = line_deal(spot, early, rows, 30000, gtok)
        late = plane_deal(spot, [beside(keep_b, give_b)], early[0])
        early, early_parts = line_up(spot, early, late[0], y_far)
        late, late_parts = line_up(spot, line_deal(spot, late, rows, 1, early))
        pieces = line_up_plane(spot, early, early_parts, late) + line_up_plane(
            spot, late, late_parts, gin, block_out
        )
        half = features // 2
        heads = lambda start, place: tuple(
            (start + part * half, half, 2, part * features + place * half) for part in range(3)
        )
        orders = (
            ((0, features, 0, 0), (features, 128, 1, 0)) + heads(features + 128, 0),
            heads(0, 1) + ((some, 128, 3, 0),),
        )
        shapes = [(features, features), (features, 3 * features), (1, features), (1, features), (features, experts)]
        grad_o, grad_qkv, gain_attn_grad, gain_moe_grad, grad_router = call(
            functools.partial(finish_kernel, orders, experts),
            (1,),
            (spot, *pieces),
            [scalar] + [whole(v.shape) for v in pieces],
            [shape_of(v, F32) for v in shapes],
            [whole_out(v) for v in shapes],
            [pltpu.VMEM((features, 128), F32)] * 2,
        )
    else:
        low = (replica & 1) == 0

        def rejoin(keep, give):
            return jnp.concatenate([jnp.where(low, keep, give), jnp.where(low, give, keep)], axis=0)

        gain_steps = [("dp", b) for b in bits_of("dp")] + [("expert", b) for b in bits_of("expert")]
        both = all_sum(rejoin(keep_o, give_o), gain_steps).astype(F32)
        grad_o, side_o = both[:, :features], both[:, features:]
        first = all_sum(rejoin(keep_a, give_a), gain_steps).astype(F32)
        last = all_sum(rejoin(keep_b, give_b), gain_steps).astype(F32)
        half = features // 2
        cut = lambda part: slice(part * half, (part + 1) * half)
        grad_qkv = jnp.concatenate([v[:, cut(part)] for part in range(3) for v in (first, last)], axis=1)
        gain_attn_grad, gain_moe_grad = last[:, some], side_o[:, experts]
        grad_router = side_o[:, :experts]
    return (
        block_out.reshape(sequences, length, features),
        gtok.reshape(sequences, length, features),
        gain_attn_grad.reshape(features),
        grad_qkv,
        grad_o,
        gain_moe_grad.reshape(features),
        grad_router,
        gin[None],
        gout[None],
    )


def solution(mesh):
    rows = P(("dp", "expert"), None, None)
    flat = P(("dp", "expert"), None)
    first = P("expert", None, "dp")
    second = P("expert", "dp", None)
    return jax.shard_map(
        local,
        mesh=mesh,
        in_specs=(rows, flat, flat, rows, flat, P(), P(), P(), P(), P(), first, second, rows),
        out_specs=(rows, rows, P(), P(), P(), P(), P(), first, second),
        check_vma=False,
    )
```

```python
import functools

import jax
import jax.numpy as jnp
from jax import lax
from jax.experimental import pallas as pl
from jax.experimental.pallas import tpu as pltpu
from jax.sharding import PartitionSpec as P

HEADS = 12
HEAD_DIM = 64
LEVELS = 64
BINS = 2 * LEVELS
LIMIT = 60 * 1024 * 1024
F32 = jnp.float32
BF16 = jnp.bfloat16


def dot(a, b, ca=1, cb=0, precision=None):
    return lax.dot_general(
        a, b, (((ca,), (cb,)), ((), ())), precision=precision, preferred_element_type=F32
    )


def whole(shape):
    zeros = (0,) * len(shape)
    return pl.BlockSpec(shape, lambda *_: zeros, pipeline_mode=pl.Buffered(1))


def whole_out(shape):
    zeros = (0,) * len(shape)
    return pl.BlockSpec(shape, lambda *_: zeros)


def iota(shape, dim):
    return lax.broadcasted_iota(jnp.int32, shape, dim)


def call(kernel, grid, ins, in_specs, outs, out_specs, scratch=(), us=1, after=(), alias=()):
    late = len(after)

    def body(*refs):
        kernel(*refs[late:])

    return pl.pallas_call(
        body,
        grid=grid,
        in_specs=[pl.BlockSpec(memory_space=pl.ANY)] * late + in_specs,
        out_specs=out_specs,
        out_shape=outs,
        scratch_shapes=list(scratch),
        input_output_aliases={late + i: o for i, o in alias},
        compiler_params=pltpu.CompilerParams(vmem_limit_bytes=LIMIT),
        cost_estimate=pl.CostEstimate(flops=us * 10**6, bytes_accessed=0, transcendentals=0),
    )(*after, *ins)


def shape_of(shape, dtype):
    return jax.ShapeDtypeStruct(shape, dtype)


def norm_parts(values):
    center = values - jnp.mean(values, axis=-1, keepdims=True)
    spread = jnp.mean(center * center, axis=-1, keepdims=True)
    scale = lax.rsqrt(spread + 1e-06)
    return center * scale, scale


def norm_back(unit, scale, grad_unit):
    return scale * (
        grad_unit
        - jnp.mean(grad_unit, axis=-1, keepdims=True)
        - unit * jnp.mean(grad_unit * unit, axis=-1, keepdims=True)
    )


def class_rows(level_row, which, tokens):
    return (iota((BINS, tokens), 0) == which * LEVELS + (LEVELS - 1) - level_row).astype(F32)


def route_kernel(slots, experts, routes_ref, prio_ref, pad_ref, hist_ref, info_ref, target_ref):
    tokens = routes_ref.shape[1]
    rows = routes_ref[...].astype(F32)
    prio = prio_ref[...]
    valid = (pad_ref[...] > 0).astype(F32)
    early = iota((tokens, tokens), 0) < iota((tokens, tokens), 1)
    hot = [(iota((experts, tokens), 0) == rows[k : k + 1].astype(jnp.int32)).astype(F32) for k in (0, 1)]
    count = dot((hot[0] + hot[1]).astype(BF16), early.astype(BF16))
    hist = jnp.zeros((experts, BINS), F32)
    sides = jnp.where(iota((8, tokens), 0) == 2, prio.astype(F32), valid)
    for k in (0, 1):
        sides = jnp.where(iota((8, tokens), 0) == k, rows[k : k + 1], sides)
    eye = (iota((8, 8), 0) == iota((8, 8), 1)).astype(F32)
    cols = dot(sides, eye, 0, 0)
    prio_col = cols[:, 2:3]
    valid_col = cols[:, 3:4]
    for k in (0, 1):
        slot = jnp.sum(hot[k] * count, axis=0, keepdims=True)
        info_ref[k : k + 1, :] = rows[k : k + 1]
        info_ref[2 + k : 3 + k, :] = rows[k : k + 1] * slots + slot
        hist = hist + dot(hot[k] * valid, class_rows(prio, k, tokens), 1, 1)
        code_row = rows[k : k + 1] * LEVELS + prio.astype(F32)
        code_col = jnp.where(valid_col > 0, cols[:, k : k + 1] * LEVELS + prio_col, -1.0)
        same = (code_col == code_row) & early
        info_ref[4 + k : 5 + k, :] = jnp.sum(same.astype(F32), axis=0, keepdims=True)
    info_ref[6:7, :] = prio.astype(F32)
    info_ref[7:8, :] = valid
    target_ref[...] = jnp.full(target_ref.shape, -1, jnp.int32)
    target_ref[0:2, :] = info_ref[2:4, :].astype(jnp.int32)
    hist_ref[...] = jnp.broadcast_to(hist.astype(jnp.int32)[None], hist_ref.shape)


def slot_hot(target_rows, expert, slots, tokens):
    place = iota((slots, tokens), 0) + expert * slots
    return ((place == target_rows[0:1]) | (place == target_rows[1:2])).astype(F32).astype(BF16)


def spread_kernel(slots, spot_ref, target_ref, rows_ref, *out_refs):
    tokens = target_ref.shape[1]
    for j, out_ref in enumerate(out_refs):
        hot = slot_hot(target_ref[0:2, :], spot_ref[0] ^ j, slots, tokens)
        out_ref[...] = dot(hot, rows_ref[:tokens, :]).astype(BF16)


def spread_joint_kernel(slots, spot_ref, x_ref, g_ref, out_ref, kept_ref):
    expert, tokens = spot_ref[3] + pl.program_id(0), g_ref.shape[0]

    @pl.when(pl.program_id(0) == 0)
    def _():
        codes = x_ref[tokens:, :tokens].astype(F32).astype(jnp.int32)
        kept_ref[...] = jnp.full(kept_ref.shape, -1, jnp.int32)
        for k in (0, 1):
            kept_ref[k : k + 1, :] = codes[2 * k : 2 * k + 1] * 64 + codes[2 * k + 1 : 2 * k + 2] - 1

    hot = slot_hot(kept_ref[0:2, :], expert, slots, tokens)
    out_ref[0, :slots] = dot(hot, x_ref[:tokens, :]).astype(BF16)
    out_ref[0, slots:] = dot(hot, g_ref[...]).astype(BF16)


def hidden_kernel(
    capacity, me_ref, hist_ref, info_ref, target_ref, tok_ref, mix_ref, wo_ref, gm_ref,
    hidden_ref, cross_ref, kept_ref,
):
    devices, experts, bins = hist_ref.shape
    tokens = info_ref.shape[1]
    hidden = tok_ref[...].astype(F32) + dot(mix_ref[...], wo_ref[...])
    hidden_ref[...] = hidden
    unit, _ = norm_parts(hidden)
    cross_ref[:tokens, :] = (unit * gm_ref[...]).astype(BF16)

    def add(j, sums):
        block = hist_ref[j].astype(F32)
        lower = (j < me_ref[0]).astype(F32)
        return sums[0] + block, sums[1] + block * lower

    zero = jnp.zeros((experts, bins), F32)
    totals, before = lax.fori_loop(0, devices, add, (zero, zero))
    early = (iota((bins, bins), 0) < iota((bins, bins), 1)).astype(F32)
    exact = lax.Precision.HIGHEST
    base = dot(totals, early, precision=exact) + before
    prio = info_ref[6:7, :].astype(jnp.int32)
    valid = info_ref[7:8, :] > 0
    kept_ref[...] = jnp.full(kept_ref.shape, -1, jnp.int32)
    codes = jnp.zeros((16, tokens), jnp.int32)
    row = iota((16, tokens), 0)
    for k in (0, 1):
        hot = (iota((experts, tokens), 0) == info_ref[k : k + 1, :].astype(jnp.int32)).astype(F32)
        spot = dot(base, class_rows(prio, k, tokens), precision=exact)
        rank = jnp.sum(hot * spot, axis=0, keepdims=True) + info_ref[4 + k : 5 + k, :]
        kept = valid & (rank < capacity - 0.5)
        place = jnp.where(kept, target_ref[k : k + 1, :], -1)
        kept_ref[k : k + 1, :] = place
        codes = jnp.where(row == 2 * k, (place + 1) >> 6, codes)
        codes = jnp.where(row == 2 * k + 1, (place + 1) & 63, codes)
    cross_ref[tokens:, :] = jnp.zeros((16, cross_ref.shape[1]), BF16)
    cross_ref[tokens:, :tokens] = codes.astype(F32).astype(BF16)


def project_kernel(tok_ref, ga_ref, wqkv_ref, normed_ref, proj_ref):
    unit, _ = norm_parts(tok_ref[...].astype(F32))
    normed = (unit * ga_ref[...]).astype(BF16)
    normed_ref[...] = normed
    features = tok_ref.shape[1]
    for part in range(3):
        at = slice(part * features, (part + 1) * features)
        proj_ref[:, at] = dot(normed, wqkv_ref[:, at]).astype(BF16)


def attend_kernel(query_ref, keys_ref, value_ref, seg_ref, pad_ref, mix_ref, prob_ref, bias_ref):
    step = pl.program_id(0)
    tokens = query_ref.shape[0]

    @pl.when(step == 0)
    def _():
        seg = seg_ref[...].astype(F32)
        eye = (iota((8, 8), 0) == iota((8, 8), 1)).astype(F32)
        seg_col = dot(jnp.broadcast_to(seg, (8, tokens)), eye, 0, 0)[:, 0:1]
        own = iota((tokens, tokens), 0) == iota((tokens, tokens), 1)
        allowed = (seg_col == seg) & ((pad_ref[...] > 0) | own)
        bias_ref[...] = jnp.where(allowed, 0.0, -1e30)

    query, keys, value = query_ref[...], keys_ref[...], value_ref[...]
    first = iota((tokens, 128), 1) < HEAD_DIM
    mixed = []
    for h in (0, 1):
        mine = first if h == 0 else ~first
        own_query = jnp.where(mine, query.astype(F32) * HEAD_DIM ** (-0.5), 0.0).astype(BF16)
        scores = dot(own_query, keys, 1, 1) + bias_ref[...]
        top = jnp.max(scores, axis=-1, keepdims=True)
        exponent = jnp.exp(scores - top)
        total = jnp.sum(exponent, axis=-1, keepdims=True)
        prob = (exponent * (1.0 / total)).astype(BF16)
        prob_ref[h] = prob
        mixed.append(dot(prob, value))
    mix_ref[...] = jnp.where(first, mixed[0], mixed[1]).astype(BF16)


def gather_rows(spot_ref, kept_ref, rows_refs):
    slots, features = rows_refs[0].shape
    tokens = kept_ref.shape[1]
    total = jnp.zeros((tokens, features), F32)
    for j, rows_ref in enumerate(rows_refs):
        hot = slot_hot(kept_ref[0:2, :], spot_ref[0] ^ j, slots, tokens)
        total = total + dot(hot, rows_ref[...], 0, 0)
    return total


def near_kernel(spot_ref, kept_ref, hidden_ref, *refs):
    d_ref, block_ref = refs[-2:]
    slots, tokens = refs[0].shape[0] // 2, kept_ref.shape[1]
    d_total = jnp.zeros(d_ref.shape, F32)
    y_total = hidden_ref[...]
    for j, rows_ref in enumerate(refs[:-2]):
        hot = slot_hot(kept_ref[0:2, :], spot_ref[0] ^ j, slots, tokens)
        d_total = d_total + dot(hot, rows_ref[:slots, :], 0, 0)
        y_total = y_total + dot(hot, rows_ref[slots:, :], 0, 0)
    d_ref[...] = d_total
    block_ref[...] = y_total


def gather_pass_kernel(group, spot_ref, kept_ref, *refs):
    refs[2 * group][...] = gather_rows(spot_ref, kept_ref, refs[:group]).astype(BF16)


def gather_kernel(spot_ref, kept_ref, *refs):
    refs[-1][...] = gather_rows(spot_ref, kept_ref, refs[:-1]).astype(BF16)


def block_kernel(block_ref, far_ref, out_ref):
    out_ref[...] = (block_ref[...] + far_ref[...].astype(F32)).astype(BF16)


def weight_grad_kernel(rows_ref, grad_ref, *refs):
    refs[-1][0] = dot(rows_ref[...], grad_ref[...], 0, 0).astype(BF16)


def widen_kernel(both_ref, in_ref, out_ref):
    in_ref[...] = both_ref[0].astype(F32).T
    out_ref[...] = both_ref[1].astype(F32)


def halves_by(bit, value):
    rows = value.shape[0] // 2
    low, high = value[:rows], value[rows:]
    return jnp.where(bit > 0, high, low), jnp.where(bit > 0, low, high)


def as_column(row, column):
    at = (iota((8, 128), 1) == column) & (iota((8, 128), 0) == 0)
    return dot(jnp.broadcast_to(row, (8, row.shape[1])), at.astype(F32), 0, 0, lax.Precision.HIGHEST)


def hidden_back_kernel(
    spot_ref, near_ref, far_ref, hidden_ref, cot_ref, gm_ref, wo_ref, mix_ref, gwra_ref, gwrb_ref, _,
    dhid_ref, dmix_ref, keep_ref, give_ref, __,
):
    features = hidden_ref.shape[1]
    bit = spot_ref[1]
    grad = near_ref[...] + far_ref[...].astype(F32)
    unit, scale = norm_parts(hidden_ref[...])
    gain = jnp.sum(grad * unit, axis=0, keepdims=True)
    dhid = cot_ref[...].astype(F32) + norm_back(unit, scale, grad * gm_ref[...])
    dhid_ref[...] = dhid
    branch = dhid.astype(BF16)
    keep, give = halves_by(bit, dot(mix_ref[...], branch, 0, 0))
    keep_ref[:, :features], give_ref[:, :features] = keep.astype(BF16), give.astype(BF16)
    dmix_ref[...] = dot(branch, wo_ref[...], 1, 1).astype(BF16)
    experts = gwra_ref.shape[1]
    wide = (iota((experts, 128), 0) == iota((experts, 128), 1)).astype(F32)
    side = dot(gwra_ref[...] + gwrb_ref[...], wide, precision=lax.Precision.HIGHEST)
    side = side + as_column(gain, experts)
    keep, give = halves_by(bit, side)
    keep_ref[:, features:], give_ref[:, features:] = keep.astype(BF16), give.astype(BF16)


def head_pair_back(offset, dmix_ref, proj_ref, mix_ref, prob_ref, dproj_ref):
    step = pl.program_id(0)
    tokens, features = mix_ref.shape
    width = dproj_ref.shape[1] // 3
    at = lambda part: pl.ds(pl.multiple_of(part * features + (step + offset) * 128, 128), 128)
    query, keys, value = proj_ref[:, at(0)], proj_ref[:, at(1)], proj_ref[:, at(2)]
    dmix = dmix_ref[:, at(0)]
    product = dmix.astype(F32) * mix_ref[:, at(0)].astype(F32)
    first = iota((tokens, 128), 1) < HEAD_DIM
    parts = []
    for h in (0, 1):
        mine = first if h == 0 else ~first
        own_dmix = jnp.where(mine, dmix.astype(F32), 0.0).astype(BF16)
        delta = jnp.sum(jnp.where(mine, product, 0.0), axis=-1, keepdims=True)
        prob = prob_ref[h]
        dprob = dot(own_dmix, value, 1, 1)
        dscore = (prob.astype(F32) * (dprob - delta) * HEAD_DIM ** (-0.5)).astype(BF16)
        parts.append((dot(dscore, keys), dot(dscore, query, 0, 0), dot(prob, dmix, 0, 0)))
    for part in range(3):
        to = pl.ds(pl.multiple_of(part * width + step * 128, 128), 128)
        dproj_ref[:, to] = jnp.where(first, parts[0][part], parts[1][part]).astype(BF16)


def first_heads_kernel(
    spot_ref, dmix_ref, normed_ref, proj_ref, mix_ref, prob_ref, keep_ref, give_ref, dproj_ref,
):
    head_pair_back(0, dmix_ref, proj_ref, mix_ref, prob_ref, dproj_ref)

    @pl.when(pl.program_id(0) == pl.num_programs(0) - 1)
    def _():
        keep, give = halves_by(spot_ref[1], dot(normed_ref[...], dproj_ref[...], 0, 0))
        keep_ref[...], give_ref[...] = keep.astype(BF16), give.astype(BF16)


def last_heads_kernel(
    spot_ref, dmix_ref, normed_ref, proj_ref, mix_ref, prob_ref, keep_ref, give_ref, dproj_ref,
):
    head_pair_back(pl.num_programs(0), dmix_ref, proj_ref, mix_ref, prob_ref, dproj_ref)

    @pl.when(pl.program_id(0) == pl.num_programs(0) - 1)
    def _():
        keep, give = halves_by(spot_ref[1], dot(normed_ref[...], dproj_ref[...], 0, 0))
        keep_ref[...], give_ref[...] = keep.astype(BF16), give.astype(BF16)


def token_grad_kernel(first_ref, last_ref, dhid_ref, tok_ref, ga_ref, wqkv_ref, gtok_ref):
    tokens, features = tok_ref.shape
    grad = jnp.zeros((tokens, features), F32)
    half = features // 2
    for part in range(3):
        at = slice(part * half, (part + 1) * half)
        for place, ref in ((0, first_ref), (1, last_ref)):
            start = part * features + place * half
            grad = grad + dot(ref[:, at], wqkv_ref[:, start : start + half], 1, 1)
    unit, scale = norm_parts(tok_ref[...].astype(F32))
    gtok_ref[...] = dhid_ref[...] + norm_back(unit, scale, grad * ga_ref[...])


def take(refs, count):
    return refs[:count], refs[count:]


def expert_kernel(pieces, group, near, *refs):
    step = pl.program_id(0)
    (spot_ref, wr_ref, own_ref, win_ref, wout_ref), refs = take(refs, 5)
    mine = (spot_ref[0] - spot_ref[3]) ^ step
    if near:
        x_refs, refs = take(refs, group)
        g_refs, refs = take(refs, group)
        back_refs, refs = take(refs, group)
    else:
        (far_ref,), refs = take(refs, 1)
        refs = refs[4:]
        dx_refs, refs = take(refs, group)
        y_refs, refs = take(refs, group)
    gwr_ref, dexp_ref, xcopy_ref, act_ref, dpre_ref, now_ref = refs
    slots = dexp_ref.shape[0]
    if near:
        for j in range(group):

            @pl.when(step == j)
            def _():
                xcopy_ref[...] = x_refs[j][...]
                now_ref[...] = g_refs[j][...]

    else:
        xcopy_ref[...] = far_ref[mine, :slots, :]
        now_ref[...] = far_ref[mine, slots:, :]

    x = xcopy_ref[...]
    g = now_ref[...].astype(F32)
    logits = dot(x, wr_ref[...])
    exponent = jnp.exp(logits - jnp.max(logits, axis=-1, keepdims=True))
    router = exponent / jnp.sum(exponent, axis=-1, keepdims=True)
    gate = jnp.sum(router * own_ref[...], axis=-1, keepdims=True)
    dexp = (gate * g).astype(BF16)
    dexp_ref[...] = dexp
    out = jnp.zeros(x.shape, F32)
    dx = jnp.zeros(x.shape, F32)
    width = win_ref.shape[1] // pieces
    for r in range(pieces):
        at = slice(r * width, (r + 1) * width)
        pre = dot(x, win_ref[:, at])
        square = pre * pre
        bend = jnp.tanh(pre * (0.7978845608028654 + 0.035677408136300125 * square))
        half = 0.5 + 0.5 * bend
        smooth = pre * half
        slope = half + smooth * (1.0 - half) * (1.5957691216057308 + 0.21406444881780075 * square)
        active = smooth.astype(BF16)
        act_ref[:, at] = active
        dpreact = (dot(dexp, wout_ref[at, :], 1, 1) * slope).astype(BF16)
        dpre_ref[:, at] = dpreact
        out = out + dot(active, wout_ref[at, :])
        dx = dx + dot(dpreact, win_ref[:, at], 1, 1)
    out = out.astype(BF16).astype(F32)
    y = (gate * out).astype(BF16)
    dgate = jnp.sum(g * out, axis=-1, keepdims=True)
    dlogits = (dgate * gate * (own_ref[...] - router)).astype(BF16)
    dx = (dx + dot(dlogits, wr_ref[...], 1, 1)).astype(BF16)
    if near:
        for j in range(group):

            @pl.when(step == j)
            def _():
                back_refs[j][:slots, :] = dx
                back_refs[j][slots:, :] = y

    else:
        for j in range(group):

            @pl.when(step == j)
            def _():
                y_refs[j][...] = y
                dx_refs[j][...] = dx

    @pl.when(step == 0)
    def _():
        gwr_ref[...] = jnp.zeros(gwr_ref.shape, F32)

    gwr_ref[...] += dot(x, dlogits, 0, 0)


def swap(value, axis, bit):
    size = lax.axis_size(axis)
    return lax.ppermute(value, axis, [(i, i ^ bit) for i in range(size)])


def bits_of(axis):
    size = lax.axis_size(axis)
    return [1 << b for b in range(size.bit_length() - 1)]


def deal_plane_kernel(spot_ref, *refs):
    in_refs, (own_ref, *out_refs, total_ref) = refs[:-5], refs[-5:]
    start = 0
    for keep_ref, other_ref in zip(in_refs[::2], in_refs[1::2]):
        total = keep_ref[...].astype(F32) + other_ref[...].astype(F32)
        rows, columns = total.shape
        total_ref[:, :, start : start + columns] = total.reshape(4, rows // 4, columns)
        start += columns
    spot = spot_ref[2] * 2 + spot_ref[4]
    own_ref[...] = total_ref[spot]
    for j, out_ref in enumerate(out_refs):
        out_ref[...] = total_ref[spot ^ (j + 1)].astype(BF16)


def deal_line_kernel(groups, spot_ref, own_ref, *refs):
    in_refs, (first_ref, *out_refs, total_ref) = refs[:3], refs[3:]
    total = own_ref[...]
    for ref in in_refs:
        total = total + ref[...].astype(F32)
    rows, columns = total.shape
    total_ref[...] = total.reshape(groups, rows // groups, columns)
    first_ref[...] = total_ref[spot_ref[5]]
    for j, out_ref in enumerate(out_refs):
        out_ref[...] = total_ref[spot_ref[5] ^ (j + 1)].astype(BF16)


def pile_kernel(own_ref, *refs):
    total = own_ref[...]
    for ref in refs[:-1]:
        total = total + ref[...].astype(F32)
    refs[-1][...] = total.astype(BF16)


def line_up_kernel(spot_ref, *refs):
    out_ref, total_ref = refs[-2:]
    for j, ref in enumerate(refs[:-2]):
        total_ref[spot_ref[5] ^ j] = ref[...].astype(F32)
    out_ref[...] = total_ref[...].reshape(out_ref.shape).astype(BF16)


def line_up_plane_kernel(spot_ref, *refs):
    out_ref, total_ref = refs[-2:]
    for j, ref in enumerate(refs[:-2]):
        total_ref[(spot_ref[2] * 2 + spot_ref[4]) ^ j] = ref[...]
    out_ref[...] = total_ref[...].reshape(out_ref.shape)


def finish_kernel(orders, experts, spot_ref, wqkv_ref, ga_ref, *refs):
    piece_refs, refs = take(refs, 2 * len(orders))
    grad_o_ref, grad_qkv_ref, gain_attn_ref, gain_moe_ref, router_ref, side_o_ref = refs
    out_refs = grad_o_ref, side_o_ref, grad_qkv_ref
    for place, targets in enumerate(orders):
        for k in range(2):
            ref = piece_refs[2 * place + k]
            rows = ref.shape[0]
            at = pl.ds(pl.multiple_of((spot_ref[1] ^ k) * rows, 8), rows)
            for start, width, out, column in targets:
                out_refs[out][at, column : column + width] = ref[:, start : start + width].astype(F32)
    side_o = side_o_ref[...].T
    router_ref[...] = side_o[:experts, :]
    gain_moe_ref[...] = side_o[experts : experts + 1, :]
    gain_attn_ref[...] = gain_back(wqkv_ref, grad_qkv_ref, ga_ref)


def gain_back(wqkv_ref, grad_qkv_ref, ga_ref):
    features = wqkv_ref.shape[0]
    total = jnp.zeros((features, 1), F32)
    for part in range(3):
        at = slice(part * features, (part + 1) * features)
        total = total + jnp.sum(wqkv_ref[:, at].astype(F32) * grad_qkv_ref[:, at], axis=-1, keepdims=True)
    return jnp.broadcast_to(total, (features, 128)).T[0:1, :] / ga_ref[...]


def plane_swap(value, j):
    groups = lax.axis_size("expert")
    size = lax.axis_size("dp") * groups
    apart = (j >> 1) * 2 * groups + (j & 1)
    return lax.ppermute(value, ("dp", "expert"), [(i, i ^ apart) for i in range(size)])


def plane_deal(spot, halves, *after):
    scalar = pl.BlockSpec(memory_space=pltpu.SMEM)
    ins = [v for pair in halves for v in pair]
    rows, columns = halves[0][0].shape[0] // 4, sum(pair[0].shape[1] for pair in halves)
    piece = (rows, columns)
    return call(
        deal_plane_kernel, (1,), (spot, *ins), [scalar] + [whole(v.shape) for v in ins],
        [shape_of(piece, F32)] + [shape_of(piece, BF16)] * 3, [whole_out(piece)] * 4,
        [pltpu.VMEM((4, *piece), F32)],
        after=after,
    )


def line_deal(spot, dealt, groups, us, *after):
    scalar = pl.BlockSpec(memory_space=pltpu.SMEM)
    own, *out = dealt
    rows, columns = own.shape
    piece = (rows // groups, columns)
    arrived = [plane_swap(v, j + 1) for j, v in enumerate(out)]
    scratch = [pltpu.VMEM((groups, *piece), F32)]
    own, *out = call(
        functools.partial(deal_line_kernel, groups), (1,), (spot, own, *arrived),
        [scalar] + [whole((rows, columns))] * 4,
        (shape_of(piece, F32), *[shape_of(piece, BF16)] * (groups - 1)),
        (whole_out(piece),) * groups,
        scratch,
        us=us,
        after=after,
    )
    return [own] + [swap(v, "expert", 2 * (j + 1)) for j, v in enumerate(out)]


def line_up(spot, parts, *late_pile):
    scalar = pl.BlockSpec(memory_space=pltpu.SMEM)
    groups, piece = len(parts), parts[0].shape
    rows, columns = groups * piece[0], piece[1]
    scratch = [pltpu.VMEM((groups, *piece), F32)]
    total = call(
        pile_kernel, (1,), parts, [whole(piece)] * groups, shape_of(piece, BF16), whole_out(piece),
        after=late_pile,
    )
    own = call(
        line_up_kernel, (1,), (spot, total, *[swap(total, "expert", 2 * j) for j in range(1, groups)]),
        [scalar] + [whole(piece)] * groups,
        shape_of((rows, columns), BF16), whole_out((rows, columns)), scratch,
    )
    return own, [plane_swap(own, j) for j in (1, 2, 3)]


def line_up_plane(spot, own, arrived, *after):
    scalar = pl.BlockSpec(memory_space=pltpu.SMEM)
    rows, columns = own.shape
    half = (4 * rows, columns)
    own = call(
        line_up_plane_kernel, (1,), (spot, own, *arrived),
        [scalar] + [whole((rows, columns))] * 4,
        shape_of(half, BF16), whole_out(half), [pltpu.VMEM((4, rows, columns), BF16)],
        after=after,
    )
    return [own, swap(own, "dp", 1)]


def all_sum(value, steps):
    rows = value.shape[0]
    place = []
    for axis, bit in steps:
        half = value.shape[0] // 2
        mine = ((lax.axis_index(axis) & bit) > 0).astype(jnp.int32)
        keep = lax.dynamic_slice_in_dim(value, mine * half, half, 0)
        give = lax.dynamic_slice_in_dim(value, (1 - mine) * half, half, 0)
        value = (keep.astype(F32) + swap(give, axis, bit).astype(F32)).astype(BF16)
        place.append(mine)
    for (axis, bit), mine in zip(reversed(steps), reversed(place)):
        other = swap(value, axis, bit)
        low = jnp.where(mine > 0, other, value)
        high = jnp.where(mine > 0, value, other)
        value = jnp.concatenate([low, high], axis=0)
    return value


def local(
    tokens, segment_ids, pad_mask, routes, priority, gain_attn, w_qkv, w_o, gain_moe, w_router,
    w_in, w_out, cotangent,
):
    sequences, length, features = tokens.shape
    count = sequences * length
    experts = w_router.shape[1]
    groups = lax.axis_size("expert")
    replicas = lax.axis_size("dp")
    devices = groups * replicas
    group = groups // 2
    most = 4 * count // experts
    slots = -(-most // 16) * 16
    capacity = (42 * count * devices + 20 * experts - 1) // (20 * experts)
    me = lax.axis_index(("dp", "expert")).astype(jnp.int32).reshape(1)
    replica = lax.axis_index("dp")
    column = lax.axis_index("expert")
    spot = jnp.stack(
        [column, replica & 1, replica >> 1 & 1, column // group * group, column & 1, column >> 1]
    ).astype(jnp.int32)
    tok = tokens.reshape(count, features)
    cot = cotangent.reshape(count, features)
    ga = gain_attn.reshape(1, features)
    gm = gain_moe.reshape(1, features)
    full = (count, features)
    scalar = pl.BlockSpec(memory_space=pltpu.SMEM)
    sent = shape_of((slots, features), BF16)

    def across(value):
        return swap(value, "expert", group)

    def among(values):
        return [v if j == 0 else swap(v, "expert", j) for j, v in enumerate(values)]

    halves = [list(range(group)), list(range(group, groups))]
    joint = (group, 2 * slots, features)

    def half_exchange(value):
        return lax.all_to_all(value, "expert", 0, 0, axis_index_groups=halves, tiled=True)

    far_cot = across(cot)
    full_in = lax.all_gather(w_in[0], "dp", axis=1, tiled=True)
    full_out = lax.all_gather(w_out[0], "dp", axis=0, tiled=True)

    pairs = features // 128
    tile = lambda dtype: shape_of((count, features), dtype)
    prob_block = pl.BlockSpec((2, count, count), lambda i: (i, 0, 0))
    hist_shape = (devices, experts, BINS)
    hist, info, target = call(
        functools.partial(route_kernel, slots, experts),
        (1,),
        (routes.reshape(count, 2).T, priority.reshape(1, count), pad_mask.reshape(1, count)),
        [whole((2, count)), whole((1, count)), whole((1, count))],
        (shape_of(hist_shape, jnp.int32), shape_of((8, count), F32), shape_of((8, count), jnp.int32)),
        (whole_out(hist_shape), whole_out((8, count)), whole_out((8, count))),
    )
    def spread(target, rows, us, *after):
        return call(
            functools.partial(spread_kernel, slots),
            (1,),
            (spot, target, rows),
            [scalar, whole((8, count)), whole(rows.shape)],
            [sent] * group,
            [whole_out((slots, features))] * group,
            us=us,
            after=after,
        )

    near_g_sent = spread(target, cot, 1)
    near_g = among(near_g_sent)
    every = lax.all_to_all(hist, ("dp", "expert"), 0, 0, tiled=True)
    normed, proj = call(
        project_kernel,
        (1,),
        (tok, ga, w_qkv),
        [whole(full), whole((1, features)), whole(w_qkv.shape)],
        (tile(BF16), shape_of((count, 3 * features), BF16)),
        (whole_out(full), whole_out((count, 3 * features))),
        after=(near_g_sent[0],),
    )
    lanes = lambda part: pl.BlockSpec((count, 128), lambda i: (0, part * pairs + i))
    mix, prob = call(
        attend_kernel,
        (pairs,),
        (proj, proj, proj, segment_ids.reshape(1, count), pad_mask.reshape(1, count)),
        [lanes(0), lanes(1), lanes(2), whole((1, count)), whole((1, count))],
        (tile(BF16), shape_of((HEADS, count, count), BF16)),
        (lanes(0), prob_block),
        [pltpu.VMEM((count, count), F32)],
        us=20000,
        after=(target,),
    )
    cross_shape = (count + 16, features)
    hidden, cross, kept = call(
        functools.partial(hidden_kernel, capacity),
        (1,),
        (me, every, info, target, tok, mix, w_o, gm),
        [scalar, whole(hist_shape), whole((8, count)), whole((8, count)), whole(full), whole(full), whole(w_o.shape), whole((1, features))],
        (tile(F32), shape_of(cross_shape, BF16), shape_of((8, count), jnp.int32)),
        (whole_out(full), whole_out(cross_shape), whole_out((8, count))),
    )
    far_x = across(cross)
    near_sent = spread(kept, cross, 20000, *near_g)
    near_x = among(near_sent)
    far_sent, far_kept = call(
        functools.partial(spread_joint_kernel, slots),
        (group,),
        (spot, far_x, far_cot),
        [scalar, whole(cross_shape), whole(full)],
        (shape_of(joint, BF16), shape_of((8, count), jnp.int32)),
        (pl.BlockSpec((1, 2 * slots, features), lambda e: (e, 0, 0)), whole_out((8, count))),
        after=(near_sent[0],),
    )
    far_rows = half_exchange(far_sent)

    hidden_units = w_out.shape[1] * replicas
    own = (iota((1, experts), 1) == column).astype(F32)
    flat = group * slots
    slot_spec = whole_out((slots, features))
    weights = (spot, w_router, own, full_in, full_out)
    weight_specs = [scalar, whole(w_router.shape), whole((1, experts)), whole(full_in.shape), whole(full_out.shape)]
    tall = [shape_of((2 * flat, n), BF16) for n in (features, features, hidden_units, hidden_units)]
    tall_blocks = lambda first: [
        pl.BlockSpec((slots, v.shape[1]), lambda e: (first + e, 0)) for v in tall
    ]
    outs = call(
        functools.partial(expert_kernel, 4, group, True),
        (group,),
        (*weights, *near_x, *near_g),
        weight_specs + [whole((slots, features))] * (2 * group),
        (*[shape_of((2 * slots, features), BF16)] * group, shape_of(w_router.shape, F32), *tall),
        (*[whole_out((2 * slots, features))] * group, whole_out(w_router.shape), *tall_blocks(0)),
        [pltpu.VMEM((slots, features), BF16)],
        us=300000,
        after=(far_sent,),
    )
    near_back, outs = take(outs, group)
    near_back = among(near_back)
    gwr_a, kept_rows = outs[0], outs[1:]
    outs = call(
        functools.partial(expert_kernel, 4, group, False),
        (group,),
        (*weights, far_rows, *kept_rows),
        weight_specs + [whole(joint)] + [pl.BlockSpec(memory_space=pl.ANY)] * 4,
        (*[sent] * (2 * group), shape_of(w_router.shape, F32), *tall),
        (*[slot_spec] * (2 * group), whole_out(w_router.shape), *tall_blocks(group)),
        [pltpu.VMEM((slots, features), BF16)],
        after=(gwr_a,),
        alias=[(6 + i, 2 * group + 1 + i) for i in range(4)],
    )
    d_far, outs = take(outs, group)
    y_far, outs = take(outs, group)
    gwr_b, all_dexp, all_x, all_act, all_dpre = outs
    d_far = among(d_far)
    def gather(rows, *after):
        return call(
            gather_kernel,
            (1,),
            (spot, far_kept, *rows),
            [scalar, whole((8, count))] + [whole((slots, features))] * group,
            tile(BF16),
            whole_out(full),
            after=after,
        )

    anywhere = pl.BlockSpec(memory_space=pl.ANY)
    part = hidden_units // 4
    both_shape = shape_of((2, hidden_units, features), BF16)

    def weight_grad(which, rows, grad, us, after, *given):
        return call(
            weight_grad_kernel,
            (4,),
            (rows, grad, *given),
            [pl.BlockSpec((2 * flat, part), lambda i: (0, i)), whole((2 * flat, features))] + [anywhere] * len(given),
            both_shape,
            pl.BlockSpec((1, part, features), lambda i: (which, i, 0)),
            us=us,
            after=after,
            alias=[(2, 0)] if given else (),
        )

    both = weight_grad(1, all_act, all_dexp, 1, near_back)
    d_far, *y_far = call(
        functools.partial(gather_pass_kernel, group),
        (1,),
        (spot, far_kept, *d_far, *y_far),
        [scalar, whole((8, count))] + [whole((slots, features))] * group + [anywhere] * group,
        [tile(BF16)] + [sent] * group,
        [whole_out(full)] + [anywhere] * group,
        after=(both,),
        alias=[(2 + group + j, 1 + j) for j in range(group)],
    )
    y_far = among(y_far)
    both = weight_grad(0, all_dpre, all_x, 60000, (d_far,), both)
    near_d, block_part = call(
        near_kernel,
        (1,),
        (spot, kept, hidden, *near_back),
        [scalar, whole((8, count)), whole(full)] + [whole((2 * slots, features))] * group,
        (tile(F32), tile(F32)),
        (whole_out(full), whole_out(full)),
        after=(both,),
    )

    y_far = gather(y_far, near_d)
    d_far = across(d_far)
    both = lax.psum_scatter(both, "dp", scatter_dimension=1, tiled=True)

    o_half = (features // 2, features + 128)
    a_half = (features // 2, 3 * features // 2)
    dhid, dmix, keep_o, give_o, y_far = call(
        hidden_back_kernel,
        (1,),
        (spot, near_d, d_far, hidden, cot, gm, w_o, mix, gwr_a, gwr_b, y_far),
        [scalar] + [whole(full)] * 4 + [whole((1, features)), whole(w_o.shape), whole(full)] + [whole(gwr_a.shape)] * 2 + [anywhere],
        (tile(F32), tile(BF16), *[shape_of(o_half, BF16)] * 2, tile(BF16)),
        (whole_out(full), whole_out(full), *[whole_out(o_half)] * 2, anywhere),
        us=400000,
        alias=[(10, 4)],
    )
    y_far = across(y_far)
    some = 3 * features // 2
    head_specs = lambda offset: [scalar] + [whole(full)] * 2 + [whole((count, 3 * features)), whole(full)] + [
        pl.BlockSpec((2, count, count), lambda i: (i + offset, 0, 0))
    ]
    keep_a, give_a, dproj_a = call(
        first_heads_kernel,
        (pairs // 2,),
        (spot, dmix, normed, proj, mix, prob),
        head_specs(0),
        (shape_of(a_half, BF16), shape_of(a_half, BF16), shape_of((count, some), BF16)),
        (whole_out(a_half), whole_out(a_half), whole_out((count, some))),
        us=13000,
    )
    by_hand = replicas == 4 and groups == 8 and features % (8 * devices) == 0
    if by_hand:
        beside = lambda keep, give: (keep, swap(give, "dp", 1))
        early = plane_deal(spot, [beside(keep_o, give_o), beside(keep_a, give_a)])
    keep_b, give_b, dproj_b = call(
        last_heads_kernel,
        (pairs // 2,),
        (spot, dmix, normed, proj, mix, prob),
        head_specs(pairs // 2),
        (shape_of(a_half, BF16), shape_of(a_half, BF16), shape_of((count, some), BF16)),
        (whole_out(a_half), whole_out(a_half), whole_out((count, some))),
        us=4000,
        after=early[:1] if by_hand else (),
    )
    gtok = call(
        token_grad_kernel,
        (1,),
        (dproj_a, dproj_b, dhid, tok, ga, w_qkv),
        [whole((count, some))] * 2 + [whole(full)] * 2 + [whole((1, features)), whole(w_qkv.shape)],
        tile(F32),
        whole_out(full),
    )
    block_out = call(
        block_kernel,
        (1,),
        (block_part, y_far),
        [whole(full)] * 2,
        tile(BF16),
        whole_out(full),
        after=(gtok,),
    )
    shapes = [w_in.shape[1:], w_out.shape[1:]]
    gin, gout = call(
        widen_kernel,
        (1,),
        (both,),
        [whole(both.shape)],
        [shape_of(v, F32) for v in shapes],
        [whole_out(v) for v in shapes],
        after=(gtok,),
    )
    if by_hand:
        rows = groups // 2
        early = line_deal(spot, early, rows, 30000, gtok)
        late = plane_deal(spot, [beside(keep_b, give_b)], early[0])
        early, early_parts = line_up(spot, early, late[0], y_far)
        late, late_parts = line_up(spot, line_deal(spot, late, rows, 1, early))
        pieces = line_up_plane(spot, early, early_parts, late) + line_up_plane(
            spot, late, late_parts, gin, block_out
        )
        half = features // 2
        heads = lambda start, place: tuple(
            (start + part * half, half, 2, part * features + place * half) for part in range(3)
        )
        orders = (
            ((0, features, 0, 0), (features, 128, 1, 0)) + heads(features + 128, 0),
            heads(0, 1),
        )
        shapes = [(features, features), (features, 3 * features), (1, features), (1, features), (experts, features)]
        grad_o, grad_qkv, gain_attn_grad, gain_moe_grad, grad_router = call(
            functools.partial(finish_kernel, orders, experts),
            (1,),
            (spot, w_qkv, ga, *pieces),
            [scalar, whole(w_qkv.shape), whole((1, features))] + [whole(v.shape) for v in pieces],
            [shape_of(v, F32) for v in shapes],
            [whole_out(v) for v in shapes],
            [pltpu.VMEM((features, 128), F32)],
        )
    else:
        low = (replica & 1) == 0

        def rejoin(keep, give):
            return jnp.concatenate([jnp.where(low, keep, give), jnp.where(low, give, keep)], axis=0)

        gain_steps = [("dp", b) for b in bits_of("dp")] + [("expert", b) for b in bits_of("expert")]
        both = all_sum(rejoin(keep_o, give_o), gain_steps).astype(F32)
        grad_o, side_o = both[:, :features], both[:, features:]
        first = all_sum(rejoin(keep_a, give_a), gain_steps).astype(F32)
        last = all_sum(rejoin(keep_b, give_b), gain_steps).astype(F32)
        half = features // 2
        cut = lambda part: slice(part * half, (part + 1) * half)
        grad_qkv = jnp.concatenate([v[:, cut(part)] for part in range(3) for v in (first, last)], axis=1)
        product = jnp.sum(w_qkv.astype(F32) * grad_qkv, axis=1)
        gain_attn_grad, gain_moe_grad = product / gain_attn, side_o[:, experts]
        grad_router = side_o[:, :experts].T
    return (
        block_out.reshape(sequences, length, features),
        gtok.reshape(sequences, length, features),
        gain_attn_grad.reshape(features),
        grad_qkv,
        grad_o,
        gain_moe_grad.reshape(features),
        grad_router.T,
        gin[None],
        gout[None],
    )


def solution(mesh):
    rows = P(("dp", "expert"), None, None)
    flat = P(("dp", "expert"), None)
    first = P("expert", None, "dp")
    second = P("expert", "dp", None)
    return jax.shard_map(
        local,
        mesh=mesh,
        in_specs=(rows, flat, flat, rows, flat, P(), P(), P(), P(), P(), first, second, rows),
        out_specs=(rows, rows, P(), P(), P(), P(), P(), first, second),
        check_vma=False,
    )
```

```python
import functools

import jax
import jax.numpy as jnp
from jax import lax
from jax.experimental import pallas as pl
from jax.experimental.pallas import tpu as pltpu
from jax.sharding import PartitionSpec as P

HEADS = 12
HEAD_DIM = 64
LEVELS = 64
BINS = 2 * LEVELS
LIMIT = 60 * 1024 * 1024
LATE = 44 * 1024 * 1024
F32 = jnp.float32
BF16 = jnp.bfloat16


def dot(a, b, ca=1, cb=0, precision=None):
    return lax.dot_general(
        a, b, (((ca,), (cb,)), ((), ())), precision=precision, preferred_element_type=F32
    )


def whole(shape):
    zeros = (0,) * len(shape)
    return pl.BlockSpec(shape, lambda *_: zeros, pipeline_mode=pl.Buffered(1))


def whole_out(shape):
    zeros = (0,) * len(shape)
    return pl.BlockSpec(shape, lambda *_: zeros)


def iota(shape, dim):
    return lax.broadcasted_iota(jnp.int32, shape, dim)


def call(kernel, grid, ins, in_specs, outs, out_specs, scratch=(), us=1, after=(), alias=(), limit=None):
    late = len(after)

    def body(*refs):
        kernel(*refs[late:])

    return pl.pallas_call(
        body,
        grid=grid,
        in_specs=[pl.BlockSpec(memory_space=pl.ANY)] * late + in_specs,
        out_specs=out_specs,
        out_shape=outs,
        scratch_shapes=list(scratch),
        input_output_aliases={late + i: o for i, o in alias},
        compiler_params=pltpu.CompilerParams(vmem_limit_bytes=limit or LATE),
        cost_estimate=pl.CostEstimate(flops=us * 10**6, bytes_accessed=0, transcendentals=0),
    )(*after, *ins)


def shape_of(shape, dtype):
    return jax.ShapeDtypeStruct(shape, dtype)


def norm_parts(values):
    center = values - jnp.mean(values, axis=-1, keepdims=True)
    spread = jnp.mean(center * center, axis=-1, keepdims=True)
    scale = lax.rsqrt(spread + 1e-06)
    return center * scale, scale


def norm_back(unit, scale, grad_unit):
    return scale * (
        grad_unit
        - jnp.mean(grad_unit, axis=-1, keepdims=True)
        - unit * jnp.mean(grad_unit * unit, axis=-1, keepdims=True)
    )


def class_rows(level_row, which, tokens):
    return (iota((BINS, tokens), 0) == which * LEVELS + (LEVELS - 1) - level_row).astype(F32)


def route_kernel(slots, experts, routes_ref, prio_ref, pad_ref, hist_ref, info_ref, target_ref):
    tokens = routes_ref.shape[1]
    rows = routes_ref[...].astype(F32)
    prio = prio_ref[...]
    valid = (pad_ref[...] > 0).astype(F32)
    early = iota((tokens, tokens), 0) < iota((tokens, tokens), 1)
    hot = [(iota((experts, tokens), 0) == rows[k : k + 1].astype(jnp.int32)).astype(F32) for k in (0, 1)]
    count = dot((hot[0] + hot[1]).astype(BF16), early.astype(BF16))
    hist = jnp.zeros((experts, BINS), F32)
    sides = jnp.where(iota((8, tokens), 0) == 2, prio.astype(F32), valid)
    for k in (0, 1):
        sides = jnp.where(iota((8, tokens), 0) == k, rows[k : k + 1], sides)
    eye = (iota((8, 8), 0) == iota((8, 8), 1)).astype(F32)
    cols = dot(sides, eye, 0, 0)
    prio_col = cols[:, 2:3]
    valid_col = cols[:, 3:4]
    for k in (0, 1):
        slot = jnp.sum(hot[k] * count, axis=0, keepdims=True)
        info_ref[k : k + 1, :] = rows[k : k + 1]
        info_ref[2 + k : 3 + k, :] = rows[k : k + 1] * slots + slot
        hist = hist + dot(hot[k] * valid, class_rows(prio, k, tokens), 1, 1)
        code_row = rows[k : k + 1] * LEVELS + prio.astype(F32)
        code_col = jnp.where(valid_col > 0, cols[:, k : k + 1] * LEVELS + prio_col, -1.0)
        same = (code_col == code_row) & early
        info_ref[4 + k : 5 + k, :] = jnp.sum(same.astype(F32), axis=0, keepdims=True)
    info_ref[6:7, :] = prio.astype(F32)
    info_ref[7:8, :] = valid
    target_ref[...] = jnp.full(target_ref.shape, -1, jnp.int32)
    target_ref[0:2, :] = info_ref[2:4, :].astype(jnp.int32)
    hist_ref[...] = jnp.broadcast_to(hist.astype(jnp.int32)[None], hist_ref.shape)


def slot_hot(target_rows, expert, slots, tokens):
    place = iota((slots, tokens), 0) + expert * slots
    return ((place == target_rows[0:1]) | (place == target_rows[1:2])).astype(F32).astype(BF16)


def spread_kernel(slots, spot_ref, target_ref, rows_ref, *out_refs):
    tokens = target_ref.shape[1]
    for j, out_ref in enumerate(out_refs):
        hot = slot_hot(target_ref[0:2, :], spot_ref[0] ^ j, slots, tokens)
        out_ref[...] = dot(hot, rows_ref[:tokens, :]).astype(BF16)


def spread_joint_kernel(slots, spot_ref, x_ref, g_ref, out_ref, kept_ref):
    expert, tokens = spot_ref[3] + pl.program_id(0), g_ref.shape[0]

    @pl.when(pl.program_id(0) == 0)
    def _():
        codes = x_ref[tokens:, :tokens].astype(F32).astype(jnp.int32)
        kept_ref[...] = jnp.full(kept_ref.shape, -1, jnp.int32)
        for k in (0, 1):
            kept_ref[k : k + 1, :] = codes[2 * k : 2 * k + 1] * 64 + codes[2 * k + 1 : 2 * k + 2] - 1

    hot = slot_hot(kept_ref[0:2, :], expert, slots, tokens)
    out_ref[0, :slots] = dot(hot, x_ref[:tokens, :]).astype(BF16)
    out_ref[0, slots:] = dot(hot, g_ref[...]).astype(BF16)


def hidden_kernel(
    capacity, me_ref, hist_ref, info_ref, target_ref, tok_ref, mix_ref, wo_ref, gm_ref,
    hidden_ref, cross_ref, kept_ref,
):
    devices, experts, bins = hist_ref.shape
    tokens = info_ref.shape[1]
    hidden = tok_ref[...].astype(F32) + dot(mix_ref[...], wo_ref[...])
    hidden_ref[...] = hidden
    unit, _ = norm_parts(hidden)
    cross_ref[:tokens, :] = (unit * gm_ref[...]).astype(BF16)

    def add(j, sums):
        block = hist_ref[j].astype(F32)
        lower = (j < me_ref[0]).astype(F32)
        return sums[0] + block, sums[1] + block * lower

    zero = jnp.zeros((experts, bins), F32)
    totals, before = lax.fori_loop(0, devices, add, (zero, zero))
    early = (iota((bins, bins), 0) < iota((bins, bins), 1)).astype(F32)
    exact = lax.Precision.HIGHEST
    base = dot(totals, early, precision=exact) + before
    prio = info_ref[6:7, :].astype(jnp.int32)
    valid = info_ref[7:8, :] > 0
    kept_ref[...] = jnp.full(kept_ref.shape, -1, jnp.int32)
    codes = jnp.zeros((16, tokens), jnp.int32)
    row = iota((16, tokens), 0)
    for k in (0, 1):
        hot = (iota((experts, tokens), 0) == info_ref[k : k + 1, :].astype(jnp.int32)).astype(F32)
        spot = dot(base, class_rows(prio, k, tokens), precision=exact)
        rank = jnp.sum(hot * spot, axis=0, keepdims=True) + info_ref[4 + k : 5 + k, :]
        kept = valid & (rank < capacity - 0.5)
        place = jnp.where(kept, target_ref[k : k + 1, :], -1)
        kept_ref[k : k + 1, :] = place
        codes = jnp.where(row == 2 * k, (place + 1) >> 6, codes)
        codes = jnp.where(row == 2 * k + 1, (place + 1) & 63, codes)
    cross_ref[tokens:, :] = jnp.zeros((16, cross_ref.shape[1]), BF16)
    cross_ref[tokens:, :tokens] = codes.astype(F32).astype(BF16)


def project_kernel(tok_ref, ga_ref, wqkv_ref, normed_ref, proj_ref):
    unit, _ = norm_parts(tok_ref[...].astype(F32))
    normed = (unit * ga_ref[...]).astype(BF16)
    normed_ref[...] = normed
    features = tok_ref.shape[1]
    for part in range(3):
        at = slice(part * features, (part + 1) * features)
        proj_ref[:, at] = dot(normed, wqkv_ref[:, at]).astype(BF16)


def attend_kernel(query_ref, keys_ref, value_ref, seg_ref, pad_ref, mix_ref, prob_ref, bias_ref):
    step = pl.program_id(0)
    tokens = query_ref.shape[0]

    @pl.when(step == 0)
    def _():
        seg = seg_ref[...].astype(F32)
        eye = (iota((8, 8), 0) == iota((8, 8), 1)).astype(F32)
        seg_col = dot(jnp.broadcast_to(seg, (8, tokens)), eye, 0, 0)[:, 0:1]
        own = iota((tokens, tokens), 0) == iota((tokens, tokens), 1)
        allowed = (seg_col == seg) & ((pad_ref[...] > 0) | own)
        bias_ref[...] = jnp.where(allowed, 0.0, -1e30)

    query, keys, value = query_ref[...], keys_ref[...], value_ref[...]
    first = iota((tokens, 128), 1) < HEAD_DIM
    mixed = []
    for h in (0, 1):
        mine = first if h == 0 else ~first
        own_query = jnp.where(mine, query.astype(F32) * HEAD_DIM ** (-0.5), 0.0).astype(BF16)
        scores = dot(own_query, keys, 1, 1) + bias_ref[...]
        top = jnp.max(scores, axis=-1, keepdims=True)
        exponent = jnp.exp(scores - top)
        total = jnp.sum(exponent, axis=-1, keepdims=True)
        prob = (exponent * (1.0 / total)).astype(BF16)
        prob_ref[h] = prob
        mixed.append(dot(prob, value))
    mix_ref[...] = jnp.where(first, mixed[0], mixed[1]).astype(BF16)


def gather_rows(spot_ref, kept_ref, rows_refs):
    slots, features = rows_refs[0].shape
    tokens = kept_ref.shape[1]
    total = jnp.zeros((tokens, features), F32)
    for j, rows_ref in enumerate(rows_refs):
        hot = slot_hot(kept_ref[0:2, :], spot_ref[0] ^ j, slots, tokens)
        total = total + dot(hot, rows_ref[...], 0, 0)
    return total


def near_kernel(spot_ref, kept_ref, hidden_ref, *refs):
    d_ref, block_ref = refs[-2:]
    slots, tokens = refs[0].shape[0] // 2, kept_ref.shape[1]
    d_total = jnp.zeros(d_ref.shape, F32)
    y_total = hidden_ref[...]
    for j, rows_ref in enumerate(refs[:-2]):
        hot = slot_hot(kept_ref[0:2, :], spot_ref[0] ^ j, slots, tokens)
        d_total = d_total + dot(hot, rows_ref[:slots, :], 0, 0)
        y_total = y_total + dot(hot, rows_ref[slots:, :], 0, 0)
    d_ref[...] = d_total
    block_ref[...] = y_total


def gather_pass_kernel(group, spot_ref, kept_ref, *refs):
    refs[2 * group][...] = gather_rows(spot_ref, kept_ref, refs[:group]).astype(BF16)


def gather_kernel(spot_ref, kept_ref, *refs):
    refs[-1][...] = gather_rows(spot_ref, kept_ref, refs[:-1]).astype(BF16)


def block_kernel(block_ref, far_ref, out_ref):
    out_ref[...] = (block_ref[...] + far_ref[...].astype(F32)).astype(BF16)


def weight_grad_kernel(rows_ref, grad_ref, *refs):
    refs[-1][0] = dot(rows_ref[...], grad_ref[...], 0, 0).astype(BF16)


def widen_kernel(both_ref, in_ref, out_ref):
    in_ref[...] = both_ref[0].astype(F32).T
    out_ref[...] = both_ref[1].astype(F32)


def halves_by(bit, value):
    rows = value.shape[0] // 2
    low, high = value[:rows], value[rows:]
    return jnp.where(bit > 0, high, low), jnp.where(bit > 0, low, high)


def as_column(row, column):
    at = (iota((8, 128), 1) == column) & (iota((8, 128), 0) == 0)
    return dot(jnp.broadcast_to(row, (8, row.shape[1])), at.astype(F32), 0, 0, lax.Precision.HIGHEST)


def hidden_back_kernel(
    spot_ref, near_ref, far_ref, hidden_ref, cot_ref, gm_ref, wo_ref, mix_ref, gwra_ref, gwrb_ref, _,
    dhid_ref, dmix_ref, keep_ref, give_ref, __,
):
    features = hidden_ref.shape[1]
    bit = spot_ref[1]
    grad = near_ref[...] + far_ref[...].astype(F32)
    unit, scale = norm_parts(hidden_ref[...])
    gain = jnp.sum(grad * unit, axis=0, keepdims=True)
    dhid = cot_ref[...].astype(F32) + norm_back(unit, scale, grad * gm_ref[...])
    dhid_ref[...] = dhid
    branch = dhid.astype(BF16)
    keep, give = halves_by(bit, dot(mix_ref[...], branch, 0, 0))
    keep_ref[:, :features], give_ref[:, :features] = keep.astype(BF16), give.astype(BF16)
    dmix_ref[...] = dot(branch, wo_ref[...], 1, 1).astype(BF16)
    experts = gwra_ref.shape[1]
    wide = (iota((experts, 128), 0) == iota((experts, 128), 1)).astype(F32)
    side = dot(gwra_ref[...] + gwrb_ref[...], wide, precision=lax.Precision.HIGHEST)
    side = side + as_column(gain, experts)
    keep, give = halves_by(bit, side)
    keep_ref[:, features:], give_ref[:, features:] = keep.astype(BF16), give.astype(BF16)


def head_pair_back(offset, dmix_ref, proj_ref, mix_ref, prob_ref, dproj_ref):
    step = pl.program_id(0)
    tokens, features = mix_ref.shape
    width = dproj_ref.shape[1] // 3
    at = lambda part: pl.ds(pl.multiple_of(part * features + (step + offset) * 128, 128), 128)
    query, keys, value = proj_ref[:, at(0)], proj_ref[:, at(1)], proj_ref[:, at(2)]
    dmix = dmix_ref[:, at(0)]
    product = dmix.astype(F32) * mix_ref[:, at(0)].astype(F32)
    first = iota((tokens, 128), 1) < HEAD_DIM
    parts = []
    for h in (0, 1):
        mine = first if h == 0 else ~first
        own_dmix = jnp.where(mine, dmix.astype(F32), 0.0).astype(BF16)
        delta = jnp.sum(jnp.where(mine, product, 0.0), axis=-1, keepdims=True)
        prob = prob_ref[h]
        dprob = dot(own_dmix, value, 1, 1)
        dscore = (prob.astype(F32) * (dprob - delta) * HEAD_DIM ** (-0.5)).astype(BF16)
        parts.append((dot(dscore, keys), dot(dscore, query, 0, 0), dot(prob, dmix, 0, 0)))
    for part in range(3):
        to = pl.ds(pl.multiple_of(part * width + step * 128, 128), 128)
        dproj_ref[:, to] = jnp.where(first, parts[0][part], parts[1][part]).astype(BF16)


def first_heads_kernel(
    spot_ref, dmix_ref, normed_ref, proj_ref, mix_ref, prob_ref, keep_ref, give_ref, dproj_ref,
):
    head_pair_back(0, dmix_ref, proj_ref, mix_ref, prob_ref, dproj_ref)

    @pl.when(pl.program_id(0) == pl.num_programs(0) - 1)
    def _():
        keep, give = halves_by(spot_ref[1], dot(normed_ref[...], dproj_ref[...], 0, 0))
        keep_ref[...], give_ref[...] = keep.astype(BF16), give.astype(BF16)


def last_heads_kernel(
    spot_ref, dmix_ref, normed_ref, proj_ref, mix_ref, prob_ref, keep_ref, give_ref, dproj_ref,
):
    head_pair_back(pl.num_programs(0), dmix_ref, proj_ref, mix_ref, prob_ref, dproj_ref)

    @pl.when(pl.program_id(0) == pl.num_programs(0) - 1)
    def _():
        keep, give = halves_by(spot_ref[1], dot(normed_ref[...], dproj_ref[...], 0, 0))
        keep_ref[...], give_ref[...] = keep.astype(BF16), give.astype(BF16)


def token_grad_kernel(first_ref, last_ref, dhid_ref, tok_ref, ga_ref, wqkv_ref, gtok_ref):
    tokens, features = tok_ref.shape
    grad = jnp.zeros((tokens, features), F32)
    half = features // 2
    for part in range(3):
        at = slice(part * half, (part + 1) * half)
        for place, ref in ((0, first_ref), (1, last_ref)):
            start = part * features + place * half
            grad = grad + dot(ref[:, at], wqkv_ref[:, start : start + half], 1, 1)
    unit, scale = norm_parts(tok_ref[...].astype(F32))
    gtok_ref[...] = dhid_ref[...] + norm_back(unit, scale, grad * ga_ref[...])


def take(refs, count):
    return refs[:count], refs[count:]


def expert_kernel(pieces, group, near, *refs):
    step = pl.program_id(0)
    (spot_ref, wr_ref, own_ref, win_ref, wout_ref), refs = take(refs, 5)
    mine = (spot_ref[0] - spot_ref[3]) ^ step
    if near:
        x_refs, refs = take(refs, group)
        g_refs, refs = take(refs, group)
        back_refs, refs = take(refs, group)
    else:
        (far_ref,), refs = take(refs, 1)
        refs = refs[4:]
        dx_refs, refs = take(refs, group)
        y_refs, refs = take(refs, group)
    gwr_ref, dexp_ref, xcopy_ref, act_ref, dpre_ref, now_ref = refs
    slots = dexp_ref.shape[0]
    if near:
        for j in range(group):

            @pl.when(step == j)
            def _():
                xcopy_ref[...] = x_refs[j][...]
                now_ref[...] = g_refs[j][...]

    else:
        xcopy_ref[...] = far_ref[mine, :slots, :]
        now_ref[...] = far_ref[mine, slots:, :]

    x = xcopy_ref[...]
    g = now_ref[...].astype(F32)
    logits = dot(x, wr_ref[...])
    exponent = jnp.exp(logits - jnp.max(logits, axis=-1, keepdims=True))
    router = exponent / jnp.sum(exponent, axis=-1, keepdims=True)
    gate = jnp.sum(router * own_ref[...], axis=-1, keepdims=True)
    dexp = (gate * g).astype(BF16)
    dexp_ref[...] = dexp
    out = jnp.zeros(x.shape, F32)
    dx = jnp.zeros(x.shape, F32)
    width = win_ref.shape[1] // pieces
    for r in range(pieces):
        at = slice(r * width, (r + 1) * width)
        pre = dot(x, win_ref[:, at])
        square = pre * pre
        bend = jnp.tanh(pre * (0.7978845608028654 + 0.035677408136300125 * square))
        half = 0.5 + 0.5 * bend
        smooth = pre * half
        slope = half + smooth * (1.0 - half) * (1.5957691216057308 + 0.21406444881780075 * square)
        active = smooth.astype(BF16)
        act_ref[:, at] = active
        dpreact = (dot(dexp, wout_ref[at, :], 1, 1) * slope).astype(BF16)
        dpre_ref[:, at] = dpreact
        out = out + dot(active, wout_ref[at, :])
        dx = dx + dot(dpreact, win_ref[:, at], 1, 1)
    out = out.astype(BF16).astype(F32)
    y = (gate * out).astype(BF16)
    dgate = jnp.sum(g * out, axis=-1, keepdims=True)
    dlogits = (dgate * gate * (own_ref[...] - router)).astype(BF16)
    dx = (dx + dot(dlogits, wr_ref[...], 1, 1)).astype(BF16)
    if near:
        for j in range(group):

            @pl.when(step == j)
            def _():
                back_refs[j][:slots, :] = dx
                back_refs[j][slots:, :] = y

    else:
        for j in range(group):

            @pl.when(step == j)
            def _():
                y_refs[j][...] = y
                dx_refs[j][...] = dx

    @pl.when(step == 0)
    def _():
        gwr_ref[...] = jnp.zeros(gwr_ref.shape, F32)

    gwr_ref[...] += dot(x, dlogits, 0, 0)


def swap(value, axis, bit):
    size = lax.axis_size(axis)
    return lax.ppermute(value, axis, [(i, i ^ bit) for i in range(size)])


def bits_of(axis):
    size = lax.axis_size(axis)
    return [1 << b for b in range(size.bit_length() - 1)]


def deal_plane_kernel(spot_ref, *refs):
    in_refs, (own_ref, *out_refs, total_ref) = refs[:-5], refs[-5:]
    start = 0
    for keep_ref, other_ref in zip(in_refs[::2], in_refs[1::2]):
        total = keep_ref[...].astype(F32) + other_ref[...].astype(F32)
        rows, columns = total.shape
        total_ref[:, :, start : start + columns] = total.reshape(4, rows // 4, columns)
        start += columns
    spot = spot_ref[2] * 2 + spot_ref[4]
    own_ref[...] = total_ref[spot]
    for j, out_ref in enumerate(out_refs):
        out_ref[...] = total_ref[spot ^ (j + 1)].astype(BF16)


def deal_line_kernel(groups, spot_ref, own_ref, *refs):
    in_refs, (first_ref, *out_refs, total_ref) = refs[:3], refs[3:]
    total = own_ref[...]
    for ref in in_refs:
        total = total + ref[...].astype(F32)
    rows, columns = total.shape
    total_ref[...] = total.reshape(groups, rows // groups, columns)
    first_ref[...] = total_ref[spot_ref[5]]
    for j, out_ref in enumerate(out_refs):
        out_ref[...] = total_ref[spot_ref[5] ^ (j + 1)].astype(BF16)


def pile_kernel(own_ref, *refs):
    total = own_ref[...]
    for ref in refs[:-1]:
        total = total + ref[...].astype(F32)
    refs[-1][...] = total.astype(BF16)


def line_up_kernel(spot_ref, *refs):
    out_ref, total_ref = refs[-2:]
    for j, ref in enumerate(refs[:-2]):
        total_ref[spot_ref[5] ^ j] = ref[...].astype(F32)
    out_ref[...] = total_ref[...].reshape(out_ref.shape).astype(BF16)


def line_up_plane_kernel(spot_ref, *refs):
    out_ref, total_ref = refs[-2:]
    for j, ref in enumerate(refs[:-2]):
        total_ref[(spot_ref[2] * 2 + spot_ref[4]) ^ j] = ref[...]
    out_ref[...] = total_ref[...].reshape(out_ref.shape)


def finish_kernel(
    experts, spot_ref, wqkv_ref, ga_ref, a0, a1, o0, o1, s0, s1, b0, b1,
    grad_o_ref, grad_qkv_ref, gain_attn_ref, gain_moe_ref, router_ref, total_ref, side_ref,
):
    step = pl.program_id(0)
    rows, half = a0.shape
    for k, (a_ref, o_ref, s_ref, b_ref) in enumerate(((a0, o0, s0, b0), (a1, o1, s1, b1))):
        at = pl.ds(pl.multiple_of((spot_ref[1] ^ k) * rows, 8), rows)
        grad_qkv_ref[at, :half] = a_ref[...].astype(F32)
        grad_qkv_ref[at, half:] = b_ref[...].astype(F32)

        @pl.when(step < 2)
        def _():
            grad_o_ref[at, :] = o_ref[...].astype(F32)

        @pl.when(step == 0)
        def _():
            side_ref[at, :] = s_ref[...].astype(F32)

    part = jnp.sum(wqkv_ref[...].astype(F32) * grad_qkv_ref[...], axis=-1, keepdims=True)
    part = jnp.broadcast_to(part, total_ref.shape)

    @pl.when(step == 0)
    def _():
        total_ref[...] = part

    @pl.when(step > 0)
    def _():
        total_ref[...] += part

    @pl.when(step == 2)
    def _():
        side = side_ref[...].T
        router_ref[...] = side[:experts, :]
        gain_moe_ref[...] = side[experts : experts + 1, :].reshape(gain_moe_ref.shape)
        gain_attn_ref[...] = (total_ref[...].T[0:1, :] / ga_ref[...]).reshape(gain_attn_ref.shape)


def plane_swap(value, j):
    groups = lax.axis_size("expert")
    size = lax.axis_size("dp") * groups
    apart = (j >> 1) * 2 * groups + (j & 1)
    return lax.ppermute(value, ("dp", "expert"), [(i, i ^ apart) for i in range(size)])


def plane_deal(spot, halves, *after):
    scalar = pl.BlockSpec(memory_space=pltpu.SMEM)
    ins = [v for pair in halves for v in pair]
    rows, columns = halves[0][0].shape[0] // 4, sum(pair[0].shape[1] for pair in halves)
    piece = (rows, columns)
    return call(
        deal_plane_kernel, (1,), (spot, *ins), [scalar] + [whole(v.shape) for v in ins],
        [shape_of(piece, F32)] + [shape_of(piece, BF16)] * 3, [whole_out(piece)] * 4,
        [pltpu.VMEM((4, *piece), F32)],
        after=after,
    )


def line_deal(spot, dealt, groups, us, *after):
    scalar = pl.BlockSpec(memory_space=pltpu.SMEM)
    own, *out = dealt
    rows, columns = own.shape
    piece = (rows // groups, columns)
    arrived = [plane_swap(v, j + 1) for j, v in enumerate(out)]
    scratch = [pltpu.VMEM((groups, *piece), F32)]
    own, *out = call(
        functools.partial(deal_line_kernel, groups), (1,), (spot, own, *arrived),
        [scalar] + [whole((rows, columns))] * 4,
        (shape_of(piece, F32), *[shape_of(piece, BF16)] * (groups - 1)),
        (whole_out(piece),) * groups,
        scratch,
        us=us,
        after=after,
    )
    return [own] + [swap(v, "expert", 2 * (j + 1)) for j, v in enumerate(out)]


def line_up(spot, parts, *late_pile):
    scalar = pl.BlockSpec(memory_space=pltpu.SMEM)
    groups, piece = len(parts), parts[0].shape
    rows, columns = groups * piece[0], piece[1]
    scratch = [pltpu.VMEM((groups, *piece), F32)]
    total = call(
        pile_kernel, (1,), parts, [whole(piece)] * groups, shape_of(piece, BF16), whole_out(piece),
        after=late_pile,
    )
    own = call(
        line_up_kernel, (1,), (spot, total, *[swap(total, "expert", 2 * j) for j in range(1, groups)]),
        [scalar] + [whole(piece)] * groups,
        shape_of((rows, columns), BF16), whole_out((rows, columns)), scratch,
    )
    return own, [plane_swap(own, j) for j in (1, 2, 3)]


def line_up_plane(spot, own, arrived, *after):
    scalar = pl.BlockSpec(memory_space=pltpu.SMEM)
    rows, columns = own.shape
    half = (4 * rows, columns)
    own = call(
        line_up_plane_kernel, (1,), (spot, own, *arrived),
        [scalar] + [whole((rows, columns))] * 4,
        shape_of(half, BF16), whole_out(half), [pltpu.VMEM((4, rows, columns), BF16)],
        after=after,
    )
    return [own, swap(own, "dp", 1)]


def all_sum(value, steps):
    rows = value.shape[0]
    place = []
    for axis, bit in steps:
        half = value.shape[0] // 2
        mine = ((lax.axis_index(axis) & bit) > 0).astype(jnp.int32)
        keep = lax.dynamic_slice_in_dim(value, mine * half, half, 0)
        give = lax.dynamic_slice_in_dim(value, (1 - mine) * half, half, 0)
        value = (keep.astype(F32) + swap(give, axis, bit).astype(F32)).astype(BF16)
        place.append(mine)
    for (axis, bit), mine in zip(reversed(steps), reversed(place)):
        other = swap(value, axis, bit)
        low = jnp.where(mine > 0, other, value)
        high = jnp.where(mine > 0, value, other)
        value = jnp.concatenate([low, high], axis=0)
    return value


def local(
    tokens, segment_ids, pad_mask, routes, priority, gain_attn, w_qkv, w_o, gain_moe, w_router,
    w_in, w_out, cotangent,
):
    sequences, length, features = tokens.shape
    count = sequences * length
    experts = w_router.shape[1]
    groups = lax.axis_size("expert")
    replicas = lax.axis_size("dp")
    devices = groups * replicas
    group = groups // 2
    most = 4 * count // experts
    slots = -(-most // 16) * 16
    capacity = (42 * count * devices + 20 * experts - 1) // (20 * experts)
    me = lax.axis_index(("dp", "expert")).astype(jnp.int32).reshape(1)
    replica = lax.axis_index("dp")
    column = lax.axis_index("expert")
    spot = jnp.stack(
        [column, replica & 1, replica >> 1 & 1, column // group * group, column & 1, column >> 1]
    ).astype(jnp.int32)
    tok = tokens.reshape(count, features)
    cot = cotangent.reshape(count, features)
    ga = gain_attn.reshape(1, features)
    gm = gain_moe.reshape(1, features)
    full = (count, features)
    scalar = pl.BlockSpec(memory_space=pltpu.SMEM)
    sent = shape_of((slots, features), BF16)

    def across(value):
        return swap(value, "expert", group)

    def among(values):
        return [v if j == 0 else swap(v, "expert", j) for j, v in enumerate(values)]

    halves = [list(range(group)), list(range(group, groups))]
    joint = (group, 2 * slots, features)

    def half_exchange(value):
        return lax.all_to_all(value, "expert", 0, 0, axis_index_groups=halves, tiled=True)

    far_cot = across(cot)
    full_in = lax.all_gather(w_in[0], "dp", axis=1, tiled=True)
    full_out = lax.all_gather(w_out[0], "dp", axis=0, tiled=True)

    pairs = features // 128
    tile = lambda dtype: shape_of((count, features), dtype)
    prob_block = pl.BlockSpec((2, count, count), lambda i: (i, 0, 0))
    hist_shape = (devices, experts, BINS)
    hist, info, target = call(
        functools.partial(route_kernel, slots, experts),
        (1,),
        (routes.reshape(count, 2).T, priority.reshape(1, count), pad_mask.reshape(1, count)),
        [whole((2, count)), whole((1, count)), whole((1, count))],
        (shape_of(hist_shape, jnp.int32), shape_of((8, count), F32), shape_of((8, count), jnp.int32)),
        (whole_out(hist_shape), whole_out((8, count)), whole_out((8, count))),
        limit=LIMIT,
    )
    def spread(target, rows, us, *after):
        return call(
            functools.partial(spread_kernel, slots),
            (1,),
            (spot, target, rows),
            [scalar, whole((8, count)), whole(rows.shape)],
            [sent] * group,
            [whole_out((slots, features))] * group,
            us=us,
            after=after,
        limit=LIMIT,
        )

    near_g_sent = spread(target, cot, 1)
    near_g = among(near_g_sent)
    every = lax.all_to_all(hist, ("dp", "expert"), 0, 0, tiled=True)
    normed, proj = call(
        project_kernel,
        (1,),
        (tok, ga, w_qkv),
        [whole(full), whole((1, features)), whole(w_qkv.shape)],
        (tile(BF16), shape_of((count, 3 * features), BF16)),
        (whole_out(full), whole_out((count, 3 * features))),
        after=(near_g_sent[0],),
        limit=LIMIT,
    )
    lanes = lambda part: pl.BlockSpec((count, 128), lambda i: (0, part * pairs + i))
    mix, prob = call(
        attend_kernel,
        (pairs,),
        (proj, proj, proj, segment_ids.reshape(1, count), pad_mask.reshape(1, count)),
        [lanes(0), lanes(1), lanes(2), whole((1, count)), whole((1, count))],
        (tile(BF16), shape_of((HEADS, count, count), BF16)),
        (lanes(0), prob_block),
        [pltpu.VMEM((count, count), F32)],
        us=20000,
        after=(target,),
        limit=LIMIT,
    )
    cross_shape = (count + 16, features)
    hidden, cross, kept = call(
        functools.partial(hidden_kernel, capacity),
        (1,),
        (me, every, info, target, tok, mix, w_o, gm),
        [scalar, whole(hist_shape), whole((8, count)), whole((8, count)), whole(full), whole(full), whole(w_o.shape), whole((1, features))],
        (tile(F32), shape_of(cross_shape, BF16), shape_of((8, count), jnp.int32)),
        (whole_out(full), whole_out(cross_shape), whole_out((8, count))),
        limit=LIMIT,
    )
    far_x = across(cross)
    near_sent = spread(kept, cross, 20000, *near_g)
    near_x = among(near_sent)
    far_sent, far_kept = call(
        functools.partial(spread_joint_kernel, slots),
        (group,),
        (spot, far_x, far_cot),
        [scalar, whole(cross_shape), whole(full)],
        (shape_of(joint, BF16), shape_of((8, count), jnp.int32)),
        (pl.BlockSpec((1, 2 * slots, features), lambda e: (e, 0, 0)), whole_out((8, count))),
        after=(near_sent[0],),
        limit=LIMIT,
    )
    far_rows = half_exchange(far_sent)

    hidden_units = w_out.shape[1] * replicas
    own = (iota((1, experts), 1) == column).astype(F32)
    flat = group * slots
    slot_spec = whole_out((slots, features))
    weights = (spot, w_router, own, full_in, full_out)
    weight_specs = [scalar, whole(w_router.shape), whole((1, experts)), whole(full_in.shape), whole(full_out.shape)]
    tall = [shape_of((2 * flat, n), BF16) for n in (features, features, hidden_units, hidden_units)]
    tall_blocks = lambda first: [
        pl.BlockSpec((slots, v.shape[1]), lambda e: (first + e, 0)) for v in tall
    ]
    outs = call(
        functools.partial(expert_kernel, 4, group, True),
        (group,),
        (*weights, *near_x, *near_g),
        weight_specs + [whole((slots, features))] * (2 * group),
        (*[shape_of((2 * slots, features), BF16)] * group, shape_of(w_router.shape, F32), *tall),
        (*[whole_out((2 * slots, features))] * group, whole_out(w_router.shape), *tall_blocks(0)),
        [pltpu.VMEM((slots, features), BF16)],
        us=300000,
        after=(far_sent,),
        limit=LIMIT,
    )
    near_back, outs = take(outs, group)
    near_back = among(near_back)
    gwr_a, kept_rows = outs[0], outs[1:]
    outs = call(
        functools.partial(expert_kernel, 4, group, False),
        (group,),
        (*weights, far_rows, *kept_rows),
        weight_specs + [whole(joint)] + [pl.BlockSpec(memory_space=pl.ANY)] * 4,
        (*[sent] * (2 * group), shape_of(w_router.shape, F32), *tall),
        (*[slot_spec] * (2 * group), whole_out(w_router.shape), *tall_blocks(group)),
        [pltpu.VMEM((slots, features), BF16)],
        after=(gwr_a,),
        alias=[(6 + i, 2 * group + 1 + i) for i in range(4)],
    )
    d_far, outs = take(outs, group)
    y_far, outs = take(outs, group)
    gwr_b, all_dexp, all_x, all_act, all_dpre = outs
    d_far = among(d_far)
    def gather(rows, *after):
        return call(
            gather_kernel,
            (1,),
            (spot, far_kept, *rows),
            [scalar, whole((8, count))] + [whole((slots, features))] * group,
            tile(BF16),
            whole_out(full),
            after=after,
        )

    anywhere = pl.BlockSpec(memory_space=pl.ANY)
    part = hidden_units // 4
    both_shape = shape_of((2, hidden_units, features), BF16)

    def weight_grad(which, rows, grad, us, after, *given):
        return call(
            weight_grad_kernel,
            (4,),
            (rows, grad, *given),
            [pl.BlockSpec((2 * flat, part), lambda i: (0, i)), whole((2 * flat, features))] + [anywhere] * len(given),
            both_shape,
            pl.BlockSpec((1, part, features), lambda i: (which, i, 0)),
            us=us,
            after=after,
            alias=[(2, 0)] if given else (),
        )

    both = weight_grad(1, all_act, all_dexp, 1, near_back)
    d_far, *y_far = call(
        functools.partial(gather_pass_kernel, group),
        (1,),
        (spot, far_kept, *d_far, *y_far),
        [scalar, whole((8, count))] + [whole((slots, features))] * group + [anywhere] * group,
        [tile(BF16)] + [sent] * group,
        [whole_out(full)] + [anywhere] * group,
        after=(both,),
        alias=[(2 + group + j, 1 + j) for j in range(group)],
    )
    y_far = among(y_far)
    both = weight_grad(0, all_dpre, all_x, 60000, (d_far,), both)
    near_d, block_part = call(
        near_kernel,
        (1,),
        (spot, kept, hidden, *near_back),
        [scalar, whole((8, count)), whole(full)] + [whole((2 * slots, features))] * group,
        (tile(F32), tile(F32)),
        (whole_out(full), whole_out(full)),
        after=(both,),
    )

    y_far = gather(y_far, near_d)
    d_far = across(d_far)
    both = lax.psum_scatter(both, "dp", scatter_dimension=1, tiled=True)

    o_half = (features // 2, features + 128)
    a_half = (features // 2, 3 * features // 2)
    dhid, dmix, keep_o, give_o, y_far = call(
        hidden_back_kernel,
        (1,),
        (spot, near_d, d_far, hidden, cot, gm, w_o, mix, gwr_a, gwr_b, y_far),
        [scalar] + [whole(full)] * 4 + [whole((1, features)), whole(w_o.shape), whole(full)] + [whole(gwr_a.shape)] * 2 + [anywhere],
        (tile(F32), tile(BF16), *[shape_of(o_half, BF16)] * 2, tile(BF16)),
        (whole_out(full), whole_out(full), *[whole_out(o_half)] * 2, anywhere),
        us=400000,
        alias=[(10, 4)],
    )
    y_far = across(y_far)
    some = 3 * features // 2
    head_specs = lambda offset: [scalar] + [whole(full)] * 2 + [whole((count, 3 * features)), whole(full)] + [
        pl.BlockSpec((2, count, count), lambda i: (i + offset, 0, 0))
    ]
    keep_a, give_a, dproj_a = call(
        first_heads_kernel,
        (pairs // 2,),
        (spot, dmix, normed, proj, mix, prob),
        head_specs(0),
        (shape_of(a_half, BF16), shape_of(a_half, BF16), shape_of((count, some), BF16)),
        (whole_out(a_half), whole_out(a_half), whole_out((count, some))),
        us=13000,
    )
    by_hand = replicas == 4 and groups == 8 and features % (8 * devices) == 0
    if by_hand:
        beside = lambda keep, give: (keep, swap(give, "dp", 1))
        early = plane_deal(spot, [beside(keep_a, give_a), beside(keep_o, give_o)])
    keep_b, give_b, dproj_b = call(
        last_heads_kernel,
        (pairs // 2,),
        (spot, dmix, normed, proj, mix, prob),
        head_specs(pairs // 2),
        (shape_of(a_half, BF16), shape_of(a_half, BF16), shape_of((count, some), BF16)),
        (whole_out(a_half), whole_out(a_half), whole_out((count, some))),
        us=50000,
        after=early[:1] if by_hand else (),
    )
    gtok = call(
        token_grad_kernel,
        (1,),
        (dproj_a, dproj_b, dhid, tok, ga, w_qkv),
        [whole((count, some))] * 2 + [whole(full)] * 2 + [whole((1, features)), whole(w_qkv.shape)],
        tile(F32),
        whole_out(full),
    )
    block_out = call(
        block_kernel,
        (1,),
        (block_part, y_far),
        [whole(full)] * 2,
        tile(BF16),
        whole_out(full),
        after=(gtok,),
    )
    shapes = [w_in.shape[1:], w_out.shape[1:]]
    gin, gout = call(
        widen_kernel,
        (1,),
        (both,),
        [whole(both.shape)],
        [shape_of(v, F32) for v in shapes],
        [whole_out(v) for v in shapes],
        after=(gtok,),
    )
    if by_hand:
        rows = groups // 2
        early = line_deal(spot, early, rows, 30000, gtok)
        late = plane_deal(spot, [beside(keep_b, give_b)], early[0])
        early, early_parts = line_up(spot, early, late[0], y_far)
        late, late_parts = line_up(spot, line_deal(spot, late, rows, 1, early))
        pieces = line_up_plane(spot, early, early_parts, late) + line_up_plane(
            spot, late, late_parts, gin, block_out
        )
        half = features // 2
        block = lambda width, index: [pl.BlockSpec((half, width), lambda i: (0, index(i)))] * 2
        third = lambda i: (0, i)
        grad_o, grad_qkv, gain_attn_grad, gain_moe_grad, grad_router = call(
            functools.partial(finish_kernel, experts),
            (3,),
            (spot, w_qkv, ga, *pieces[:2] * 3, *pieces[2:]),
            [scalar, pl.BlockSpec((features, features), third), whole((1, features))]
            + block(half, lambda i: i)
            + block(half, lambda i: jnp.minimum(3 + i, 4))
            + block(128, lambda i: 5 * half // 128)
            + block(half, lambda i: i),
            [shape_of(v, F32) for v in ((features, features), (features, 3 * features), (features,), (features,), (experts, features))],
            [
                pl.BlockSpec((features, half), lambda i: (0, jnp.minimum(i, 1))),
                pl.BlockSpec((features, features), third),
                whole_out((features,)),
                whole_out((features,)),
                whole_out((experts, features)),
            ],
            [pltpu.VMEM((features, 128), F32)] * 2,
        )
    else:
        low = (replica & 1) == 0

        def rejoin(keep, give):
            return jnp.concatenate([jnp.where(low, keep, give), jnp.where(low, give, keep)], axis=0)

        gain_steps = [("dp", b) for b in bits_of("dp")] + [("expert", b) for b in bits_of("expert")]
        both = all_sum(rejoin(keep_o, give_o), gain_steps).astype(F32)
        grad_o, side_o = both[:, :features], both[:, features:]
        first = all_sum(rejoin(keep_a, give_a), gain_steps).astype(F32)
        last = all_sum(rejoin(keep_b, give_b), gain_steps).astype(F32)
        half = features // 2
        cut = lambda part: slice(part * half, (part + 1) * half)
        grad_qkv = jnp.concatenate([v[:, cut(part)] for part in range(3) for v in (first, last)], axis=1)
        product = jnp.sum(w_qkv.astype(F32) * grad_qkv, axis=1)
        gain_attn_grad, gain_moe_grad = product / gain_attn, side_o[:, experts]
        grad_router = side_o[:, :experts].T
    return (
        block_out.reshape(sequences, length, features),
        gtok.reshape(sequences, length, features),
        gain_attn_grad.reshape(features),
        grad_qkv,
        grad_o,
        gain_moe_grad.reshape(features),
        grad_router.T,
        gin[None],
        gout[None],
    )


def solution(mesh):
    rows = P(("dp", "expert"), None, None)
    flat = P(("dp", "expert"), None)
    first = P("expert", None, "dp")
    second = P("expert", "dp", None)
    return jax.shard_map(
        local,
        mesh=mesh,
        in_specs=(rows, flat, flat, rows, flat, P(), P(), P(), P(), P(), first, second, rows),
        out_specs=(rows, rows, P(), P(), P(), P(), P(), first, second),
        check_vma=False,
    )
```

```python
import functools

import jax
import jax.numpy as jnp
from jax import lax
from jax.experimental import pallas as pl
from jax.experimental.pallas import tpu as pltpu
from jax.sharding import PartitionSpec as P

HEADS = 12
HEAD_DIM = 64
LEVELS = 64
BINS = 2 * LEVELS
LIMIT = 60 * 1024 * 1024
LATE = 44 * 1024 * 1024
F32 = jnp.float32
BF16 = jnp.bfloat16


def dot(a, b, ca=1, cb=0, precision=None):
    return lax.dot_general(
        a, b, (((ca,), (cb,)), ((), ())), precision=precision, preferred_element_type=F32
    )


def whole(shape):
    zeros = (0,) * len(shape)
    return pl.BlockSpec(shape, lambda *_: zeros, pipeline_mode=pl.Buffered(1))


def whole_out(shape):
    zeros = (0,) * len(shape)
    return pl.BlockSpec(shape, lambda *_: zeros)


def iota(shape, dim):
    return lax.broadcasted_iota(jnp.int32, shape, dim)


def call(kernel, grid, ins, in_specs, outs, out_specs, scratch=(), us=1, after=(), alias=(), limit=None):
    late = len(after)

    def body(*refs):
        kernel(*refs[late:])

    return pl.pallas_call(
        body,
        grid=grid,
        in_specs=[pl.BlockSpec(memory_space=pl.ANY)] * late + in_specs,
        out_specs=out_specs,
        out_shape=outs,
        scratch_shapes=list(scratch),
        input_output_aliases={late + i: o for i, o in alias},
        compiler_params=pltpu.CompilerParams(vmem_limit_bytes=limit or LATE),
        cost_estimate=pl.CostEstimate(flops=us * 10**6, bytes_accessed=0, transcendentals=0),
    )(*after, *ins)


def shape_of(shape, dtype):
    return jax.ShapeDtypeStruct(shape, dtype)


def norm_parts(values):
    center = values - jnp.mean(values, axis=-1, keepdims=True)
    spread = jnp.mean(center * center, axis=-1, keepdims=True)
    scale = lax.rsqrt(spread + 1e-06)
    return center * scale, scale


def norm_back(unit, scale, grad_unit):
    return scale * (
        grad_unit
        - jnp.mean(grad_unit, axis=-1, keepdims=True)
        - unit * jnp.mean(grad_unit * unit, axis=-1, keepdims=True)
    )


def class_rows(level_row, which, tokens):
    return (iota((BINS, tokens), 0) == which * LEVELS + (LEVELS - 1) - level_row).astype(F32)


def route_kernel(slots, experts, routes_ref, prio_ref, pad_ref, hist_ref, info_ref, target_ref):
    tokens = routes_ref.shape[1]
    rows = routes_ref[...].astype(F32)
    prio = prio_ref[...]
    valid = (pad_ref[...] > 0).astype(F32)
    early = iota((tokens, tokens), 0) < iota((tokens, tokens), 1)
    hot = [(iota((experts, tokens), 0) == rows[k : k + 1].astype(jnp.int32)).astype(F32) for k in (0, 1)]
    count = dot((hot[0] + hot[1]).astype(BF16), early.astype(BF16))
    hist = jnp.zeros((experts, BINS), F32)
    sides = jnp.where(iota((8, tokens), 0) == 2, prio.astype(F32), valid)
    for k in (0, 1):
        sides = jnp.where(iota((8, tokens), 0) == k, rows[k : k + 1], sides)
    eye = (iota((8, 8), 0) == iota((8, 8), 1)).astype(F32)
    cols = dot(sides, eye, 0, 0)
    prio_col = cols[:, 2:3]
    valid_col = cols[:, 3:4]
    for k in (0, 1):
        slot = jnp.sum(hot[k] * count, axis=0, keepdims=True)
        info_ref[k : k + 1, :] = rows[k : k + 1]
        info_ref[2 + k : 3 + k, :] = rows[k : k + 1] * slots + slot
        hist = hist + dot(hot[k] * valid, class_rows(prio, k, tokens), 1, 1)
        code_row = rows[k : k + 1] * LEVELS + prio.astype(F32)
        code_col = jnp.where(valid_col > 0, cols[:, k : k + 1] * LEVELS + prio_col, -1.0)
        same = (code_col == code_row) & early
        info_ref[4 + k : 5 + k, :] = jnp.sum(same.astype(F32), axis=0, keepdims=True)
    info_ref[6:7, :] = prio.astype(F32)
    info_ref[7:8, :] = valid
    target_ref[...] = jnp.full(target_ref.shape, -1, jnp.int32)
    target_ref[0:2, :] = info_ref[2:4, :].astype(jnp.int32)
    hist_ref[...] = jnp.broadcast_to(hist.astype(jnp.int32)[None], hist_ref.shape)


def slot_hot(target_rows, expert, slots, tokens):
    place = iota((slots, tokens), 0) + expert * slots
    return ((place == target_rows[0:1]) | (place == target_rows[1:2])).astype(F32).astype(BF16)


def spread_kernel(slots, spot_ref, target_ref, rows_ref, *out_refs):
    tokens = target_ref.shape[1]
    for j, out_ref in enumerate(out_refs):
        hot = slot_hot(target_ref[0:2, :], spot_ref[0] ^ j, slots, tokens)
        out_ref[...] = dot(hot, rows_ref[:tokens, :]).astype(BF16)


def spread_joint_kernel(slots, spot_ref, x_ref, g_ref, out_ref, kept_ref):
    expert, tokens = spot_ref[3] + pl.program_id(0), g_ref.shape[0]

    @pl.when(pl.program_id(0) == 0)
    def _():
        codes = x_ref[tokens:, :tokens].astype(F32).astype(jnp.int32)
        kept_ref[...] = jnp.full(kept_ref.shape, -1, jnp.int32)
        for k in (0, 1):
            kept_ref[k : k + 1, :] = codes[2 * k : 2 * k + 1] * 64 + codes[2 * k + 1 : 2 * k + 2] - 1

    hot = slot_hot(kept_ref[0:2, :], expert, slots, tokens)
    out_ref[0, :slots] = dot(hot, x_ref[:tokens, :]).astype(BF16)
    out_ref[0, slots:] = dot(hot, g_ref[...]).astype(BF16)


def hidden_kernel(
    capacity, me_ref, hist_ref, info_ref, target_ref, tok_ref, mix_ref, wo_ref, gm_ref,
    hidden_ref, cross_ref, kept_ref,
):
    devices, experts, bins = hist_ref.shape
    tokens = info_ref.shape[1]
    hidden = tok_ref[...].astype(F32) + dot(mix_ref[...], wo_ref[...])
    hidden_ref[...] = hidden
    unit, _ = norm_parts(hidden)
    cross_ref[:tokens, :] = (unit * gm_ref[...]).astype(BF16)

    def add(j, sums):
        block = hist_ref[j].astype(F32)
        lower = (j < me_ref[0]).astype(F32)
        return sums[0] + block, sums[1] + block * lower

    zero = jnp.zeros((experts, bins), F32)
    totals, before = lax.fori_loop(0, devices, add, (zero, zero))
    early = (iota((bins, bins), 0) < iota((bins, bins), 1)).astype(F32)
    exact = lax.Precision.HIGHEST
    base = dot(totals, early, precision=exact) + before
    prio = info_ref[6:7, :].astype(jnp.int32)
    valid = info_ref[7:8, :] > 0
    kept_ref[...] = jnp.full(kept_ref.shape, -1, jnp.int32)
    codes = jnp.zeros((16, tokens), jnp.int32)
    row = iota((16, tokens), 0)
    for k in (0, 1):
        hot = (iota((experts, tokens), 0) == info_ref[k : k + 1, :].astype(jnp.int32)).astype(F32)
        spot = dot(base, class_rows(prio, k, tokens), precision=exact)
        rank = jnp.sum(hot * spot, axis=0, keepdims=True) + info_ref[4 + k : 5 + k, :]
        kept = valid & (rank < capacity - 0.5)
        place = jnp.where(kept, target_ref[k : k + 1, :], -1)
        kept_ref[k : k + 1, :] = place
        codes = jnp.where(row == 2 * k, (place + 1) >> 6, codes)
        codes = jnp.where(row == 2 * k + 1, (place + 1) & 63, codes)
    cross_ref[tokens:, :] = jnp.zeros((16, cross_ref.shape[1]), BF16)
    cross_ref[tokens:, :tokens] = codes.astype(F32).astype(BF16)


def project_kernel(tok_ref, ga_ref, wqkv_ref, normed_ref, proj_ref):
    unit, _ = norm_parts(tok_ref[...].astype(F32))
    normed = (unit * ga_ref[...]).astype(BF16)
    normed_ref[...] = normed
    features = tok_ref.shape[1]
    for part in range(3):
        at = slice(part * features, (part + 1) * features)
        proj_ref[:, at] = dot(normed, wqkv_ref[:, at]).astype(BF16)


def attend_kernel(query_ref, keys_ref, value_ref, seg_ref, pad_ref, mix_ref, prob_ref, bias_ref):
    step = pl.program_id(0)
    tokens = query_ref.shape[0]

    @pl.when(step == 0)
    def _():
        seg = seg_ref[...].astype(F32)
        eye = (iota((8, 8), 0) == iota((8, 8), 1)).astype(F32)
        seg_col = dot(jnp.broadcast_to(seg, (8, tokens)), eye, 0, 0)[:, 0:1]
        own = iota((tokens, tokens), 0) == iota((tokens, tokens), 1)
        allowed = (seg_col == seg) & ((pad_ref[...] > 0) | own)
        bias_ref[...] = jnp.where(allowed, 0.0, -1e30)

    query, keys, value = query_ref[...], keys_ref[...], value_ref[...]
    first = iota((tokens, 128), 1) < HEAD_DIM
    mixed = []
    for h in (0, 1):
        mine = first if h == 0 else ~first
        own_query = jnp.where(mine, query.astype(F32) * HEAD_DIM ** (-0.5), 0.0).astype(BF16)
        scores = dot(own_query, keys, 1, 1) + bias_ref[...]
        top = jnp.max(scores, axis=-1, keepdims=True)
        exponent = jnp.exp(scores - top)
        total = jnp.sum(exponent, axis=-1, keepdims=True)
        prob = (exponent * (1.0 / total)).astype(BF16)
        prob_ref[h] = prob
        mixed.append(dot(prob, value))
    mix_ref[...] = jnp.where(first, mixed[0], mixed[1]).astype(BF16)


def gather_rows(spot_ref, kept_ref, rows_refs):
    slots, features = rows_refs[0].shape
    tokens = kept_ref.shape[1]
    total = jnp.zeros((tokens, features), F32)
    for j, rows_ref in enumerate(rows_refs):
        hot = slot_hot(kept_ref[0:2, :], spot_ref[0] ^ j, slots, tokens)
        total = total + dot(hot, rows_ref[...], 0, 0)
    return total


def near_kernel(spot_ref, kept_ref, hidden_ref, *refs):
    d_ref, block_ref = refs[-2:]
    slots, tokens = refs[0].shape[0] // 2, kept_ref.shape[1]
    d_total = jnp.zeros(d_ref.shape, F32)
    y_total = hidden_ref[...]
    for j, rows_ref in enumerate(refs[:-2]):
        hot = slot_hot(kept_ref[0:2, :], spot_ref[0] ^ j, slots, tokens)
        d_total = d_total + dot(hot, rows_ref[:slots, :], 0, 0)
        y_total = y_total + dot(hot, rows_ref[slots:, :], 0, 0)
    d_ref[...] = d_total
    block_ref[...] = y_total


def gather_pass_kernel(group, spot_ref, kept_ref, *refs):
    refs[2 * group][...] = gather_rows(spot_ref, kept_ref, refs[:group]).astype(BF16)


def gather_kernel(spot_ref, kept_ref, *refs):
    refs[-1][...] = gather_rows(spot_ref, kept_ref, refs[:-1]).astype(BF16)


def block_kernel(block_ref, far_ref, out_ref):
    out_ref[...] = (block_ref[...] + far_ref[...].astype(F32)).astype(BF16)


def weight_grad_kernel(rows_ref, grad_ref, *refs):
    refs[-1][0] = dot(rows_ref[...], grad_ref[...], 0, 0).astype(BF16)


def widen_kernel(both_ref, in_ref, out_ref):
    in_ref[...] = both_ref[0].astype(F32).T
    out_ref[...] = both_ref[1].astype(F32)


def halves_by(bit, value):
    rows = value.shape[0] // 2
    low, high = value[:rows], value[rows:]
    return jnp.where(bit > 0, high, low), jnp.where(bit > 0, low, high)


def as_column(row, column):
    at = (iota((8, 128), 1) == column) & (iota((8, 128), 0) == 0)
    return dot(jnp.broadcast_to(row, (8, row.shape[1])), at.astype(F32), 0, 0, lax.Precision.HIGHEST)


def hidden_back_kernel(
    spot_ref, near_ref, far_ref, hidden_ref, cot_ref, gm_ref, wo_ref, mix_ref, gwra_ref, gwrb_ref, _,
    dhid_ref, dmix_ref, keep_ref, give_ref, __,
):
    features = hidden_ref.shape[1]
    bit = spot_ref[1]
    grad = near_ref[...] + far_ref[...].astype(F32)
    unit, scale = norm_parts(hidden_ref[...])
    gain = jnp.sum(grad * unit, axis=0, keepdims=True)
    dhid = cot_ref[...].astype(F32) + norm_back(unit, scale, grad * gm_ref[...])
    dhid_ref[...] = dhid
    branch = dhid.astype(BF16)
    keep, give = halves_by(bit, dot(mix_ref[...], branch, 0, 0))
    keep_ref[:, :features], give_ref[:, :features] = keep.astype(BF16), give.astype(BF16)
    dmix_ref[...] = dot(branch, wo_ref[...], 1, 1).astype(BF16)
    experts = gwra_ref.shape[1]
    wide = (iota((experts, 128), 0) == iota((experts, 128), 1)).astype(F32)
    side = dot(gwra_ref[...] + gwrb_ref[...], wide, precision=lax.Precision.HIGHEST)
    side = side + as_column(gain, experts)
    keep, give = halves_by(bit, side)
    keep_ref[:, features:], give_ref[:, features:] = keep.astype(BF16), give.astype(BF16)


def head_pair_back(offset, dmix_ref, proj_ref, mix_ref, prob_ref, dproj_ref):
    step = pl.program_id(0)
    tokens, features = mix_ref.shape
    width = dproj_ref.shape[1] // 3
    at = lambda part: pl.ds(pl.multiple_of(part * features + (step + offset) * 128, 128), 128)
    query, keys, value = proj_ref[:, at(0)], proj_ref[:, at(1)], proj_ref[:, at(2)]
    dmix = dmix_ref[:, at(0)]
    product = dmix.astype(F32) * mix_ref[:, at(0)].astype(F32)
    first = iota((tokens, 128), 1) < HEAD_DIM
    parts = []
    for h in (0, 1):
        mine = first if h == 0 else ~first
        own_dmix = jnp.where(mine, dmix.astype(F32), 0.0).astype(BF16)
        delta = jnp.sum(jnp.where(mine, product, 0.0), axis=-1, keepdims=True)
        prob = prob_ref[h]
        dprob = dot(own_dmix, value, 1, 1)
        dscore = (prob.astype(F32) * (dprob - delta) * HEAD_DIM ** (-0.5)).astype(BF16)
        parts.append((dot(dscore, keys), dot(dscore, query, 0, 0), dot(prob, dmix, 0, 0)))
    for part in range(3):
        to = pl.ds(pl.multiple_of(part * width + step * 128, 128), 128)
        dproj_ref[:, to] = jnp.where(first, parts[0][part], parts[1][part]).astype(BF16)


def first_heads_kernel(
    spot_ref, dmix_ref, normed_ref, proj_ref, mix_ref, prob_ref, keep_ref, give_ref, dproj_ref,
):
    head_pair_back(0, dmix_ref, proj_ref, mix_ref, prob_ref, dproj_ref)

    @pl.when(pl.program_id(0) == pl.num_programs(0) - 1)
    def _():
        keep, give = halves_by(spot_ref[1], dot(normed_ref[...], dproj_ref[...], 0, 0))
        keep_ref[...], give_ref[...] = keep.astype(BF16), give.astype(BF16)


def last_heads_kernel(
    spot_ref, dmix_ref, normed_ref, proj_ref, mix_ref, prob_ref, keep_ref, give_ref, dproj_ref,
):
    head_pair_back(pl.num_programs(0), dmix_ref, proj_ref, mix_ref, prob_ref, dproj_ref)

    @pl.when(pl.program_id(0) == pl.num_programs(0) - 1)
    def _():
        keep, give = halves_by(spot_ref[1], dot(normed_ref[...], dproj_ref[...], 0, 0))
        keep_ref[...], give_ref[...] = keep.astype(BF16), give.astype(BF16)


def token_grad_kernel(first_ref, last_ref, dhid_ref, tok_ref, ga_ref, wqkv_ref, gtok_ref):
    tokens, features = tok_ref.shape
    grad = jnp.zeros((tokens, features), F32)
    half = features // 2
    for part in range(3):
        at = slice(part * half, (part + 1) * half)
        for place, ref in ((0, first_ref), (1, last_ref)):
            start = part * features + place * half
            grad = grad + dot(ref[:, at], wqkv_ref[:, start : start + half], 1, 1)
    unit, scale = norm_parts(tok_ref[...].astype(F32))
    gtok_ref[...] = dhid_ref[...] + norm_back(unit, scale, grad * ga_ref[...])


def take(refs, count):
    return refs[:count], refs[count:]


def expert_kernel(pieces, group, near, *refs):
    step = pl.program_id(0)
    (spot_ref, wr_ref, own_ref, win_ref, wout_ref), refs = take(refs, 5)
    mine = (spot_ref[0] - spot_ref[3]) ^ step
    if near:
        x_refs, refs = take(refs, group)
        g_refs, refs = take(refs, group)
        back_refs, refs = take(refs, group)
    else:
        (far_ref,), refs = take(refs, 1)
        refs = refs[4:]
        dx_refs, refs = take(refs, group)
        y_refs, refs = take(refs, group)
    gwr_ref, dexp_ref, xcopy_ref, act_ref, dpre_ref, now_ref = refs
    slots = dexp_ref.shape[0]
    if near:
        for j in range(group):

            @pl.when(step == j)
            def _():
                xcopy_ref[...] = x_refs[j][...]
                now_ref[...] = g_refs[j][...]

    else:
        xcopy_ref[...] = far_ref[mine, :slots, :]
        now_ref[...] = far_ref[mine, slots:, :]

    x = xcopy_ref[...]
    g = now_ref[...].astype(F32)
    logits = dot(x, wr_ref[...])
    exponent = jnp.exp(logits - jnp.max(logits, axis=-1, keepdims=True))
    router = exponent / jnp.sum(exponent, axis=-1, keepdims=True)
    gate = jnp.sum(router * own_ref[...], axis=-1, keepdims=True)
    dexp = (gate * g).astype(BF16)
    dexp_ref[...] = dexp
    out = jnp.zeros(x.shape, F32)
    dx = jnp.zeros(x.shape, F32)
    width = win_ref.shape[1] // pieces
    for r in range(pieces):
        at = slice(r * width, (r + 1) * width)
        pre = dot(x, win_ref[:, at])
        square = pre * pre
        bend = jnp.tanh(pre * (0.7978845608028654 + 0.035677408136300125 * square))
        half = 0.5 + 0.5 * bend
        smooth = pre * half
        slope = half + smooth * (1.0 - half) * (1.5957691216057308 + 0.21406444881780075 * square)
        active = smooth.astype(BF16)
        act_ref[:, at] = active
        dpreact = (dot(dexp, wout_ref[at, :], 1, 1) * slope).astype(BF16)
        dpre_ref[:, at] = dpreact
        out = out + dot(active, wout_ref[at, :])
        dx = dx + dot(dpreact, win_ref[:, at], 1, 1)
    out = out.astype(BF16).astype(F32)
    y = (gate * out).astype(BF16)
    dgate = jnp.sum(g * out, axis=-1, keepdims=True)
    dlogits = (dgate * gate * (own_ref[...] - router)).astype(BF16)
    dx = (dx + dot(dlogits, wr_ref[...], 1, 1)).astype(BF16)
    if near:
        for j in range(group):

            @pl.when(step == j)
            def _():
                back_refs[j][:slots, :] = dx
                back_refs[j][slots:, :] = y

    else:
        for j in range(group):

            @pl.when(step == j)
            def _():
                y_refs[j][...] = y
                dx_refs[j][...] = dx

    @pl.when(step == 0)
    def _():
        gwr_ref[...] = jnp.zeros(gwr_ref.shape, F32)

    gwr_ref[...] += dot(x, dlogits, 0, 0)


def swap(value, axis, bit):
    size = lax.axis_size(axis)
    return lax.ppermute(value, axis, [(i, i ^ bit) for i in range(size)])


def bits_of(axis):
    size = lax.axis_size(axis)
    return [1 << b for b in range(size.bit_length() - 1)]


def deal_plane_kernel(spot_ref, *refs):
    in_refs, (own_ref, *out_refs, total_ref) = refs[:-5], refs[-5:]
    start = 0
    for keep_ref, other_ref in zip(in_refs[::2], in_refs[1::2]):
        total = keep_ref[...].astype(F32) + other_ref[...].astype(F32)
        rows, columns = total.shape
        total_ref[:, :, start : start + columns] = total.reshape(4, rows // 4, columns)
        start += columns
    spot = spot_ref[2] * 2 + spot_ref[4]
    own_ref[...] = total_ref[spot]
    for j, out_ref in enumerate(out_refs):
        out_ref[...] = total_ref[spot ^ (j + 1)].astype(BF16)


def deal_line_kernel(groups, spot_ref, own_ref, *refs):
    in_refs, (first_ref, *out_refs, total_ref) = refs[:3], refs[3:]
    total = own_ref[...]
    for ref in in_refs:
        total = total + ref[...].astype(F32)
    rows, columns = total.shape
    total_ref[...] = total.reshape(groups, rows // groups, columns)
    first_ref[...] = total_ref[spot_ref[5]]
    for j, out_ref in enumerate(out_refs):
        out_ref[...] = total_ref[spot_ref[5] ^ (j + 1)].astype(BF16)


def pile_kernel(own_ref, *refs):
    total = own_ref[...]
    for ref in refs[:-1]:
        total = total + ref[...].astype(F32)
    refs[-1][...] = total.astype(BF16)


def line_up_kernel(spot_ref, *refs):
    out_ref, total_ref = refs[-2:]
    for j, ref in enumerate(refs[:-2]):
        total_ref[spot_ref[5] ^ j] = ref[...].astype(F32)
    out_ref[...] = total_ref[...].reshape(out_ref.shape).astype(BF16)


def line_up_plane_kernel(spot_ref, *refs):
    out_ref, total_ref = refs[-2:]
    for j, ref in enumerate(refs[:-2]):
        total_ref[(spot_ref[2] * 2 + spot_ref[4]) ^ j] = ref[...]
    out_ref[...] = total_ref[...].reshape(out_ref.shape)


def finish_kernel(
    experts, spot_ref, wqkv_ref, ga_ref, a0, a1, o0, o1, s0, s1, b0, b1,
    grad_o_ref, grad_qkv_ref, gain_attn_ref, gain_moe_ref, router_ref, total_ref, side_ref,
):
    step = pl.program_id(0)
    rows, half = a0.shape
    for k, (a_ref, o_ref, s_ref, b_ref) in enumerate(((a0, o0, s0, b0), (a1, o1, s1, b1))):
        at = pl.ds(pl.multiple_of((spot_ref[1] ^ k) * rows, 8), rows)
        grad_qkv_ref[at, :half] = a_ref[...].astype(F32)
        grad_qkv_ref[at, half:] = b_ref[...].astype(F32)

        @pl.when(step < 2)
        def _():
            grad_o_ref[at, :] = o_ref[...].astype(F32)

        @pl.when(step == 0)
        def _():
            side_ref[at, :] = s_ref[...].astype(F32)

    part = jnp.sum(wqkv_ref[...].astype(F32) * grad_qkv_ref[...], axis=-1, keepdims=True)
    part = jnp.broadcast_to(part, total_ref.shape)

    @pl.when(step == 0)
    def _():
        total_ref[...] = part

    @pl.when(step > 0)
    def _():
        total_ref[...] += part

    @pl.when(step == 2)
    def _():
        side = side_ref[...].T
        router_ref[...] = side[:experts, :]
        gain_moe_ref[...] = side[experts : experts + 1, :].reshape(gain_moe_ref.shape)
        gain_attn_ref[...] = (total_ref[...].T[0:1, :] / ga_ref[...]).reshape(gain_attn_ref.shape)


def plane_swap(value, j):
    groups = lax.axis_size("expert")
    size = lax.axis_size("dp") * groups
    apart = (j >> 1) * 2 * groups + (j & 1)
    return lax.ppermute(value, ("dp", "expert"), [(i, i ^ apart) for i in range(size)])


def plane_deal(spot, halves, *after):
    scalar = pl.BlockSpec(memory_space=pltpu.SMEM)
    ins = [v for pair in halves for v in pair]
    rows, columns = halves[0][0].shape[0] // 4, sum(pair[0].shape[1] for pair in halves)
    piece = (rows, columns)
    return call(
        deal_plane_kernel, (1,), (spot, *ins), [scalar] + [whole(v.shape) for v in ins],
        [shape_of(piece, F32)] + [shape_of(piece, BF16)] * 3, [whole_out(piece)] * 4,
        [pltpu.VMEM((4, *piece), F32)],
        after=after,
    )


def line_deal(spot, dealt, groups, us, *after, ready=False):
    scalar = pl.BlockSpec(memory_space=pltpu.SMEM)
    own, *out = dealt
    rows, columns = own.shape
    piece = (rows // groups, columns)
    arrived = out if ready else [plane_swap(v, j + 1) for j, v in enumerate(out)]
    scratch = [pltpu.VMEM((groups, *piece), F32)]
    own, *out = call(
        functools.partial(deal_line_kernel, groups), (1,), (spot, own, *arrived),
        [scalar] + [whole((rows, columns))] * 4,
        (shape_of(piece, F32), *[shape_of(piece, BF16)] * (groups - 1)),
        (whole_out(piece),) * groups,
        scratch,
        us=us,
        after=after,
    )
    return [own] + [swap(v, "expert", 2 * (j + 1)) for j, v in enumerate(out)]


def line_up(spot, parts, *late_pile, waits=()):
    scalar = pl.BlockSpec(memory_space=pltpu.SMEM)
    groups, piece = len(parts), parts[0].shape
    rows, columns = groups * piece[0], piece[1]
    scratch = [pltpu.VMEM((groups, *piece), F32)]
    total = call(
        pile_kernel, (1,), parts, [whole(piece)] * groups, shape_of(piece, BF16), whole_out(piece),
        after=late_pile,
    )
    own = call(
        line_up_kernel, (1,), (spot, total, *[swap(total, "expert", 2 * j) for j in range(1, groups)]),
        [scalar] + [whole(piece)] * groups,
        shape_of((rows, columns), BF16), whole_out((rows, columns)), scratch,
        after=waits,
    )
    return own, [plane_swap(own, j) for j in (1, 2, 3)]


def line_up_plane(spot, own, arrived, *after):
    scalar = pl.BlockSpec(memory_space=pltpu.SMEM)
    rows, columns = own.shape
    half = (4 * rows, columns)
    own = call(
        line_up_plane_kernel, (1,), (spot, own, *arrived),
        [scalar] + [whole((rows, columns))] * 4,
        shape_of(half, BF16), whole_out(half), [pltpu.VMEM((4, rows, columns), BF16)],
        after=after,
    )
    return [own, swap(own, "dp", 1)]


def all_sum(value, steps):
    rows = value.shape[0]
    place = []
    for axis, bit in steps:
        half = value.shape[0] // 2
        mine = ((lax.axis_index(axis) & bit) > 0).astype(jnp.int32)
        keep = lax.dynamic_slice_in_dim(value, mine * half, half, 0)
        give = lax.dynamic_slice_in_dim(value, (1 - mine) * half, half, 0)
        value = (keep.astype(F32) + swap(give, axis, bit).astype(F32)).astype(BF16)
        place.append(mine)
    for (axis, bit), mine in zip(reversed(steps), reversed(place)):
        other = swap(value, axis, bit)
        low = jnp.where(mine > 0, other, value)
        high = jnp.where(mine > 0, value, other)
        value = jnp.concatenate([low, high], axis=0)
    return value


def local(
    tokens, segment_ids, pad_mask, routes, priority, gain_attn, w_qkv, w_o, gain_moe, w_router,
    w_in, w_out, cotangent,
):
    sequences, length, features = tokens.shape
    count = sequences * length
    experts = w_router.shape[1]
    groups = lax.axis_size("expert")
    replicas = lax.axis_size("dp")
    devices = groups * replicas
    group = groups // 2
    most = 4 * count // experts
    slots = -(-most // 16) * 16
    capacity = (42 * count * devices + 20 * experts - 1) // (20 * experts)
    me = lax.axis_index(("dp", "expert")).astype(jnp.int32).reshape(1)
    replica = lax.axis_index("dp")
    column = lax.axis_index("expert")
    spot = jnp.stack(
        [column, replica & 1, replica >> 1 & 1, column // group * group, column & 1, column >> 1]
    ).astype(jnp.int32)
    tok = tokens.reshape(count, features)
    cot = cotangent.reshape(count, features)
    ga = gain_attn.reshape(1, features)
    gm = gain_moe.reshape(1, features)
    full = (count, features)
    scalar = pl.BlockSpec(memory_space=pltpu.SMEM)
    sent = shape_of((slots, features), BF16)

    def across(value):
        return swap(value, "expert", group)

    def among(values):
        return [v if j == 0 else swap(v, "expert", j) for j, v in enumerate(values)]

    halves = [list(range(group)), list(range(group, groups))]
    joint = (group, 2 * slots, features)

    def half_exchange(value):
        return lax.all_to_all(value, "expert", 0, 0, axis_index_groups=halves, tiled=True)

    far_cot = across(cot)
    full_in = lax.all_gather(w_in[0], "dp", axis=1, tiled=True)
    full_out = lax.all_gather(w_out[0], "dp", axis=0, tiled=True)

    pairs = features // 128
    tile = lambda dtype: shape_of((count, features), dtype)
    prob_block = pl.BlockSpec((2, count, count), lambda i: (i, 0, 0))
    hist_shape = (devices, experts, BINS)
    hist, info, target = call(
        functools.partial(route_kernel, slots, experts),
        (1,),
        (routes.reshape(count, 2).T, priority.reshape(1, count), pad_mask.reshape(1, count)),
        [whole((2, count)), whole((1, count)), whole((1, count))],
        (shape_of(hist_shape, jnp.int32), shape_of((8, count), F32), shape_of((8, count), jnp.int32)),
        (whole_out(hist_shape), whole_out((8, count)), whole_out((8, count))),
        limit=LIMIT,
    )
    def spread(target, rows, us, *after):
        return call(
            functools.partial(spread_kernel, slots),
            (1,),
            (spot, target, rows),
            [scalar, whole((8, count)), whole(rows.shape)],
            [sent] * group,
            [whole_out((slots, features))] * group,
            us=us,
            after=after,
        limit=LIMIT,
        )

    near_g_sent = spread(target, cot, 1)
    near_g = among(near_g_sent)
    every = lax.all_to_all(hist, ("dp", "expert"), 0, 0, tiled=True)
    normed, proj = call(
        project_kernel,
        (1,),
        (tok, ga, w_qkv),
        [whole(full), whole((1, features)), whole(w_qkv.shape)],
        (tile(BF16), shape_of((count, 3 * features), BF16)),
        (whole_out(full), whole_out((count, 3 * features))),
        after=(near_g_sent[0],),
        limit=LIMIT,
    )
    lanes = lambda part: pl.BlockSpec((count, 128), lambda i: (0, part * pairs + i))
    mix, prob = call(
        attend_kernel,
        (pairs,),
        (proj, proj, proj, segment_ids.reshape(1, count), pad_mask.reshape(1, count)),
        [lanes(0), lanes(1), lanes(2), whole((1, count)), whole((1, count))],
        (tile(BF16), shape_of((HEADS, count, count), BF16)),
        (lanes(0), prob_block),
        [pltpu.VMEM((count, count), F32)],
        us=20000,
        after=(target,),
        limit=LIMIT,
    )
    cross_shape = (count + 16, features)
    hidden, cross, kept = call(
        functools.partial(hidden_kernel, capacity),
        (1,),
        (me, every, info, target, tok, mix, w_o, gm),
        [scalar, whole(hist_shape), whole((8, count)), whole((8, count)), whole(full), whole(full), whole(w_o.shape), whole((1, features))],
        (tile(F32), shape_of(cross_shape, BF16), shape_of((8, count), jnp.int32)),
        (whole_out(full), whole_out(cross_shape), whole_out((8, count))),
        limit=LIMIT,
    )
    far_x = across(cross)
    near_sent = spread(kept, cross, 20000, *near_g)
    near_x = among(near_sent)
    far_sent, far_kept = call(
        functools.partial(spread_joint_kernel, slots),
        (group,),
        (spot, far_x, far_cot),
        [scalar, whole(cross_shape), whole(full)],
        (shape_of(joint, BF16), shape_of((8, count), jnp.int32)),
        (pl.BlockSpec((1, 2 * slots, features), lambda e: (e, 0, 0)), whole_out((8, count))),
        after=(near_sent[0],),
        limit=LIMIT,
    )
    far_rows = half_exchange(far_sent)

    hidden_units = w_out.shape[1] * replicas
    own = (iota((1, experts), 1) == column).astype(F32)
    flat = group * slots
    slot_spec = whole_out((slots, features))
    weights = (spot, w_router, own, full_in, full_out)
    weight_specs = [scalar, whole(w_router.shape), whole((1, experts)), whole(full_in.shape), whole(full_out.shape)]
    tall = [shape_of((2 * flat, n), BF16) for n in (features, features, hidden_units, hidden_units)]
    tall_blocks = lambda first: [
        pl.BlockSpec((slots, v.shape[1]), lambda e: (first + e, 0)) for v in tall
    ]
    outs = call(
        functools.partial(expert_kernel, 4, group, True),
        (group,),
        (*weights, *near_x, *near_g),
        weight_specs + [whole((slots, features))] * (2 * group),
        (*[shape_of((2 * slots, features), BF16)] * group, shape_of(w_router.shape, F32), *tall),
        (*[whole_out((2 * slots, features))] * group, whole_out(w_router.shape), *tall_blocks(0)),
        [pltpu.VMEM((slots, features), BF16)],
        us=300000,
        after=(far_sent,),
        limit=LIMIT,
    )
    near_back, outs = take(outs, group)
    near_back = among(near_back)
    gwr_a, kept_rows = outs[0], outs[1:]
    outs = call(
        functools.partial(expert_kernel, 4, group, False),
        (group,),
        (*weights, far_rows, *kept_rows),
        weight_specs + [whole(joint)] + [pl.BlockSpec(memory_space=pl.ANY)] * 4,
        (*[sent] * (2 * group), shape_of(w_router.shape, F32), *tall),
        (*[slot_spec] * (2 * group), whole_out(w_router.shape), *tall_blocks(group)),
        [pltpu.VMEM((slots, features), BF16)],
        after=(gwr_a,),
        alias=[(6 + i, 2 * group + 1 + i) for i in range(4)],
    )
    d_far, outs = take(outs, group)
    y_far, outs = take(outs, group)
    gwr_b, all_dexp, all_x, all_act, all_dpre = outs
    d_far = among(d_far)
    def gather(rows, *after):
        return call(
            gather_kernel,
            (1,),
            (spot, far_kept, *rows),
            [scalar, whole((8, count))] + [whole((slots, features))] * group,
            tile(BF16),
            whole_out(full),
            after=after,
        )

    anywhere = pl.BlockSpec(memory_space=pl.ANY)
    part = hidden_units // 4
    both_shape = shape_of((2, hidden_units, features), BF16)

    def weight_grad(which, rows, grad, us, after, *given):
        return call(
            weight_grad_kernel,
            (4,),
            (rows, grad, *given),
            [pl.BlockSpec((2 * flat, part), lambda i: (0, i)), whole((2 * flat, features))] + [anywhere] * len(given),
            both_shape,
            pl.BlockSpec((1, part, features), lambda i: (which, i, 0)),
            us=us,
            after=after,
            alias=[(2, 0)] if given else (),
        )

    both = weight_grad(1, all_act, all_dexp, 1, near_back)
    d_far, *y_far = call(
        functools.partial(gather_pass_kernel, group),
        (1,),
        (spot, far_kept, *d_far, *y_far),
        [scalar, whole((8, count))] + [whole((slots, features))] * group + [anywhere] * group,
        [tile(BF16)] + [sent] * group,
        [whole_out(full)] + [anywhere] * group,
        after=(both,),
        alias=[(2 + group + j, 1 + j) for j in range(group)],
    )
    y_far = among(y_far)
    both = weight_grad(0, all_dpre, all_x, 60000, (d_far,), both)
    near_d, block_part = call(
        near_kernel,
        (1,),
        (spot, kept, hidden, *near_back),
        [scalar, whole((8, count)), whole(full)] + [whole((2 * slots, features))] * group,
        (tile(F32), tile(F32)),
        (whole_out(full), whole_out(full)),
        after=(both,),
    )

    y_far = gather(y_far, near_d)
    d_far = across(d_far)
    both = lax.psum_scatter(both, "dp", scatter_dimension=1, tiled=True)

    o_half = (features // 2, features + 128)
    a_half = (features // 2, 3 * features // 2)
    dhid, dmix, keep_o, give_o, y_far = call(
        hidden_back_kernel,
        (1,),
        (spot, near_d, d_far, hidden, cot, gm, w_o, mix, gwr_a, gwr_b, y_far),
        [scalar] + [whole(full)] * 4 + [whole((1, features)), whole(w_o.shape), whole(full)] + [whole(gwr_a.shape)] * 2 + [anywhere],
        (tile(F32), tile(BF16), *[shape_of(o_half, BF16)] * 2, tile(BF16)),
        (whole_out(full), whole_out(full), *[whole_out(o_half)] * 2, anywhere),
        us=400000,
        alias=[(10, 4)],
    )
    y_far = across(y_far)
    some = 3 * features // 2
    head_specs = lambda offset: [scalar] + [whole(full)] * 2 + [whole((count, 3 * features)), whole(full)] + [
        pl.BlockSpec((2, count, count), lambda i: (i + offset, 0, 0))
    ]
    keep_a, give_a, dproj_a = call(
        first_heads_kernel,
        (pairs // 2,),
        (spot, dmix, normed, proj, mix, prob),
        head_specs(0),
        (shape_of(a_half, BF16), shape_of(a_half, BF16), shape_of((count, some), BF16)),
        (whole_out(a_half), whole_out(a_half), whole_out((count, some))),
        us=13000,
    )
    by_hand = replicas == 4 and groups == 8 and features % (8 * devices) == 0
    if by_hand:
        beside = lambda keep, give: (keep, swap(give, "dp", 1))
        early = plane_deal(spot, [beside(keep_a, give_a), beside(keep_o, give_o)])
    keep_b, give_b, dproj_b = call(
        last_heads_kernel,
        (pairs // 2,),
        (spot, dmix, normed, proj, mix, prob),
        head_specs(pairs // 2),
        (shape_of(a_half, BF16), shape_of(a_half, BF16), shape_of((count, some), BF16)),
        (whole_out(a_half), whole_out(a_half), whole_out((count, some))),
        us=50000,
        after=early[:1] if by_hand else (),
    )
    gtok = call(
        token_grad_kernel,
        (1,),
        (dproj_a, dproj_b, dhid, tok, ga, w_qkv),
        [whole((count, some))] * 2 + [whole(full)] * 2 + [whole((1, features)), whole(w_qkv.shape)],
        tile(F32),
        whole_out(full),
    )
    block_out = call(
        block_kernel,
        (1,),
        (block_part, y_far),
        [whole(full)] * 2,
        tile(BF16),
        whole_out(full),
        after=(gtok,),
    )
    shapes = [w_in.shape[1:], w_out.shape[1:]]
    gin, gout = call(
        widen_kernel,
        (1,),
        (both,),
        [whole(both.shape)],
        [shape_of(v, F32) for v in shapes],
        [whole_out(v) for v in shapes],
        after=(gtok,),
    )
    if by_hand:
        rows = groups // 2
        early = line_deal(spot, early, rows, 30000, gtok)
        late = plane_deal(spot, [beside(keep_b, give_b)], early[0], y_far)
        late = [late[0]] + [plane_swap(v, j + 1) for j, v in enumerate(late[1:])]
        early, early_parts = line_up(spot, early, late[0], waits=late[2:])
        late, late_parts = line_up(spot, line_deal(spot, late, rows, 1, early, ready=True))
        pieces = line_up_plane(spot, early, early_parts, late) + line_up_plane(
            spot, late, late_parts, gin, block_out
        )
        half = features // 2
        block = lambda width, index: [pl.BlockSpec((half, width), lambda i: (0, index(i)))] * 2
        third = lambda i: (0, i)
        grad_o, grad_qkv, gain_attn_grad, gain_moe_grad, grad_router = call(
            functools.partial(finish_kernel, experts),
            (3,),
            (spot, w_qkv, ga, *pieces[:2] * 3, *pieces[2:]),
            [scalar, pl.BlockSpec((features, features), third), whole((1, features))]
            + block(half, lambda i: i)
            + block(half, lambda i: jnp.minimum(3 + i, 4))
            + block(128, lambda i: 5 * half // 128)
            + block(half, lambda i: i),
            [shape_of(v, F32) for v in ((features, features), (features, 3 * features), (features,), (features,), (experts, features))],
            [
                pl.BlockSpec((features, half), lambda i: (0, jnp.minimum(i, 1))),
                pl.BlockSpec((features, features), third),
                whole_out((features,)),
                whole_out((features,)),
                whole_out((experts, features)),
            ],
            [pltpu.VMEM((features, 128), F32)] * 2,
        )
    else:
        low = (replica & 1) == 0

        def rejoin(keep, give):
            return jnp.concatenate([jnp.where(low, keep, give), jnp.where(low, give, keep)], axis=0)

        gain_steps = [("dp", b) for b in bits_of("dp")] + [("expert", b) for b in bits_of("expert")]
        both = all_sum(rejoin(keep_o, give_o), gain_steps).astype(F32)
        grad_o, side_o = both[:, :features], both[:, features:]
        first = all_sum(rejoin(keep_a, give_a), gain_steps).astype(F32)
        last = all_sum(rejoin(keep_b, give_b), gain_steps).astype(F32)
        half = features // 2
        cut = lambda part: slice(part * half, (part + 1) * half)
        grad_qkv = jnp.concatenate([v[:, cut(part)] for part in range(3) for v in (first, last)], axis=1)
        product = jnp.sum(w_qkv.astype(F32) * grad_qkv, axis=1)
        gain_attn_grad, gain_moe_grad = product / gain_attn, side_o[:, experts]
        grad_router = side_o[:, :experts].T
    return (
        block_out.reshape(sequences, length, features),
        gtok.reshape(sequences, length, features),
        gain_attn_grad.reshape(features),
        grad_qkv,
        grad_o,
        gain_moe_grad.reshape(features),
        grad_router.T,
        gin[None],
        gout[None],
    )


def solution(mesh):
    rows = P(("dp", "expert"), None, None)
    flat = P(("dp", "expert"), None)
    first = P("expert", None, "dp")
    second = P("expert", "dp", None)
    return jax.shard_map(
        local,
        mesh=mesh,
        in_specs=(rows, flat, flat, rows, flat, P(), P(), P(), P(), P(), first, second, rows),
        out_specs=(rows, rows, P(), P(), P(), P(), P(), first, second),
        check_vma=False,
    )
```

```python
import functools

import jax
import jax.numpy as jnp
from jax import lax
from jax.experimental import pallas as pl
from jax.experimental.pallas import tpu as pltpu
from jax.sharding import PartitionSpec as P

HEADS = 12
HEAD_DIM = 64
LEVELS = 64
BINS = 2 * LEVELS
LIMIT = 60 * 1024 * 1024
LATE = 44 * 1024 * 1024
F32 = jnp.float32
BF16 = jnp.bfloat16


def dot(a, b, ca=1, cb=0, precision=None):
    return lax.dot_general(
        a, b, (((ca,), (cb,)), ((), ())), precision=precision, preferred_element_type=F32
    )


def whole(shape):
    zeros = (0,) * len(shape)
    return pl.BlockSpec(shape, lambda *_: zeros, pipeline_mode=pl.Buffered(1))


def whole_out(shape):
    zeros = (0,) * len(shape)
    return pl.BlockSpec(shape, lambda *_: zeros)


def iota(shape, dim):
    return lax.broadcasted_iota(jnp.int32, shape, dim)


def call(kernel, grid, ins, in_specs, outs, out_specs, scratch=(), us=1, after=(), alias=(), limit=None):
    late = len(after)

    def body(*refs):
        kernel(*refs[late:])

    return pl.pallas_call(
        body,
        grid=grid,
        in_specs=[pl.BlockSpec(memory_space=pl.ANY)] * late + in_specs,
        out_specs=out_specs,
        out_shape=outs,
        scratch_shapes=list(scratch),
        input_output_aliases={late + i: o for i, o in alias},
        compiler_params=pltpu.CompilerParams(vmem_limit_bytes=limit or LATE),
        cost_estimate=pl.CostEstimate(flops=us * 10**6, bytes_accessed=0, transcendentals=0),
    )(*after, *ins)


def shape_of(shape, dtype):
    return jax.ShapeDtypeStruct(shape, dtype)


def norm_parts(values):
    center = values - jnp.mean(values, axis=-1, keepdims=True)
    spread = jnp.mean(center * center, axis=-1, keepdims=True)
    scale = lax.rsqrt(spread + 1e-06)
    return center * scale, scale


def norm_back(unit, scale, grad_unit):
    return scale * (
        grad_unit
        - jnp.mean(grad_unit, axis=-1, keepdims=True)
        - unit * jnp.mean(grad_unit * unit, axis=-1, keepdims=True)
    )


def class_rows(level_row, which, tokens):
    return (iota((BINS, tokens), 0) == which * LEVELS + (LEVELS - 1) - level_row).astype(F32)


def route_kernel(slots, experts, routes_ref, prio_ref, pad_ref, hist_ref, info_ref, target_ref):
    tokens = routes_ref.shape[1]
    rows = routes_ref[...].astype(F32)
    prio = prio_ref[...]
    valid = (pad_ref[...] > 0).astype(F32)
    early = iota((tokens, tokens), 0) < iota((tokens, tokens), 1)
    hot = [(iota((experts, tokens), 0) == rows[k : k + 1].astype(jnp.int32)).astype(F32) for k in (0, 1)]
    count = dot((hot[0] + hot[1]).astype(BF16), early.astype(BF16))
    hist = jnp.zeros((experts, BINS), F32)
    sides = jnp.where(iota((8, tokens), 0) == 2, prio.astype(F32), valid)
    for k in (0, 1):
        sides = jnp.where(iota((8, tokens), 0) == k, rows[k : k + 1], sides)
    eye = (iota((8, 8), 0) == iota((8, 8), 1)).astype(F32)
    cols = dot(sides, eye, 0, 0)
    prio_col = cols[:, 2:3]
    valid_col = cols[:, 3:4]
    for k in (0, 1):
        slot = jnp.sum(hot[k] * count, axis=0, keepdims=True)
        info_ref[k : k + 1, :] = rows[k : k + 1]
        info_ref[2 + k : 3 + k, :] = rows[k : k + 1] * slots + slot
        hist = hist + dot(hot[k] * valid, class_rows(prio, k, tokens), 1, 1)
        code_row = rows[k : k + 1] * LEVELS + prio.astype(F32)
        code_col = jnp.where(valid_col > 0, cols[:, k : k + 1] * LEVELS + prio_col, -1.0)
        same = (code_col == code_row) & early
        info_ref[4 + k : 5 + k, :] = jnp.sum(same.astype(F32), axis=0, keepdims=True)
    info_ref[6:7, :] = prio.astype(F32)
    info_ref[7:8, :] = valid
    target_ref[...] = jnp.full(target_ref.shape, -1, jnp.int32)
    target_ref[0:2, :] = info_ref[2:4, :].astype(jnp.int32)
    hist_ref[...] = jnp.broadcast_to(hist.astype(jnp.int32)[None], hist_ref.shape)


def slot_hot(target_rows, expert, slots, tokens):
    place = iota((slots, tokens), 0) + expert * slots
    return ((place == target_rows[0:1]) | (place == target_rows[1:2])).astype(F32).astype(BF16)


def spread_kernel(slots, spot_ref, target_ref, rows_ref, *out_refs):
    tokens = target_ref.shape[1]
    for j, out_ref in enumerate(out_refs):
        hot = slot_hot(target_ref[0:2, :], spot_ref[0] ^ j, slots, tokens)
        out_ref[...] = dot(hot, rows_ref[:tokens, :]).astype(BF16)


def spread_joint_kernel(slots, spot_ref, x_ref, g_ref, out_ref, kept_ref):
    expert, tokens = spot_ref[3] + pl.program_id(0), g_ref.shape[0]

    @pl.when(pl.program_id(0) == 0)
    def _():
        codes = x_ref[tokens:, :tokens].astype(F32).astype(jnp.int32)
        kept_ref[...] = jnp.full(kept_ref.shape, -1, jnp.int32)
        for k in (0, 1):
            kept_ref[k : k + 1, :] = codes[2 * k : 2 * k + 1] * 64 + codes[2 * k + 1 : 2 * k + 2] - 1

    hot = slot_hot(kept_ref[0:2, :], expert, slots, tokens)
    out_ref[0, :slots] = dot(hot, x_ref[:tokens, :]).astype(BF16)
    out_ref[0, slots:] = dot(hot, g_ref[...]).astype(BF16)


def hidden_kernel(
    capacity, me_ref, hist_ref, info_ref, target_ref, tok_ref, mix_ref, wo_ref, gm_ref,
    hidden_ref, cross_ref, kept_ref,
):
    devices, experts, bins = hist_ref.shape
    tokens = info_ref.shape[1]
    hidden = tok_ref[...].astype(F32) + dot(mix_ref[...], wo_ref[...])
    hidden_ref[...] = hidden
    unit, _ = norm_parts(hidden)
    cross_ref[:tokens, :] = (unit * gm_ref[...]).astype(BF16)

    def add(j, sums):
        block = hist_ref[j].astype(F32)
        lower = (j < me_ref[0]).astype(F32)
        return sums[0] + block, sums[1] + block * lower

    zero = jnp.zeros((experts, bins), F32)
    totals, before = lax.fori_loop(0, devices, add, (zero, zero))
    early = (iota((bins, bins), 0) < iota((bins, bins), 1)).astype(F32)
    exact = lax.Precision.HIGHEST
    base = dot(totals, early, precision=exact) + before
    prio = info_ref[6:7, :].astype(jnp.int32)
    valid = info_ref[7:8, :] > 0
    kept_ref[...] = jnp.full(kept_ref.shape, -1, jnp.int32)
    codes = jnp.zeros((16, tokens), jnp.int32)
    row = iota((16, tokens), 0)
    for k in (0, 1):
        hot = (iota((experts, tokens), 0) == info_ref[k : k + 1, :].astype(jnp.int32)).astype(F32)
        spot = dot(base, class_rows(prio, k, tokens), precision=exact)
        rank = jnp.sum(hot * spot, axis=0, keepdims=True) + info_ref[4 + k : 5 + k, :]
        kept = valid & (rank < capacity - 0.5)
        place = jnp.where(kept, target_ref[k : k + 1, :], -1)
        kept_ref[k : k + 1, :] = place
        codes = jnp.where(row == 2 * k, (place + 1) >> 6, codes)
        codes = jnp.where(row == 2 * k + 1, (place + 1) & 63, codes)
    cross_ref[tokens:, :] = jnp.zeros((16, cross_ref.shape[1]), BF16)
    cross_ref[tokens:, :tokens] = codes.astype(F32).astype(BF16)


def project_kernel(tok_ref, ga_ref, wqkv_ref, normed_ref, proj_ref):
    unit, _ = norm_parts(tok_ref[...].astype(F32))
    normed = (unit * ga_ref[...]).astype(BF16)
    normed_ref[...] = normed
    features = tok_ref.shape[1]
    for part in range(3):
        at = slice(part * features, (part + 1) * features)
        proj_ref[:, at] = dot(normed, wqkv_ref[:, at]).astype(BF16)


def attend_kernel(query_ref, keys_ref, value_ref, seg_ref, pad_ref, mix_ref, prob_ref, bias_ref):
    step = pl.program_id(0)
    tokens = query_ref.shape[0]

    @pl.when(step == 0)
    def _():
        seg = seg_ref[...].astype(F32)
        eye = (iota((8, 8), 0) == iota((8, 8), 1)).astype(F32)
        seg_col = dot(jnp.broadcast_to(seg, (8, tokens)), eye, 0, 0)[:, 0:1]
        own = iota((tokens, tokens), 0) == iota((tokens, tokens), 1)
        allowed = (seg_col == seg) & ((pad_ref[...] > 0) | own)
        bias_ref[...] = jnp.where(allowed, 0.0, -1e30)

    query, keys, value = query_ref[...], keys_ref[...], value_ref[...]
    first = iota((tokens, 128), 1) < HEAD_DIM
    mixed = []
    for h in (0, 1):
        mine = first if h == 0 else ~first
        own_query = jnp.where(mine, query.astype(F32) * HEAD_DIM ** (-0.5), 0.0).astype(BF16)
        scores = dot(own_query, keys, 1, 1) + bias_ref[...]
        top = jnp.max(scores, axis=-1, keepdims=True)
        exponent = jnp.exp(scores - top)
        total = jnp.sum(exponent, axis=-1, keepdims=True)
        prob = (exponent * (1.0 / total)).astype(BF16)
        prob_ref[h] = prob
        mixed.append(dot(prob, value))
    mix_ref[...] = jnp.where(first, mixed[0], mixed[1]).astype(BF16)


def gather_rows(spot_ref, kept_ref, rows_refs):
    slots, features = rows_refs[0].shape
    tokens = kept_ref.shape[1]
    total = jnp.zeros((tokens, features), F32)
    for j, rows_ref in enumerate(rows_refs):
        hot = slot_hot(kept_ref[0:2, :], spot_ref[0] ^ j, slots, tokens)
        total = total + dot(hot, rows_ref[...], 0, 0)
    return total


def near_kernel(spot_ref, kept_ref, hidden_ref, *refs):
    d_ref, block_ref = refs[-2:]
    slots, tokens = refs[0].shape[0] // 2, kept_ref.shape[1]
    d_total = jnp.zeros(d_ref.shape, F32)
    y_total = hidden_ref[...]
    for j, rows_ref in enumerate(refs[:-2]):
        hot = slot_hot(kept_ref[0:2, :], spot_ref[0] ^ j, slots, tokens)
        d_total = d_total + dot(hot, rows_ref[:slots, :], 0, 0)
        y_total = y_total + dot(hot, rows_ref[slots:, :], 0, 0)
    d_ref[...] = d_total
    block_ref[...] = y_total


def gather_pass_kernel(group, spot_ref, kept_ref, *refs):
    refs[2 * group][...] = gather_rows(spot_ref, kept_ref, refs[:group]).astype(BF16)


def gather_kernel(spot_ref, kept_ref, *refs):
    refs[-1][...] = gather_rows(spot_ref, kept_ref, refs[:-1]).astype(BF16)


def block_kernel(block_ref, far_ref, out_ref):
    out_ref[...] = (block_ref[...] + far_ref[...].astype(F32)).astype(BF16)


def weight_grad_kernel(rows_ref, grad_ref, *refs):
    refs[-1][0] = dot(rows_ref[...], grad_ref[...], 0, 0).astype(BF16)


def widen_kernel(both_ref, in_ref, out_ref):
    in_ref[...] = both_ref[0].astype(F32).T
    out_ref[...] = both_ref[1].astype(F32)


def halves_by(bit, value):
    rows = value.shape[0] // 2
    low, high = value[:rows], value[rows:]
    return jnp.where(bit > 0, high, low), jnp.where(bit > 0, low, high)


def as_column(row, column):
    at = (iota((8, 128), 1) == column) & (iota((8, 128), 0) == 0)
    return dot(jnp.broadcast_to(row, (8, row.shape[1])), at.astype(F32), 0, 0, lax.Precision.HIGHEST)


def hidden_back_kernel(
    spot_ref, near_ref, far_ref, hidden_ref, cot_ref, gm_ref, wo_ref, mix_ref, gwra_ref, gwrb_ref, _,
    dhid_ref, dmix_ref, keep_ref, give_ref, __,
):
    features = hidden_ref.shape[1]
    bit = spot_ref[1]
    grad = near_ref[...] + far_ref[...].astype(F32)
    unit, scale = norm_parts(hidden_ref[...])
    gain = jnp.sum(grad * unit, axis=0, keepdims=True)
    dhid = cot_ref[...].astype(F32) + norm_back(unit, scale, grad * gm_ref[...])
    dhid_ref[...] = dhid
    branch = dhid.astype(BF16)
    keep, give = halves_by(bit, dot(mix_ref[...], branch, 0, 0))
    keep_ref[:, :features], give_ref[:, :features] = keep.astype(BF16), give.astype(BF16)
    dmix_ref[...] = dot(branch, wo_ref[...], 1, 1).astype(BF16)
    experts = gwra_ref.shape[1]
    wide = (iota((experts, 128), 0) == iota((experts, 128), 1)).astype(F32)
    side = dot(gwra_ref[...] + gwrb_ref[...], wide, precision=lax.Precision.HIGHEST)
    side = side + as_column(gain, experts)
    keep, give = halves_by(bit, side)
    keep_ref[:, features:], give_ref[:, features:] = keep.astype(BF16), give.astype(BF16)


def head_pair_back(offset, dmix_ref, proj_ref, mix_ref, prob_ref, dproj_ref):
    step = pl.program_id(0)
    tokens, features = mix_ref.shape
    width = dproj_ref.shape[1] // 3
    at = lambda part: pl.ds(pl.multiple_of(part * features + (step + offset) * 128, 128), 128)
    query, keys, value = proj_ref[:, at(0)], proj_ref[:, at(1)], proj_ref[:, at(2)]
    dmix = dmix_ref[:, at(0)]
    product = dmix.astype(F32) * mix_ref[:, at(0)].astype(F32)
    first = iota((tokens, 128), 1) < HEAD_DIM
    parts = []
    for h in (0, 1):
        mine = first if h == 0 else ~first
        own_dmix = jnp.where(mine, dmix.astype(F32), 0.0).astype(BF16)
        delta = jnp.sum(jnp.where(mine, product, 0.0), axis=-1, keepdims=True)
        prob = prob_ref[h]
        dprob = dot(own_dmix, value, 1, 1)
        dscore = (prob.astype(F32) * (dprob - delta) * HEAD_DIM ** (-0.5)).astype(BF16)
        parts.append((dot(dscore, keys), dot(dscore, query, 0, 0), dot(prob, dmix, 0, 0)))
    for part in range(3):
        to = pl.ds(pl.multiple_of(part * width + step * 128, 128), 128)
        dproj_ref[:, to] = jnp.where(first, parts[0][part], parts[1][part]).astype(BF16)


def first_heads_kernel(
    spot_ref, dmix_ref, normed_ref, proj_ref, mix_ref, prob_ref, keep_ref, give_ref, dproj_ref,
):
    head_pair_back(0, dmix_ref, proj_ref, mix_ref, prob_ref, dproj_ref)

    @pl.when(pl.program_id(0) == pl.num_programs(0) - 1)
    def _():
        keep, give = halves_by(spot_ref[1], dot(normed_ref[...], dproj_ref[...], 0, 0))
        keep_ref[...], give_ref[...] = keep.astype(BF16), give.astype(BF16)


def last_heads_kernel(
    spot_ref, dmix_ref, normed_ref, proj_ref, mix_ref, prob_ref, keep_ref, give_ref, dproj_ref,
):
    head_pair_back(pl.num_programs(0), dmix_ref, proj_ref, mix_ref, prob_ref, dproj_ref)

    @pl.when(pl.program_id(0) == pl.num_programs(0) - 1)
    def _():
        keep, give = halves_by(spot_ref[1], dot(normed_ref[...], dproj_ref[...], 0, 0))
        keep_ref[...], give_ref[...] = keep.astype(BF16), give.astype(BF16)


def token_grad_kernel(first_ref, last_ref, dhid_ref, tok_ref, ga_ref, wqkv_ref, gtok_ref):
    tokens, features = tok_ref.shape
    grad = jnp.zeros((tokens, features), F32)
    half = features // 2
    for part in range(3):
        at = slice(part * half, (part + 1) * half)
        for place, ref in ((0, first_ref), (1, last_ref)):
            start = part * features + place * half
            grad = grad + dot(ref[:, at], wqkv_ref[:, start : start + half], 1, 1)
    unit, scale = norm_parts(tok_ref[...].astype(F32))
    gtok_ref[...] = dhid_ref[...] + norm_back(unit, scale, grad * ga_ref[...])


def take(refs, count):
    return refs[:count], refs[count:]


def expert_kernel(pieces, group, near, *refs):
    step = pl.program_id(0)
    (spot_ref, wr_ref, own_ref, win_ref, wout_ref), refs = take(refs, 5)
    mine = (spot_ref[0] - spot_ref[3]) ^ step
    if near:
        x_refs, refs = take(refs, group)
        g_refs, refs = take(refs, group)
        back_refs, refs = take(refs, group)
    else:
        (far_ref,), refs = take(refs, 1)
        refs = refs[4:]
        dx_refs, refs = take(refs, group)
        y_refs, refs = take(refs, group)
    gwr_ref, dexp_ref, xcopy_ref, act_ref, dpre_ref, now_ref = refs
    slots = dexp_ref.shape[0]
    if near:
        for j in range(group):

            @pl.when(step == j)
            def _():
                xcopy_ref[...] = x_refs[j][...]
                now_ref[...] = g_refs[j][...]

    else:
        xcopy_ref[...] = far_ref[mine, :slots, :]
        now_ref[...] = far_ref[mine, slots:, :]

    x = xcopy_ref[...]
    g = now_ref[...].astype(F32)
    logits = dot(x, wr_ref[...])
    exponent = jnp.exp(logits - jnp.max(logits, axis=-1, keepdims=True))
    router = exponent / jnp.sum(exponent, axis=-1, keepdims=True)
    gate = jnp.sum(router * own_ref[...], axis=-1, keepdims=True)
    dexp = (gate * g).astype(BF16)
    dexp_ref[...] = dexp
    out = jnp.zeros(x.shape, F32)
    dx = jnp.zeros(x.shape, F32)
    width = win_ref.shape[1] // pieces
    for r in range(pieces):
        at = slice(r * width, (r + 1) * width)
        pre = dot(x, win_ref[:, at])
        square = pre * pre
        bend = jnp.tanh(pre * (0.7978845608028654 + 0.035677408136300125 * square))
        half = 0.5 + 0.5 * bend
        smooth = pre * half
        slope = half + smooth * (1.0 - half) * (1.5957691216057308 + 0.21406444881780075 * square)
        active = smooth.astype(BF16)
        act_ref[:, at] = active
        dpreact = (dot(dexp, wout_ref[at, :], 1, 1) * slope).astype(BF16)
        dpre_ref[:, at] = dpreact
        out = out + dot(active, wout_ref[at, :])
        dx = dx + dot(dpreact, win_ref[:, at], 1, 1)
    out = out.astype(BF16).astype(F32)
    y = (gate * out).astype(BF16)
    dgate = jnp.sum(g * out, axis=-1, keepdims=True)
    dlogits = (dgate * gate * (own_ref[...] - router)).astype(BF16)
    dx = (dx + dot(dlogits, wr_ref[...], 1, 1)).astype(BF16)
    if near:
        for j in range(group):

            @pl.when(step == j)
            def _():
                back_refs[j][:slots, :] = dx
                back_refs[j][slots:, :] = y

    else:
        for j in range(group):

            @pl.when(step == j)
            def _():
                y_refs[j][...] = y
                dx_refs[j][...] = dx

    @pl.when(step == 0)
    def _():
        gwr_ref[...] = jnp.zeros(gwr_ref.shape, F32)

    gwr_ref[...] += dot(x, dlogits, 0, 0)


def swap(value, axis, bit):
    size = lax.axis_size(axis)
    return lax.ppermute(value, axis, [(i, i ^ bit) for i in range(size)])


def bits_of(axis):
    size = lax.axis_size(axis)
    return [1 << b for b in range(size.bit_length() - 1)]


def deal_plane_kernel(spot_ref, *refs):
    in_refs, (own_ref, *out_refs, total_ref) = refs[:-5], refs[-5:]
    start = 0
    for keep_ref, other_ref in zip(in_refs[::2], in_refs[1::2]):
        total = keep_ref[...].astype(F32) + other_ref[...].astype(F32)
        rows, columns = total.shape
        total_ref[:, :, start : start + columns] = total.reshape(4, rows // 4, columns)
        start += columns
    spot = spot_ref[2] * 2 + spot_ref[4]
    own_ref[...] = total_ref[spot]
    for j, out_ref in enumerate(out_refs):
        out_ref[...] = total_ref[spot ^ (j + 1)].astype(BF16)


def deal_line_kernel(groups, spot_ref, own_ref, *refs):
    in_refs, (first_ref, *out_refs, total_ref) = refs[:3], refs[3:]
    total = own_ref[...]
    for ref in in_refs:
        total = total + ref[...].astype(F32)
    rows, columns = total.shape
    total_ref[...] = total.reshape(groups, rows // groups, columns)
    first_ref[...] = total_ref[spot_ref[5]]
    for j, out_ref in enumerate(out_refs):
        out_ref[...] = total_ref[spot_ref[5] ^ (j + 1)].astype(BF16)


def pile_kernel(own_ref, *refs):
    total = own_ref[...]
    for ref in refs[:-1]:
        total = total + ref[...].astype(F32)
    refs[-1][...] = total.astype(BF16)


def line_up_kernel(spot_ref, *refs):
    out_ref, total_ref = refs[-2:]
    for j, ref in enumerate(refs[:-2]):
        total_ref[spot_ref[5] ^ j] = ref[...].astype(F32)
    out_ref[...] = total_ref[...].reshape(out_ref.shape).astype(BF16)


def line_up_plane_kernel(spot_ref, *refs):
    out_ref, total_ref = refs[-2:]
    for j, ref in enumerate(refs[:-2]):
        total_ref[(spot_ref[2] * 2 + spot_ref[4]) ^ j] = ref[...]
    out_ref[...] = total_ref[...].reshape(out_ref.shape)


def finish_kernel(
    experts, spot_ref, wqkv_ref, ga_ref, a0, a1, o0, o1, s0, s1, b0, b1,
    grad_o_ref, grad_qkv_ref, gain_attn_ref, gain_moe_ref, router_ref, total_ref, side_ref,
):
    step = pl.program_id(0)
    rows, half = a0.shape
    for k, (a_ref, o_ref, s_ref, b_ref) in enumerate(((a0, o0, s0, b0), (a1, o1, s1, b1))):
        at = pl.ds(pl.multiple_of((spot_ref[1] ^ k) * rows, 8), rows)
        grad_qkv_ref[at, :half] = a_ref[...].astype(F32)
        grad_qkv_ref[at, half:] = b_ref[...].astype(F32)

        @pl.when(step < 2)
        def _():
            grad_o_ref[at, :] = o_ref[...].astype(F32)

        @pl.when(step == 0)
        def _():
            side_ref[at, :] = s_ref[...].astype(F32)

    part = jnp.sum(wqkv_ref[...].astype(F32) * grad_qkv_ref[...], axis=-1, keepdims=True)
    part = jnp.broadcast_to(part, total_ref.shape)

    @pl.when(step == 0)
    def _():
        total_ref[...] = part

    @pl.when(step > 0)
    def _():
        total_ref[...] += part

    @pl.when(step == 2)
    def _():
        side = side_ref[...].T
        router_ref[...] = side[:experts, :]
        gain_moe_ref[...] = side[experts : experts + 1, :].reshape(gain_moe_ref.shape)
        gain_attn_ref[...] = (total_ref[...].T[0:1, :] / ga_ref[...]).reshape(gain_attn_ref.shape)


def plane_swap(value, j):
    groups = lax.axis_size("expert")
    size = lax.axis_size("dp") * groups
    apart = (j >> 1) * 2 * groups + (j & 1)
    return lax.ppermute(value, ("dp", "expert"), [(i, i ^ apart) for i in range(size)])


def plane_deal(spot, halves, *after):
    scalar = pl.BlockSpec(memory_space=pltpu.SMEM)
    ins = [v for pair in halves for v in pair]
    rows, columns = halves[0][0].shape[0] // 4, sum(pair[0].shape[1] for pair in halves)
    piece = (rows, columns)
    return call(
        deal_plane_kernel, (1,), (spot, *ins), [scalar] + [whole(v.shape) for v in ins],
        [shape_of(piece, F32)] + [shape_of(piece, BF16)] * 3, [whole_out(piece)] * 4,
        [pltpu.VMEM((4, *piece), F32)],
        after=after,
    )


def line_deal(spot, dealt, groups, us, *after, ready=False):
    scalar = pl.BlockSpec(memory_space=pltpu.SMEM)
    own, *out = dealt
    rows, columns = own.shape
    piece = (rows // groups, columns)
    arrived = out if ready else [plane_swap(v, j + 1) for j, v in enumerate(out)]
    scratch = [pltpu.VMEM((groups, *piece), F32)]
    own, *out = call(
        functools.partial(deal_line_kernel, groups), (1,), (spot, own, *arrived),
        [scalar] + [whole((rows, columns))] * 4,
        (shape_of(piece, F32), *[shape_of(piece, BF16)] * (groups - 1)),
        (whole_out(piece),) * groups,
        scratch,
        us=us,
        after=after,
    )
    return [own] + [swap(v, "expert", 2 * (j + 1)) for j, v in enumerate(out)]


def line_up(spot, parts, *late_pile, waits=()):
    scalar = pl.BlockSpec(memory_space=pltpu.SMEM)
    groups, piece = len(parts), parts[0].shape
    rows, columns = groups * piece[0], piece[1]
    scratch = [pltpu.VMEM((groups, *piece), F32)]
    total = call(
        pile_kernel, (1,), parts, [whole(piece)] * groups, shape_of(piece, BF16), whole_out(piece),
        after=late_pile,
    )
    own = call(
        line_up_kernel, (1,), (spot, total, *[swap(total, "expert", 2 * j) for j in range(1, groups)]),
        [scalar] + [whole(piece)] * groups,
        shape_of((rows, columns), BF16), whole_out((rows, columns)), scratch,
        after=waits,
    )
    return own, [plane_swap(own, j) for j in (1, 2, 3)]


def line_up_plane(spot, own, arrived, *after):
    scalar = pl.BlockSpec(memory_space=pltpu.SMEM)
    rows, columns = own.shape
    half = (4 * rows, columns)
    own = call(
        line_up_plane_kernel, (1,), (spot, own, *arrived),
        [scalar] + [whole((rows, columns))] * 4,
        shape_of(half, BF16), whole_out(half), [pltpu.VMEM((4, rows, columns), BF16)],
        after=after,
    )
    return [own, swap(own, "dp", 1)]


def all_sum(value, steps):
    rows = value.shape[0]
    place = []
    for axis, bit in steps:
        half = value.shape[0] // 2
        mine = ((lax.axis_index(axis) & bit) > 0).astype(jnp.int32)
        keep = lax.dynamic_slice_in_dim(value, mine * half, half, 0)
        give = lax.dynamic_slice_in_dim(value, (1 - mine) * half, half, 0)
        value = (keep.astype(F32) + swap(give, axis, bit).astype(F32)).astype(BF16)
        place.append(mine)
    for (axis, bit), mine in zip(reversed(steps), reversed(place)):
        other = swap(value, axis, bit)
        low = jnp.where(mine > 0, other, value)
        high = jnp.where(mine > 0, value, other)
        value = jnp.concatenate([low, high], axis=0)
    return value


def local(
    tokens, segment_ids, pad_mask, routes, priority, gain_attn, w_qkv, w_o, gain_moe, w_router,
    w_in, w_out, cotangent,
):
    sequences, length, features = tokens.shape
    count = sequences * length
    experts = w_router.shape[1]
    groups = lax.axis_size("expert")
    replicas = lax.axis_size("dp")
    devices = groups * replicas
    group = groups // 2
    most = 4 * count // experts
    slots = -(-most // 16) * 16
    capacity = (42 * count * devices + 20 * experts - 1) // (20 * experts)
    me = lax.axis_index(("dp", "expert")).astype(jnp.int32).reshape(1)
    replica = lax.axis_index("dp")
    column = lax.axis_index("expert")
    spot = jnp.stack(
        [column, replica & 1, replica >> 1 & 1, column // group * group, column & 1, column >> 1]
    ).astype(jnp.int32)
    tok = tokens.reshape(count, features)
    cot = cotangent.reshape(count, features)
    ga = gain_attn.reshape(1, features)
    gm = gain_moe.reshape(1, features)
    full = (count, features)
    scalar = pl.BlockSpec(memory_space=pltpu.SMEM)
    sent = shape_of((slots, features), BF16)

    def across(value):
        return swap(value, "expert", group)

    def among(values):
        return [v if j == 0 else swap(v, "expert", j) for j, v in enumerate(values)]

    halves = [list(range(group)), list(range(group, groups))]
    joint = (group, 2 * slots, features)

    def half_exchange(value):
        return lax.all_to_all(value, "expert", 0, 0, axis_index_groups=halves, tiled=True)

    far_cot = across(cot)
    full_in = lax.all_gather(w_in[0], "dp", axis=1, tiled=True)
    full_out = lax.all_gather(w_out[0], "dp", axis=0, tiled=True)

    pairs = features // 128
    tile = lambda dtype: shape_of((count, features), dtype)
    prob_block = pl.BlockSpec((2, count, count), lambda i: (i, 0, 0))
    hist_shape = (devices, experts, BINS)
    hist, info, target = call(
        functools.partial(route_kernel, slots, experts),
        (1,),
        (routes.reshape(count, 2).T, priority.reshape(1, count), pad_mask.reshape(1, count)),
        [whole((2, count)), whole((1, count)), whole((1, count))],
        (shape_of(hist_shape, jnp.int32), shape_of((8, count), F32), shape_of((8, count), jnp.int32)),
        (whole_out(hist_shape), whole_out((8, count)), whole_out((8, count))),
        limit=LIMIT,
    )
    def spread(target, rows, us, *after):
        return call(
            functools.partial(spread_kernel, slots),
            (1,),
            (spot, target, rows),
            [scalar, whole((8, count)), whole(rows.shape)],
            [sent] * group,
            [whole_out((slots, features))] * group,
            us=us,
            after=after,
        limit=LIMIT,
        )

    near_g_sent = spread(target, cot, 1)
    near_g = among(near_g_sent)
    every = lax.all_to_all(hist, ("dp", "expert"), 0, 0, tiled=True)
    normed, proj = call(
        project_kernel,
        (1,),
        (tok, ga, w_qkv),
        [whole(full), whole((1, features)), whole(w_qkv.shape)],
        (tile(BF16), shape_of((count, 3 * features), BF16)),
        (whole_out(full), whole_out((count, 3 * features))),
        after=(near_g_sent[0],),
        limit=LIMIT,
    )
    lanes = lambda part: pl.BlockSpec((count, 128), lambda i: (0, part * pairs + i))
    mix, prob = call(
        attend_kernel,
        (pairs,),
        (proj, proj, proj, segment_ids.reshape(1, count), pad_mask.reshape(1, count)),
        [lanes(0), lanes(1), lanes(2), whole((1, count)), whole((1, count))],
        (tile(BF16), shape_of((HEADS, count, count), BF16)),
        (lanes(0), prob_block),
        [pltpu.VMEM((count, count), F32)],
        us=20000,
        after=(target,),
        limit=LIMIT,
    )
    cross_shape = (count + 16, features)
    hidden, cross, kept = call(
        functools.partial(hidden_kernel, capacity),
        (1,),
        (me, every, info, target, tok, mix, w_o, gm),
        [scalar, whole(hist_shape), whole((8, count)), whole((8, count)), whole(full), whole(full), whole(w_o.shape), whole((1, features))],
        (tile(F32), shape_of(cross_shape, BF16), shape_of((8, count), jnp.int32)),
        (whole_out(full), whole_out(cross_shape), whole_out((8, count))),
        limit=LIMIT,
    )
    far_x = across(cross)
    near_sent = spread(kept, cross, 20000, *near_g)
    near_x = among(near_sent)
    far_sent, far_kept = call(
        functools.partial(spread_joint_kernel, slots),
        (group,),
        (spot, far_x, far_cot),
        [scalar, whole(cross_shape), whole(full)],
        (shape_of(joint, BF16), shape_of((8, count), jnp.int32)),
        (pl.BlockSpec((1, 2 * slots, features), lambda e: (e, 0, 0)), whole_out((8, count))),
        after=(near_sent[0],),
        limit=LIMIT,
    )
    far_rows = half_exchange(far_sent)

    hidden_units = w_out.shape[1] * replicas
    own = (iota((1, experts), 1) == column).astype(F32)
    flat = group * slots
    slot_spec = whole_out((slots, features))
    weights = (spot, w_router, own, full_in, full_out)
    weight_specs = [scalar, whole(w_router.shape), whole((1, experts)), whole(full_in.shape), whole(full_out.shape)]
    tall = [shape_of((2 * flat, n), BF16) for n in (features, features, hidden_units, hidden_units)]
    tall_blocks = lambda first: [
        pl.BlockSpec((slots, v.shape[1]), lambda e: (first + e, 0)) for v in tall
    ]
    outs = call(
        functools.partial(expert_kernel, 4, group, True),
        (group,),
        (*weights, *near_x, *near_g),
        weight_specs + [whole((slots, features))] * (2 * group),
        (*[shape_of((2 * slots, features), BF16)] * group, shape_of(w_router.shape, F32), *tall),
        (*[whole_out((2 * slots, features))] * group, whole_out(w_router.shape), *tall_blocks(0)),
        [pltpu.VMEM((slots, features), BF16)],
        us=300000,
        after=(far_sent,),
        limit=LIMIT,
    )
    near_back, outs = take(outs, group)
    near_back = among(near_back)
    gwr_a, kept_rows = outs[0], outs[1:]
    outs = call(
        functools.partial(expert_kernel, 4, group, False),
        (group,),
        (*weights, far_rows, *kept_rows),
        weight_specs + [whole(joint)] + [pl.BlockSpec(memory_space=pl.ANY)] * 4,
        (*[sent] * (2 * group), shape_of(w_router.shape, F32), *tall),
        (*[slot_spec] * (2 * group), whole_out(w_router.shape), *tall_blocks(group)),
        [pltpu.VMEM((slots, features), BF16)],
        after=(gwr_a,),
        alias=[(6 + i, 2 * group + 1 + i) for i in range(4)],
        limit=LIMIT,
    )
    d_far, outs = take(outs, group)
    y_far, outs = take(outs, group)
    gwr_b, all_dexp, all_x, all_act, all_dpre = outs
    d_far = among(d_far)
    def gather(rows, *after):
        return call(
            gather_kernel,
            (1,),
            (spot, far_kept, *rows),
            [scalar, whole((8, count))] + [whole((slots, features))] * group,
            tile(BF16),
            whole_out(full),
            after=after,
        )

    anywhere = pl.BlockSpec(memory_space=pl.ANY)
    part = hidden_units // 4
    both_shape = shape_of((2, hidden_units, features), BF16)

    def weight_grad(which, rows, grad, us, after, *given):
        return call(
            weight_grad_kernel,
            (4,),
            (rows, grad, *given),
            [pl.BlockSpec((2 * flat, part), lambda i: (0, i)), whole((2 * flat, features))] + [anywhere] * len(given),
            both_shape,
            pl.BlockSpec((1, part, features), lambda i: (which, i, 0)),
            us=us,
            after=after,
            alias=[(2, 0)] if given else (),
        )

    both = weight_grad(1, all_act, all_dexp, 1, near_back)
    d_far, *y_far = call(
        functools.partial(gather_pass_kernel, group),
        (1,),
        (spot, far_kept, *d_far, *y_far),
        [scalar, whole((8, count))] + [whole((slots, features))] * group + [anywhere] * group,
        [tile(BF16)] + [sent] * group,
        [whole_out(full)] + [anywhere] * group,
        after=(both,),
        alias=[(2 + group + j, 1 + j) for j in range(group)],
    )
    y_far = among(y_far)
    both = weight_grad(0, all_dpre, all_x, 60000, (d_far,), both)
    near_d, block_part = call(
        near_kernel,
        (1,),
        (spot, kept, hidden, *near_back),
        [scalar, whole((8, count)), whole(full)] + [whole((2 * slots, features))] * group,
        (tile(F32), tile(F32)),
        (whole_out(full), whole_out(full)),
        after=(both,),
    )

    y_far = gather(y_far, near_d)
    d_far = across(d_far)
    both = lax.psum_scatter(both, "dp", scatter_dimension=1, tiled=True)

    o_half = (features // 2, features + 128)
    a_half = (features // 2, 3 * features // 2)
    dhid, dmix, keep_o, give_o, y_far = call(
        hidden_back_kernel,
        (1,),
        (spot, near_d, d_far, hidden, cot, gm, w_o, mix, gwr_a, gwr_b, y_far),
        [scalar] + [whole(full)] * 4 + [whole((1, features)), whole(w_o.shape), whole(full)] + [whole(gwr_a.shape)] * 2 + [anywhere],
        (tile(F32), tile(BF16), *[shape_of(o_half, BF16)] * 2, tile(BF16)),
        (whole_out(full), whole_out(full), *[whole_out(o_half)] * 2, anywhere),
        us=400000,
        alias=[(10, 4)],
    )
    y_far = across(y_far)
    some = 3 * features // 2
    head_specs = lambda offset: [scalar] + [whole(full)] * 2 + [whole((count, 3 * features)), whole(full)] + [
        pl.BlockSpec((2, count, count), lambda i: (i + offset, 0, 0))
    ]
    keep_a, give_a, dproj_a = call(
        first_heads_kernel,
        (pairs // 2,),
        (spot, dmix, normed, proj, mix, prob),
        head_specs(0),
        (shape_of(a_half, BF16), shape_of(a_half, BF16), shape_of((count, some), BF16)),
        (whole_out(a_half), whole_out(a_half), whole_out((count, some))),
        us=13000,
    )
    by_hand = replicas == 4 and groups == 8 and features % (8 * devices) == 0
    if by_hand:
        beside = lambda keep, give: (keep, swap(give, "dp", 1))
        early = plane_deal(spot, [beside(keep_a, give_a), beside(keep_o, give_o)])
    keep_b, give_b, dproj_b = call(
        last_heads_kernel,
        (pairs // 2,),
        (spot, dmix, normed, proj, mix, prob),
        head_specs(pairs // 2),
        (shape_of(a_half, BF16), shape_of(a_half, BF16), shape_of((count, some), BF16)),
        (whole_out(a_half), whole_out(a_half), whole_out((count, some))),
        us=50000,
        after=early[:1] if by_hand else (),
    )
    gtok = call(
        token_grad_kernel,
        (1,),
        (dproj_a, dproj_b, dhid, tok, ga, w_qkv),
        [whole((count, some))] * 2 + [whole(full)] * 2 + [whole((1, features)), whole(w_qkv.shape)],
        tile(F32),
        whole_out(full),
    )
    block_out = call(
        block_kernel,
        (1,),
        (block_part, y_far),
        [whole(full)] * 2,
        tile(BF16),
        whole_out(full),
        after=(gtok,),
    )
    shapes = [w_in.shape[1:], w_out.shape[1:]]
    gin, gout = call(
        widen_kernel,
        (1,),
        (both,),
        [whole(both.shape)],
        [shape_of(v, F32) for v in shapes],
        [whole_out(v) for v in shapes],
        after=(gtok,),
    )
    if by_hand:
        rows = groups // 2
        early = line_deal(spot, early, rows, 30000, gtok)
        late = plane_deal(spot, [beside(keep_b, give_b)], early[0], y_far)
        late = [late[0]] + [plane_swap(v, j + 1) for j, v in enumerate(late[1:])]
        early, early_parts = line_up(spot, early, late[0], waits=late[2:])
        late, late_parts = line_up(spot, line_deal(spot, late, rows, 1, early, ready=True))
        pieces = line_up_plane(spot, early, early_parts, late) + line_up_plane(
            spot, late, late_parts, gin, block_out
        )
        half = features // 2
        block = lambda width, index: [pl.BlockSpec((half, width), lambda i: (0, index(i)))] * 2
        third = lambda i: (0, i)
        grad_o, grad_qkv, gain_attn_grad, gain_moe_grad, grad_router = call(
            functools.partial(finish_kernel, experts),
            (3,),
            (spot, w_qkv, ga, *pieces[:2] * 3, *pieces[2:]),
            [scalar, pl.BlockSpec((features, features), third), whole((1, features))]
            + block(half, lambda i: i)
            + block(half, lambda i: jnp.minimum(3 + i, 4))
            + block(128, lambda i: 5 * half // 128)
            + block(half, lambda i: i),
            [shape_of(v, F32) for v in ((features, features), (features, 3 * features), (features,), (features,), (experts, features))],
            [
                pl.BlockSpec((features, half), lambda i: (0, jnp.minimum(i, 1))),
                pl.BlockSpec((features, features), third),
                whole_out((features,)),
                whole_out((features,)),
                whole_out((experts, features)),
            ],
            [pltpu.VMEM((features, 128), F32)] * 2,
        )
    else:
        low = (replica & 1) == 0

        def rejoin(keep, give):
            return jnp.concatenate([jnp.where(low, keep, give), jnp.where(low, give, keep)], axis=0)

        gain_steps = [("dp", b) for b in bits_of("dp")] + [("expert", b) for b in bits_of("expert")]
        both = all_sum(rejoin(keep_o, give_o), gain_steps).astype(F32)
        grad_o, side_o = both[:, :features], both[:, features:]
        first = all_sum(rejoin(keep_a, give_a), gain_steps).astype(F32)
        last = all_sum(rejoin(keep_b, give_b), gain_steps).astype(F32)
        half = features // 2
        cut = lambda part: slice(part * half, (part + 1) * half)
        grad_qkv = jnp.concatenate([v[:, cut(part)] for part in range(3) for v in (first, last)], axis=1)
        product = jnp.sum(w_qkv.astype(F32) * grad_qkv, axis=1)
        gain_attn_grad, gain_moe_grad = product / gain_attn, side_o[:, experts]
        grad_router = side_o[:, :experts].T
    return (
        block_out.reshape(sequences, length, features),
        gtok.reshape(sequences, length, features),
        gain_attn_grad.reshape(features),
        grad_qkv,
        grad_o,
        gain_moe_grad.reshape(features),
        grad_router.T,
        gin[None],
        gout[None],
    )


def solution(mesh):
    rows = P(("dp", "expert"), None, None)
    flat = P(("dp", "expert"), None)
    first = P("expert", None, "dp")
    second = P("expert", "dp", None)
    return jax.shard_map(
        local,
        mesh=mesh,
        in_specs=(rows, flat, flat, rows, flat, P(), P(), P(), P(), P(), first, second, rows),
        out_specs=(rows, rows, P(), P(), P(), P(), P(), first, second),
        check_vma=False,
    )
```

```python
import functools

import jax
import jax.numpy as jnp
from jax import lax
from jax.experimental import pallas as pl
from jax.experimental.pallas import tpu as pltpu
from jax.sharding import PartitionSpec as P

HEADS = 12
HEAD_DIM = 64
LEVELS = 64
BINS = 2 * LEVELS
LIMIT = 60 * 1024 * 1024
LATE = 44 * 1024 * 1024
F32 = jnp.float32
BF16 = jnp.bfloat16


def dot(a, b, ca=1, cb=0, precision=None):
    return lax.dot_general(
        a, b, (((ca,), (cb,)), ((), ())), precision=precision, preferred_element_type=F32
    )


def whole(shape):
    zeros = (0,) * len(shape)
    return pl.BlockSpec(shape, lambda *_: zeros, pipeline_mode=pl.Buffered(1))


def whole_out(shape):
    zeros = (0,) * len(shape)
    return pl.BlockSpec(shape, lambda *_: zeros)


def iota(shape, dim):
    return lax.broadcasted_iota(jnp.int32, shape, dim)


def call(kernel, grid, ins, in_specs, outs, out_specs, scratch=(), us=1, after=(), alias=(), limit=None):
    late = len(after)

    def body(*refs):
        kernel(*refs[late:])

    return pl.pallas_call(
        body,
        grid=grid,
        in_specs=[pl.BlockSpec(memory_space=pl.ANY)] * late + in_specs,
        out_specs=out_specs,
        out_shape=outs,
        scratch_shapes=list(scratch),
        input_output_aliases={late + i: o for i, o in alias},
        compiler_params=pltpu.CompilerParams(vmem_limit_bytes=limit or LATE),
        cost_estimate=pl.CostEstimate(flops=us * 10**6, bytes_accessed=0, transcendentals=0),
    )(*after, *ins)


def shape_of(shape, dtype):
    return jax.ShapeDtypeStruct(shape, dtype)


def norm_parts(values):
    center = values - jnp.mean(values, axis=-1, keepdims=True)
    spread = jnp.mean(center * center, axis=-1, keepdims=True)
    scale = lax.rsqrt(spread + 1e-06)
    return center * scale, scale


def norm_back(unit, scale, grad_unit):
    return scale * (
        grad_unit
        - jnp.mean(grad_unit, axis=-1, keepdims=True)
        - unit * jnp.mean(grad_unit * unit, axis=-1, keepdims=True)
    )


def class_rows(level_row, which, tokens):
    return (iota((BINS, tokens), 0) == which * LEVELS + (LEVELS - 1) - level_row).astype(F32)


def route_kernel(slots, experts, routes_ref, prio_ref, pad_ref, hist_ref, info_ref, target_ref):
    tokens = routes_ref.shape[1]
    rows = routes_ref[...].astype(F32)
    prio = prio_ref[...]
    valid = (pad_ref[...] > 0).astype(F32)
    early = iota((tokens, tokens), 0) < iota((tokens, tokens), 1)
    hot = [(iota((experts, tokens), 0) == rows[k : k + 1].astype(jnp.int32)).astype(F32) for k in (0, 1)]
    count = dot((hot[0] + hot[1]).astype(BF16), early.astype(BF16))
    hist = jnp.zeros((experts, BINS), F32)
    sides = jnp.where(iota((8, tokens), 0) == 2, prio.astype(F32), valid)
    for k in (0, 1):
        sides = jnp.where(iota((8, tokens), 0) == k, rows[k : k + 1], sides)
    eye = (iota((8, 8), 0) == iota((8, 8), 1)).astype(F32)
    cols = dot(sides, eye, 0, 0)
    prio_col = cols[:, 2:3]
    valid_col = cols[:, 3:4]
    for k in (0, 1):
        slot = jnp.sum(hot[k] * count, axis=0, keepdims=True)
        info_ref[k : k + 1, :] = rows[k : k + 1]
        info_ref[2 + k : 3 + k, :] = rows[k : k + 1] * slots + slot
        hist = hist + dot(hot[k] * valid, class_rows(prio, k, tokens), 1, 1)
        code_row = rows[k : k + 1] * LEVELS + prio.astype(F32)
        code_col = jnp.where(valid_col > 0, cols[:, k : k + 1] * LEVELS + prio_col, -1.0)
        same = (code_col == code_row) & early
        info_ref[4 + k : 5 + k, :] = jnp.sum(same.astype(F32), axis=0, keepdims=True)
    info_ref[6:7, :] = prio.astype(F32)
    info_ref[7:8, :] = valid
    target_ref[...] = jnp.full(target_ref.shape, -1, jnp.int32)
    target_ref[0:2, :] = info_ref[2:4, :].astype(jnp.int32)
    hist_ref[...] = jnp.broadcast_to(hist.astype(jnp.int32)[None], hist_ref.shape)


def slot_hot(target_rows, expert, slots, tokens):
    place = iota((slots, tokens), 0) + expert * slots
    return ((place == target_rows[0:1]) | (place == target_rows[1:2])).astype(F32).astype(BF16)


def spread_kernel(slots, spot_ref, target_ref, rows_ref, *out_refs):
    tokens = target_ref.shape[1]
    for j, out_ref in enumerate(out_refs):
        hot = slot_hot(target_ref[0:2, :], spot_ref[0] ^ j, slots, tokens)
        out_ref[...] = dot(hot, rows_ref[:tokens, :]).astype(BF16)


def spread_joint_kernel(slots, spot_ref, x_ref, g_ref, out_ref, kept_ref):
    expert, tokens = spot_ref[3] + pl.program_id(0), g_ref.shape[0]

    @pl.when(pl.program_id(0) == 0)
    def _():
        codes = x_ref[tokens:, :tokens].astype(F32).astype(jnp.int32)
        kept_ref[...] = jnp.full(kept_ref.shape, -1, jnp.int32)
        for k in (0, 1):
            kept_ref[k : k + 1, :] = codes[2 * k : 2 * k + 1] * 64 + codes[2 * k + 1 : 2 * k + 2] - 1

    hot = slot_hot(kept_ref[0:2, :], expert, slots, tokens)
    out_ref[0, :slots] = dot(hot, x_ref[:tokens, :]).astype(BF16)
    out_ref[0, slots:] = dot(hot, g_ref[...]).astype(BF16)


def hidden_kernel(
    capacity, me_ref, hist_ref, info_ref, target_ref, tok_ref, mix_ref, wo_ref, gm_ref,
    hidden_ref, cross_ref, kept_ref,
):
    devices, experts, bins = hist_ref.shape
    tokens = info_ref.shape[1]
    hidden = tok_ref[...].astype(F32) + dot(mix_ref[...], wo_ref[...])
    hidden_ref[...] = hidden
    unit, _ = norm_parts(hidden)
    cross_ref[:tokens, :] = (unit * gm_ref[...]).astype(BF16)

    def add(j, sums):
        block = hist_ref[j].astype(F32)
        lower = (j < me_ref[0]).astype(F32)
        return sums[0] + block, sums[1] + block * lower

    zero = jnp.zeros((experts, bins), F32)
    totals, before = lax.fori_loop(0, devices, add, (zero, zero))
    early = (iota((bins, bins), 0) < iota((bins, bins), 1)).astype(F32)
    exact = lax.Precision.HIGHEST
    base = dot(totals, early, precision=exact) + before
    prio = info_ref[6:7, :].astype(jnp.int32)
    valid = info_ref[7:8, :] > 0
    kept_ref[...] = jnp.full(kept_ref.shape, -1, jnp.int32)
    codes = jnp.zeros((16, tokens), jnp.int32)
    row = iota((16, tokens), 0)
    for k in (0, 1):
        hot = (iota((experts, tokens), 0) == info_ref[k : k + 1, :].astype(jnp.int32)).astype(F32)
        spot = dot(base, class_rows(prio, k, tokens), precision=exact)
        rank = jnp.sum(hot * spot, axis=0, keepdims=True) + info_ref[4 + k : 5 + k, :]
        kept = valid & (rank < capacity - 0.5)
        place = jnp.where(kept, target_ref[k : k + 1, :], -1)
        kept_ref[k : k + 1, :] = place
        codes = jnp.where(row == 2 * k, (place + 1) >> 6, codes)
        codes = jnp.where(row == 2 * k + 1, (place + 1) & 63, codes)
    cross_ref[tokens:, :] = jnp.zeros((16, cross_ref.shape[1]), BF16)
    cross_ref[tokens:, :tokens] = codes.astype(F32).astype(BF16)


def project_kernel(tok_ref, ga_ref, wqkv_ref, normed_ref, proj_ref):
    unit, _ = norm_parts(tok_ref[...].astype(F32))
    normed = (unit * ga_ref[...]).astype(BF16)
    normed_ref[...] = normed
    features = tok_ref.shape[1]
    for part in range(3):
        at = slice(part * features, (part + 1) * features)
        proj_ref[:, at] = dot(normed, wqkv_ref[:, at]).astype(BF16)


def attend_kernel(query_ref, keys_ref, value_ref, seg_ref, pad_ref, mix_ref, prob_ref, bias_ref):
    step = pl.program_id(0)
    tokens = query_ref.shape[0]

    @pl.when(step == 0)
    def _():
        seg = seg_ref[...].astype(F32)
        eye = (iota((8, 8), 0) == iota((8, 8), 1)).astype(F32)
        seg_col = dot(jnp.broadcast_to(seg, (8, tokens)), eye, 0, 0)[:, 0:1]
        own = iota((tokens, tokens), 0) == iota((tokens, tokens), 1)
        allowed = (seg_col == seg) & ((pad_ref[...] > 0) | own)
        bias_ref[...] = jnp.where(allowed, 0.0, -1e30)

    query, keys, value = query_ref[...], keys_ref[...], value_ref[...]
    first = iota((tokens, 128), 1) < HEAD_DIM
    mixed = []
    for h in (0, 1):
        mine = first if h == 0 else ~first
        own_query = jnp.where(mine, query.astype(F32) * HEAD_DIM ** (-0.5), 0.0).astype(BF16)
        scores = dot(own_query, keys, 1, 1) + bias_ref[...]
        top = jnp.max(scores, axis=-1, keepdims=True)
        exponent = jnp.exp(scores - top)
        total = jnp.sum(exponent, axis=-1, keepdims=True)
        prob = (exponent * (1.0 / total)).astype(BF16)
        prob_ref[h] = prob
        mixed.append(dot(prob, value))
    mix_ref[...] = jnp.where(first, mixed[0], mixed[1]).astype(BF16)


def gather_rows(spot_ref, kept_ref, rows_refs):
    slots, features = rows_refs[0].shape
    tokens = kept_ref.shape[1]
    total = jnp.zeros((tokens, features), F32)
    for j, rows_ref in enumerate(rows_refs):
        hot = slot_hot(kept_ref[0:2, :], spot_ref[0] ^ j, slots, tokens)
        total = total + dot(hot, rows_ref[...], 0, 0)
    return total


def near_kernel(spot_ref, kept_ref, hidden_ref, *refs):
    d_ref, block_ref = refs[-2:]
    slots, tokens = refs[0].shape[0] // 2, kept_ref.shape[1]
    d_total = jnp.zeros(d_ref.shape, F32)
    y_total = hidden_ref[...]
    for j, rows_ref in enumerate(refs[:-2]):
        hot = slot_hot(kept_ref[0:2, :], spot_ref[0] ^ j, slots, tokens)
        d_total = d_total + dot(hot, rows_ref[:slots, :], 0, 0)
        y_total = y_total + dot(hot, rows_ref[slots:, :], 0, 0)
    d_ref[...] = d_total
    block_ref[...] = y_total


def gather_pass_kernel(group, spot_ref, kept_ref, *refs):
    refs[2 * group][...] = gather_rows(spot_ref, kept_ref, refs[:group]).astype(BF16)


def gather_kernel(spot_ref, kept_ref, *refs):
    refs[-1][...] = gather_rows(spot_ref, kept_ref, refs[:-1]).astype(BF16)


def block_kernel(block_ref, far_ref, out_ref):
    out_ref[...] = (block_ref[...] + far_ref[...].astype(F32)).astype(BF16)


def weight_grad_kernel(rows_ref, grad_ref, *refs):
    refs[-1][0] = dot(rows_ref[...], grad_ref[...], 0, 0).astype(BF16)


def widen_kernel(both_ref, in_ref, out_ref):
    in_ref[...] = both_ref[0].astype(F32).T
    out_ref[...] = both_ref[1].astype(F32)


def halves_by(bit, value):
    rows = value.shape[0] // 2
    low, high = value[:rows], value[rows:]
    return jnp.where(bit > 0, high, low), jnp.where(bit > 0, low, high)


def as_column(row, column):
    at = (iota((8, 128), 1) == column) & (iota((8, 128), 0) == 0)
    return dot(jnp.broadcast_to(row, (8, row.shape[1])), at.astype(F32), 0, 0, lax.Precision.HIGHEST)


def hidden_back_kernel(
    spot_ref, near_ref, far_ref, hidden_ref, cot_ref, gm_ref, wo_ref, mix_ref, gwra_ref, gwrb_ref, _,
    dhid_ref, dmix_ref, keep_ref, give_ref, __,
):
    features = hidden_ref.shape[1]
    bit = spot_ref[1]
    grad = near_ref[...] + far_ref[...].astype(F32)
    unit, scale = norm_parts(hidden_ref[...])
    gain = jnp.sum(grad * unit, axis=0, keepdims=True)
    dhid = cot_ref[...].astype(F32) + norm_back(unit, scale, grad * gm_ref[...])
    dhid_ref[...] = dhid
    branch = dhid.astype(BF16)
    keep, give = halves_by(bit, dot(mix_ref[...], branch, 0, 0))
    keep_ref[:, :features], give_ref[:, :features] = keep.astype(BF16), give.astype(BF16)
    dmix_ref[...] = dot(branch, wo_ref[...], 1, 1).astype(BF16)
    experts = gwra_ref.shape[1]
    wide = (iota((experts, 128), 0) == iota((experts, 128), 1)).astype(F32)
    side = dot(gwra_ref[...] + gwrb_ref[...], wide, precision=lax.Precision.HIGHEST)
    side = side + as_column(gain, experts)
    keep, give = halves_by(bit, side)
    keep_ref[:, features:], give_ref[:, features:] = keep.astype(BF16), give.astype(BF16)


def head_pair_back(offset, dmix_ref, proj_ref, mix_ref, prob_ref, dproj_ref):
    step = pl.program_id(0)
    tokens, features = mix_ref.shape
    width = dproj_ref.shape[1] // 3
    at = lambda part: pl.ds(pl.multiple_of(part * features + (step + offset) * 128, 128), 128)
    query, keys, value = proj_ref[:, at(0)], proj_ref[:, at(1)], proj_ref[:, at(2)]
    dmix = dmix_ref[:, at(0)]
    product = dmix.astype(F32) * mix_ref[:, at(0)].astype(F32)
    first = iota((tokens, 128), 1) < HEAD_DIM
    parts = []
    for h in (0, 1):
        mine = first if h == 0 else ~first
        own_dmix = jnp.where(mine, dmix.astype(F32), 0.0).astype(BF16)
        delta = jnp.sum(jnp.where(mine, product, 0.0), axis=-1, keepdims=True)
        prob = prob_ref[h]
        dprob = dot(own_dmix, value, 1, 1)
        dscore = (prob.astype(F32) * (dprob - delta) * HEAD_DIM ** (-0.5)).astype(BF16)
        parts.append((dot(dscore, keys), dot(dscore, query, 0, 0), dot(prob, dmix, 0, 0)))
    for part in range(3):
        to = pl.ds(pl.multiple_of(part * width + step * 128, 128), 128)
        dproj_ref[:, to] = jnp.where(first, parts[0][part], parts[1][part]).astype(BF16)


def first_heads_kernel(
    spot_ref, dmix_ref, normed_ref, proj_ref, mix_ref, prob_ref, keep_ref, give_ref, dproj_ref,
):
    head_pair_back(0, dmix_ref, proj_ref, mix_ref, prob_ref, dproj_ref)

    @pl.when(pl.program_id(0) == pl.num_programs(0) - 1)
    def _():
        keep, give = halves_by(spot_ref[1], dot(normed_ref[...], dproj_ref[...], 0, 0))
        keep_ref[...], give_ref[...] = keep.astype(BF16), give.astype(BF16)


def last_heads_kernel(
    spot_ref, dmix_ref, normed_ref, proj_ref, mix_ref, prob_ref, keep_ref, give_ref, dproj_ref,
):
    head_pair_back(pl.num_programs(0), dmix_ref, proj_ref, mix_ref, prob_ref, dproj_ref)

    @pl.when(pl.program_id(0) == pl.num_programs(0) - 1)
    def _():
        keep, give = halves_by(spot_ref[1], dot(normed_ref[...], dproj_ref[...], 0, 0))
        keep_ref[...], give_ref[...] = keep.astype(BF16), give.astype(BF16)


def token_grad_kernel(first_ref, last_ref, dhid_ref, tok_ref, ga_ref, wqkv_ref, gtok_ref):
    tokens, features = tok_ref.shape
    grad = jnp.zeros((tokens, features), F32)
    half = features // 2
    for part in range(3):
        at = slice(part * half, (part + 1) * half)
        for place, ref in ((0, first_ref), (1, last_ref)):
            start = part * features + place * half
            grad = grad + dot(ref[:, at], wqkv_ref[:, start : start + half], 1, 1)
    unit, scale = norm_parts(tok_ref[...].astype(F32))
    gtok_ref[...] = dhid_ref[...] + norm_back(unit, scale, grad * ga_ref[...])


def take(refs, count):
    return refs[:count], refs[count:]


def expert_kernel(pieces, group, near, *refs):
    step = pl.program_id(0)
    (spot_ref, wr_ref, own_ref, win_ref, wout_ref), refs = take(refs, 5)
    mine = (spot_ref[0] - spot_ref[3]) ^ step
    if near:
        x_refs, refs = take(refs, group)
        g_refs, refs = take(refs, group)
        back_refs, refs = take(refs, group)
    else:
        (far_ref,), refs = take(refs, 1)
        refs = refs[4:]
        dx_refs, refs = take(refs, group)
        y_refs, refs = take(refs, group)
    gwr_ref, dexp_ref, xcopy_ref, act_ref, dpre_ref, now_ref = refs
    slots = dexp_ref.shape[0]
    if near:
        for j in range(group):

            @pl.when(step == j)
            def _():
                xcopy_ref[...] = x_refs[j][...]
                now_ref[...] = g_refs[j][...]

    else:
        xcopy_ref[...] = far_ref[mine, :slots, :]
        now_ref[...] = far_ref[mine, slots:, :]

    x = xcopy_ref[...]
    g = now_ref[...].astype(F32)
    logits = dot(x, wr_ref[...])
    exponent = jnp.exp(logits - jnp.max(logits, axis=-1, keepdims=True))
    router = exponent / jnp.sum(exponent, axis=-1, keepdims=True)
    gate = jnp.sum(router * own_ref[...], axis=-1, keepdims=True)
    dexp = (gate * g).astype(BF16)
    dexp_ref[...] = dexp
    out = jnp.zeros(x.shape, F32)
    dx = jnp.zeros(x.shape, F32)
    width = win_ref.shape[1] // pieces
    for r in range(pieces):
        at = slice(r * width, (r + 1) * width)
        pre = dot(x, win_ref[:, at])
        square = pre * pre
        bend = jnp.tanh(pre * (0.7978845608028654 + 0.035677408136300125 * square))
        half = 0.5 + 0.5 * bend
        smooth = pre * half
        slope = half + smooth * (1.0 - half) * (1.5957691216057308 + 0.21406444881780075 * square)
        active = smooth.astype(BF16)
        act_ref[:, at] = active
        dpreact = (dot(dexp, wout_ref[at, :], 1, 1) * slope).astype(BF16)
        dpre_ref[:, at] = dpreact
        out = out + dot(active, wout_ref[at, :])
        dx = dx + dot(dpreact, win_ref[:, at], 1, 1)
    out = out.astype(BF16).astype(F32)
    y = (gate * out).astype(BF16)
    dgate = jnp.sum(g * out, axis=-1, keepdims=True)
    dlogits = (dgate * gate * (own_ref[...] - router)).astype(BF16)
    dx = (dx + dot(dlogits, wr_ref[...], 1, 1)).astype(BF16)
    if near:
        for j in range(group):

            @pl.when(step == j)
            def _():
                back_refs[j][:slots, :] = dx
                back_refs[j][slots:, :] = y

    else:
        for j in range(group):

            @pl.when(step == j)
            def _():
                y_refs[j][...] = y
                dx_refs[j][...] = dx

    @pl.when(step == 0)
    def _():
        gwr_ref[...] = jnp.zeros(gwr_ref.shape, F32)

    gwr_ref[...] += dot(x, dlogits, 0, 0)


def swap(value, axis, bit):
    size = lax.axis_size(axis)
    return lax.ppermute(value, axis, [(i, i ^ bit) for i in range(size)])


def bits_of(axis):
    size = lax.axis_size(axis)
    return [1 << b for b in range(size.bit_length() - 1)]


def deal_plane_kernel(spot_ref, *refs):
    in_refs, (own_ref, *out_refs, total_ref) = refs[:-5], refs[-5:]
    start = 0
    for keep_ref, other_ref in zip(in_refs[::2], in_refs[1::2]):
        total = keep_ref[...].astype(F32) + other_ref[...].astype(F32)
        rows, columns = total.shape
        total_ref[:, :, start : start + columns] = total.reshape(4, rows // 4, columns)
        start += columns
    spot = spot_ref[2] * 2 + spot_ref[4]
    own_ref[...] = total_ref[spot]
    for j, out_ref in enumerate(out_refs):
        out_ref[...] = total_ref[spot ^ (j + 1)].astype(BF16)


def deal_line_kernel(groups, spot_ref, own_ref, *refs):
    in_refs, (first_ref, *out_refs, total_ref) = refs[:3], refs[3:]
    total = own_ref[...]
    for ref in in_refs:
        total = total + ref[...].astype(F32)
    rows, columns = total.shape
    total_ref[...] = total.reshape(groups, rows // groups, columns)
    first_ref[...] = total_ref[spot_ref[5]]
    for j, out_ref in enumerate(out_refs):
        out_ref[...] = total_ref[spot_ref[5] ^ (j + 1)].astype(BF16)


def pile_kernel(own_ref, *refs):
    total = own_ref[...]
    for ref in refs[:-1]:
        total = total + ref[...].astype(F32)
    refs[-1][...] = total.astype(BF16)


def line_up_kernel(spot_ref, *refs):
    out_ref, total_ref = refs[-2:]
    for j, ref in enumerate(refs[:-2]):
        total_ref[spot_ref[5] ^ j] = ref[...].astype(F32)
    out_ref[...] = total_ref[...].reshape(out_ref.shape).astype(BF16)


def line_up_plane_kernel(spot_ref, *refs):
    out_ref, total_ref = refs[-2:]
    for j, ref in enumerate(refs[:-2]):
        total_ref[(spot_ref[2] * 2 + spot_ref[4]) ^ j] = ref[...]
    out_ref[...] = total_ref[...].reshape(out_ref.shape)


def finish_kernel(
    experts, spot_ref, wqkv_ref, ga_ref, a0, a1, o0, o1, s0, s1, b0, b1,
    grad_o_ref, grad_qkv_ref, gain_attn_ref, gain_moe_ref, router_ref, total_ref, side_ref,
):
    step = pl.program_id(0)
    rows, half = a0.shape
    for k, (a_ref, o_ref, s_ref, b_ref) in enumerate(((a0, o0, s0, b0), (a1, o1, s1, b1))):
        at = pl.ds(pl.multiple_of((spot_ref[1] ^ k) * rows, 8), rows)
        grad_qkv_ref[at, :half] = a_ref[...].astype(F32)
        grad_qkv_ref[at, half:] = b_ref[...].astype(F32)

        @pl.when(step < 2)
        def _():
            grad_o_ref[at, :] = o_ref[...].astype(F32)

        @pl.when(step == 0)
        def _():
            side_ref[at, :] = s_ref[...].astype(F32)

    part = jnp.sum(wqkv_ref[...].astype(F32) * grad_qkv_ref[...], axis=-1, keepdims=True)
    part = jnp.broadcast_to(part, total_ref.shape)

    @pl.when(step == 0)
    def _():
        total_ref[...] = part

    @pl.when(step > 0)
    def _():
        total_ref[...] += part

    @pl.when(step == 2)
    def _():
        side = side_ref[...].T
        router_ref[...] = side[:experts, :]
        gain_moe_ref[...] = side[experts : experts + 1, :].reshape(gain_moe_ref.shape)
        gain_attn_ref[...] = (total_ref[...].T[0:1, :] / ga_ref[...]).reshape(gain_attn_ref.shape)


def plane_swap(value, j):
    groups = lax.axis_size("expert")
    size = lax.axis_size("dp") * groups
    apart = (j >> 1) * 2 * groups + (j & 1)
    return lax.ppermute(value, ("dp", "expert"), [(i, i ^ apart) for i in range(size)])


def plane_deal(spot, halves, *after):
    scalar = pl.BlockSpec(memory_space=pltpu.SMEM)
    ins = [v for pair in halves for v in pair]
    rows, columns = halves[0][0].shape[0] // 4, sum(pair[0].shape[1] for pair in halves)
    piece = (rows, columns)
    return call(
        deal_plane_kernel, (1,), (spot, *ins), [scalar] + [whole(v.shape) for v in ins],
        [shape_of(piece, F32)] + [shape_of(piece, BF16)] * 3, [whole_out(piece)] * 4,
        [pltpu.VMEM((4, *piece), F32)],
        after=after,
    )


def line_deal(spot, dealt, groups, us, *after, ready=False):
    scalar = pl.BlockSpec(memory_space=pltpu.SMEM)
    own, *out = dealt
    rows, columns = own.shape
    piece = (rows // groups, columns)
    arrived = out if ready else [plane_swap(v, j + 1) for j, v in enumerate(out)]
    scratch = [pltpu.VMEM((groups, *piece), F32)]
    own, *out = call(
        functools.partial(deal_line_kernel, groups), (1,), (spot, own, *arrived),
        [scalar] + [whole((rows, columns))] * 4,
        (shape_of(piece, F32), *[shape_of(piece, BF16)] * (groups - 1)),
        (whole_out(piece),) * groups,
        scratch,
        us=us,
        after=after,
    )
    return [own] + [swap(v, "expert", 2 * (j + 1)) for j, v in enumerate(out)]


def line_up(spot, parts, *late_pile, waits=()):
    scalar = pl.BlockSpec(memory_space=pltpu.SMEM)
    groups, piece = len(parts), parts[0].shape
    rows, columns = groups * piece[0], piece[1]
    scratch = [pltpu.VMEM((groups, *piece), F32)]
    total = call(
        pile_kernel, (1,), parts, [whole(piece)] * groups, shape_of(piece, BF16), whole_out(piece),
        after=late_pile,
    )
    own = call(
        line_up_kernel, (1,), (spot, total, *[swap(total, "expert", 2 * j) for j in range(1, groups)]),
        [scalar] + [whole(piece)] * groups,
        shape_of((rows, columns), BF16), whole_out((rows, columns)), scratch,
        after=waits,
    )
    return own, [plane_swap(own, j) for j in (1, 2, 3)]


def line_up_plane(spot, own, arrived, *after):
    scalar = pl.BlockSpec(memory_space=pltpu.SMEM)
    rows, columns = own.shape
    half = (4 * rows, columns)
    own = call(
        line_up_plane_kernel, (1,), (spot, own, *arrived),
        [scalar] + [whole((rows, columns))] * 4,
        shape_of(half, BF16), whole_out(half), [pltpu.VMEM((4, rows, columns), BF16)],
        after=after,
    )
    return [own, swap(own, "dp", 1)]


def all_sum(value, steps):
    rows = value.shape[0]
    place = []
    for axis, bit in steps:
        half = value.shape[0] // 2
        mine = ((lax.axis_index(axis) & bit) > 0).astype(jnp.int32)
        keep = lax.dynamic_slice_in_dim(value, mine * half, half, 0)
        give = lax.dynamic_slice_in_dim(value, (1 - mine) * half, half, 0)
        value = (keep.astype(F32) + swap(give, axis, bit).astype(F32)).astype(BF16)
        place.append(mine)
    for (axis, bit), mine in zip(reversed(steps), reversed(place)):
        other = swap(value, axis, bit)
        low = jnp.where(mine > 0, other, value)
        high = jnp.where(mine > 0, value, other)
        value = jnp.concatenate([low, high], axis=0)
    return value


def local(
    tokens, segment_ids, pad_mask, routes, priority, gain_attn, w_qkv, w_o, gain_moe, w_router,
    w_in, w_out, cotangent,
):
    sequences, length, features = tokens.shape
    count = sequences * length
    experts = w_router.shape[1]
    groups = lax.axis_size("expert")
    replicas = lax.axis_size("dp")
    devices = groups * replicas
    group = groups // 2
    most = 4 * count // experts
    slots = -(-most // 16) * 16
    capacity = (42 * count * devices + 20 * experts - 1) // (20 * experts)
    me = lax.axis_index(("dp", "expert")).astype(jnp.int32).reshape(1)
    replica = lax.axis_index("dp")
    column = lax.axis_index("expert")
    spot = jnp.stack(
        [column, replica & 1, replica >> 1 & 1, column // group * group, column & 1, column >> 1]
    ).astype(jnp.int32)
    tok = tokens.reshape(count, features)
    cot = cotangent.reshape(count, features)
    ga = gain_attn.reshape(1, features)
    gm = gain_moe.reshape(1, features)
    full = (count, features)
    scalar = pl.BlockSpec(memory_space=pltpu.SMEM)
    sent = shape_of((slots, features), BF16)

    def across(value):
        return swap(value, "expert", group)

    def among(values):
        return [v if j == 0 else swap(v, "expert", j) for j, v in enumerate(values)]

    halves = [list(range(group)), list(range(group, groups))]
    joint = (group, 2 * slots, features)

    def half_exchange(value):
        return lax.all_to_all(value, "expert", 0, 0, axis_index_groups=halves, tiled=True)

    far_cot = across(cot)
    full_in = lax.all_gather(w_in[0], "dp", axis=1, tiled=True)
    full_out = lax.all_gather(w_out[0], "dp", axis=0, tiled=True)

    pairs = features // 128
    tile = lambda dtype: shape_of((count, features), dtype)
    prob_block = pl.BlockSpec((2, count, count), lambda i: (i, 0, 0))
    hist_shape = (devices, experts, BINS)
    hist, info, target = call(
        functools.partial(route_kernel, slots, experts),
        (1,),
        (routes.reshape(count, 2).T, priority.reshape(1, count), pad_mask.reshape(1, count)),
        [whole((2, count)), whole((1, count)), whole((1, count))],
        (shape_of(hist_shape, jnp.int32), shape_of((8, count), F32), shape_of((8, count), jnp.int32)),
        (whole_out(hist_shape), whole_out((8, count)), whole_out((8, count))),
        limit=LIMIT,
    )
    def spread(target, rows, us, *after):
        return call(
            functools.partial(spread_kernel, slots),
            (1,),
            (spot, target, rows),
            [scalar, whole((8, count)), whole(rows.shape)],
            [sent] * group,
            [whole_out((slots, features))] * group,
            us=us,
            after=after,
        limit=LIMIT,
        )

    near_g_sent = spread(target, cot, 1)
    near_g = among(near_g_sent)
    every = lax.all_to_all(hist, ("dp", "expert"), 0, 0, tiled=True)
    normed, proj = call(
        project_kernel,
        (1,),
        (tok, ga, w_qkv),
        [whole(full), whole((1, features)), whole(w_qkv.shape)],
        (tile(BF16), shape_of((count, 3 * features), BF16)),
        (whole_out(full), whole_out((count, 3 * features))),
        after=(near_g_sent[0],),
        limit=LIMIT,
    )
    lanes = lambda part: pl.BlockSpec((count, 128), lambda i: (0, part * pairs + i))
    mix, prob = call(
        attend_kernel,
        (pairs,),
        (proj, proj, proj, segment_ids.reshape(1, count), pad_mask.reshape(1, count)),
        [lanes(0), lanes(1), lanes(2), whole((1, count)), whole((1, count))],
        (tile(BF16), shape_of((HEADS, count, count), BF16)),
        (lanes(0), prob_block),
        [pltpu.VMEM((count, count), F32)],
        us=20000,
        after=(target,),
        limit=LIMIT,
    )
    cross_shape = (count + 16, features)
    hidden, cross, kept = call(
        functools.partial(hidden_kernel, capacity),
        (1,),
        (me, every, info, target, tok, mix, w_o, gm),
        [scalar, whole(hist_shape), whole((8, count)), whole((8, count)), whole(full), whole(full), whole(w_o.shape), whole((1, features))],
        (tile(F32), shape_of(cross_shape, BF16), shape_of((8, count), jnp.int32)),
        (whole_out(full), whole_out(cross_shape), whole_out((8, count))),
        limit=LIMIT,
    )
    far_x = across(cross)
    near_sent = spread(kept, cross, 20000, *near_g)
    near_x = among(near_sent)
    far_sent, far_kept = call(
        functools.partial(spread_joint_kernel, slots),
        (group,),
        (spot, far_x, far_cot),
        [scalar, whole(cross_shape), whole(full)],
        (shape_of(joint, BF16), shape_of((8, count), jnp.int32)),
        (pl.BlockSpec((1, 2 * slots, features), lambda e: (e, 0, 0)), whole_out((8, count))),
        after=(near_sent[0],),
        limit=LIMIT,
    )
    far_rows = half_exchange(far_sent)

    hidden_units = w_out.shape[1] * replicas
    own = (iota((1, experts), 1) == column).astype(F32)
    flat = group * slots
    slot_spec = whole_out((slots, features))
    weights = (spot, w_router, own, full_in, full_out)
    weight_specs = [scalar, whole(w_router.shape), whole((1, experts)), whole(full_in.shape), whole(full_out.shape)]
    tall = [shape_of((2 * flat, n), BF16) for n in (features, features, hidden_units, hidden_units)]
    tall_blocks = lambda first: [
        pl.BlockSpec((slots, v.shape[1]), lambda e: (first + e, 0)) for v in tall
    ]
    outs = call(
        functools.partial(expert_kernel, 4, group, True),
        (group,),
        (*weights, *near_x, *near_g),
        weight_specs + [whole((slots, features))] * (2 * group),
        (*[shape_of((2 * slots, features), BF16)] * group, shape_of(w_router.shape, F32), *tall),
        (*[whole_out((2 * slots, features))] * group, whole_out(w_router.shape), *tall_blocks(0)),
        [pltpu.VMEM((slots, features), BF16)],
        us=300000,
        after=(far_sent,),
        limit=LIMIT,
    )
    near_back, outs = take(outs, group)
    near_back = among(near_back)
    gwr_a, kept_rows = outs[0], outs[1:]
    outs = call(
        functools.partial(expert_kernel, 4, group, False),
        (group,),
        (*weights, far_rows, *kept_rows),
        weight_specs + [whole(joint)] + [pl.BlockSpec(memory_space=pl.ANY)] * 4,
        (*[sent] * (2 * group), shape_of(w_router.shape, F32), *tall),
        (*[slot_spec] * (2 * group), whole_out(w_router.shape), *tall_blocks(group)),
        [pltpu.VMEM((slots, features), BF16)],
        after=(gwr_a,),
        alias=[(6 + i, 2 * group + 1 + i) for i in range(4)],
        limit=LIMIT,
    )
    d_far, outs = take(outs, group)
    y_far, outs = take(outs, group)
    gwr_b, all_dexp, all_x, all_act, all_dpre = outs
    d_far = among(d_far)
    def gather(rows, *after):
        return call(
            gather_kernel,
            (1,),
            (spot, far_kept, *rows),
            [scalar, whole((8, count))] + [whole((slots, features))] * group,
            tile(BF16),
            whole_out(full),
            after=after,
        )

    anywhere = pl.BlockSpec(memory_space=pl.ANY)
    part = hidden_units // 4
    both_shape = shape_of((2, hidden_units, features), BF16)

    def weight_grad(which, rows, grad, us, after, *given):
        return call(
            weight_grad_kernel,
            (4,),
            (rows, grad, *given),
            [pl.BlockSpec((2 * flat, part), lambda i: (0, i)), whole((2 * flat, features))] + [anywhere] * len(given),
            both_shape,
            pl.BlockSpec((1, part, features), lambda i: (which, i, 0)),
            us=us,
            after=after,
            alias=[(2, 0)] if given else (),
        limit=LIMIT,
        )

    both = weight_grad(1, all_act, all_dexp, 1, near_back)
    d_far, *y_far = call(
        functools.partial(gather_pass_kernel, group),
        (1,),
        (spot, far_kept, *d_far, *y_far),
        [scalar, whole((8, count))] + [whole((slots, features))] * group + [anywhere] * group,
        [tile(BF16)] + [sent] * group,
        [whole_out(full)] + [anywhere] * group,
        after=(both,),
        alias=[(2 + group + j, 1 + j) for j in range(group)],
    )
    y_far = among(y_far)
    both = weight_grad(0, all_dpre, all_x, 60000, (d_far,), both)
    near_d, block_part = call(
        near_kernel,
        (1,),
        (spot, kept, hidden, *near_back),
        [scalar, whole((8, count)), whole(full)] + [whole((2 * slots, features))] * group,
        (tile(F32), tile(F32)),
        (whole_out(full), whole_out(full)),
        after=(both,),
    )

    y_far = gather(y_far, near_d)
    d_far = across(d_far)
    both = lax.psum_scatter(both, "dp", scatter_dimension=1, tiled=True)

    o_half = (features // 2, features + 128)
    a_half = (features // 2, 3 * features // 2)
    dhid, dmix, keep_o, give_o, y_far = call(
        hidden_back_kernel,
        (1,),
        (spot, near_d, d_far, hidden, cot, gm, w_o, mix, gwr_a, gwr_b, y_far),
        [scalar] + [whole(full)] * 4 + [whole((1, features)), whole(w_o.shape), whole(full)] + [whole(gwr_a.shape)] * 2 + [anywhere],
        (tile(F32), tile(BF16), *[shape_of(o_half, BF16)] * 2, tile(BF16)),
        (whole_out(full), whole_out(full), *[whole_out(o_half)] * 2, anywhere),
        us=400000,
        alias=[(10, 4)],
    )
    y_far = across(y_far)
    some = 3 * features // 2
    head_specs = lambda offset: [scalar] + [whole(full)] * 2 + [whole((count, 3 * features)), whole(full)] + [
        pl.BlockSpec((2, count, count), lambda i: (i + offset, 0, 0))
    ]
    keep_a, give_a, dproj_a = call(
        first_heads_kernel,
        (pairs // 2,),
        (spot, dmix, normed, proj, mix, prob),
        head_specs(0),
        (shape_of(a_half, BF16), shape_of(a_half, BF16), shape_of((count, some), BF16)),
        (whole_out(a_half), whole_out(a_half), whole_out((count, some))),
        us=13000,
    )
    by_hand = replicas == 4 and groups == 8 and features % (8 * devices) == 0
    if by_hand:
        beside = lambda keep, give: (keep, swap(give, "dp", 1))
        early = plane_deal(spot, [beside(keep_a, give_a), beside(keep_o, give_o)])
    keep_b, give_b, dproj_b = call(
        last_heads_kernel,
        (pairs // 2,),
        (spot, dmix, normed, proj, mix, prob),
        head_specs(pairs // 2),
        (shape_of(a_half, BF16), shape_of(a_half, BF16), shape_of((count, some), BF16)),
        (whole_out(a_half), whole_out(a_half), whole_out((count, some))),
        us=50000,
        after=early[:1] if by_hand else (),
    )
    gtok = call(
        token_grad_kernel,
        (1,),
        (dproj_a, dproj_b, dhid, tok, ga, w_qkv),
        [whole((count, some))] * 2 + [whole(full)] * 2 + [whole((1, features)), whole(w_qkv.shape)],
        tile(F32),
        whole_out(full),
    )
    block_out = call(
        block_kernel,
        (1,),
        (block_part, y_far),
        [whole(full)] * 2,
        tile(BF16),
        whole_out(full),
        after=(gtok,),
    )
    shapes = [w_in.shape[1:], w_out.shape[1:]]
    gin, gout = call(
        widen_kernel,
        (1,),
        (both,),
        [whole(both.shape)],
        [shape_of(v, F32) for v in shapes],
        [whole_out(v) for v in shapes],
        after=(gtok,),
    )
    if by_hand:
        rows = groups // 2
        early = line_deal(spot, early, rows, 30000, gtok)
        late = plane_deal(spot, [beside(keep_b, give_b)], early[0], y_far)
        late = [late[0]] + [plane_swap(v, j + 1) for j, v in enumerate(late[1:])]
        early, early_parts = line_up(spot, early, late[0], waits=late[2:])
        late, late_parts = line_up(spot, line_deal(spot, late, rows, 1, early, ready=True))
        pieces = line_up_plane(spot, early, early_parts, late) + line_up_plane(
            spot, late, late_parts, gin, block_out
        )
        half = features // 2
        block = lambda width, index: [pl.BlockSpec((half, width), lambda i: (0, index(i)))] * 2
        third = lambda i: (0, i)
        grad_o, grad_qkv, gain_attn_grad, gain_moe_grad, grad_router = call(
            functools.partial(finish_kernel, experts),
            (3,),
            (spot, w_qkv, ga, *pieces[:2] * 3, *pieces[2:]),
            [scalar, pl.BlockSpec((features, features), third), whole((1, features))]
            + block(half, lambda i: i)
            + block(half, lambda i: jnp.minimum(3 + i, 4))
            + block(128, lambda i: 5 * half // 128)
            + block(half, lambda i: i),
            [shape_of(v, F32) for v in ((features, features), (features, 3 * features), (features,), (features,), (experts, features))],
            [
                pl.BlockSpec((features, half), lambda i: (0, jnp.minimum(i, 1))),
                pl.BlockSpec((features, features), third),
                whole_out((features,)),
                whole_out((features,)),
                whole_out((experts, features)),
            ],
            [pltpu.VMEM((features, 128), F32)] * 2,
        )
    else:
        low = (replica & 1) == 0

        def rejoin(keep, give):
            return jnp.concatenate([jnp.where(low, keep, give), jnp.where(low, give, keep)], axis=0)

        gain_steps = [("dp", b) for b in bits_of("dp")] + [("expert", b) for b in bits_of("expert")]
        both = all_sum(rejoin(keep_o, give_o), gain_steps).astype(F32)
        grad_o, side_o = both[:, :features], both[:, features:]
        first = all_sum(rejoin(keep_a, give_a), gain_steps).astype(F32)
        last = all_sum(rejoin(keep_b, give_b), gain_steps).astype(F32)
        half = features // 2
        cut = lambda part: slice(part * half, (part + 1) * half)
        grad_qkv = jnp.concatenate([v[:, cut(part)] for part in range(3) for v in (first, last)], axis=1)
        product = jnp.sum(w_qkv.astype(F32) * grad_qkv, axis=1)
        gain_attn_grad, gain_moe_grad = product / gain_attn, side_o[:, experts]
        grad_router = side_o[:, :experts].T
    return (
        block_out.reshape(sequences, length, features),
        gtok.reshape(sequences, length, features),
        gain_attn_grad.reshape(features),
        grad_qkv,
        grad_o,
        gain_moe_grad.reshape(features),
        grad_router.T,
        gin[None],
        gout[None],
    )


def solution(mesh):
    rows = P(("dp", "expert"), None, None)
    flat = P(("dp", "expert"), None)
    first = P("expert", None, "dp")
    second = P("expert", "dp", None)
    return jax.shard_map(
        local,
        mesh=mesh,
        in_specs=(rows, flat, flat, rows, flat, P(), P(), P(), P(), P(), first, second, rows),
        out_specs=(rows, rows, P(), P(), P(), P(), P(), first, second),
        check_vma=False,
    )
```
